32 devices in a mesh: batch: 4 (over y, x), edge: 8 (over z, core).
Axes of the slice: x: 2, y: 2, z: 4, core: 2. Of those that a mesh axis runs over, the one named last changes fastest.
Arguments:
- node: bfloat16 [4, 768, 512], P('batch', 'edge'), may hold values from -6 to 6
- edge: bfloat16 [4, 46080, 192], P('batch', 'edge'), may hold values from -6 to 6
- dest_device: int32 [4, 46080, 1], P('batch', 'edge'), may hold values from 0 to 7; in each aligned block of 5760 rows (0 to 5759, 5760 to 11519, ..., all dimensions but the last counted through in order) at most 1440 rows name the same one
- dest_local: int32 [4, 46080], P('batch', 'edge'), may hold values from 0 to 95
- node_valid: int32 [4, 768], P('batch', 'edge'), may hold values 0 or 1
- node_cot: bfloat16 [4, 768, 512], P('batch', 'edge'), may hold values from -6 to 6
- edge_cot: bfloat16 [4, 46080, 192], P('batch', 'edge'), may hold values from -6 to 6
- big_weight: float32 [768, 4096], P(('batch', 'edge')), may hold values from -2 to 2
- big_first: float32 [768, 4096], P(('batch', 'edge')), may hold values from -3 to 3
- big_second: float32 [768, 4096], P(('batch', 'edge')), may hold values from 0 to 2, as said below
- big_left: float32 [768, 4096], P(('batch', 'edge')), may hold values from -1 to 1, as said below
- big_right: float32 [768, 4096], P(('batch', 'edge')), may hold values from -1 to 1, as said below
- small_weight: float32 [99, 4096], replicated, may hold values from -2 to 2
- small_first: float32 [99, 4096], replicated, may hold values from -3 to 3
- small_second: float32 [99, 4096], replicated, may hold values from 0 to 2, as said below
- small_left: float32 [99, 4096], replicated, may hold values from -1 to 1, as said below
- small_right: float32 [99, 4096], replicated, may hold values from -1 to 1, as said below
- norm_params: float32 [2432], replicated, may hold values from -0.4 to 1.3
- norm_first: float32 [2432], replicated, may hold values from -4 to 4
- norm_second: float32 [2432], replicated, may hold values from 0 to 3, as said below
Outputs:
- node_out: bfloat16 [4, 768, 512], P('batch', 'edge')
- edge_out: bfloat16 [4, 46080, 192], P('batch', 'edge')
- node_grad: float32 [4, 768, 512], P('batch', 'edge')
- edge_grad: float32 [4, 46080, 192], P('batch', 'edge')
- big_first_new: float32 [768, 4096], P(('batch', 'edge'))
- big_second_new: float32 [768, 4096], P(('batch', 'edge'))
- big_weight_new: float32 [768, 4096], P(('batch', 'edge'))
- big_weight_low: bfloat16 [768, 4096], P(('batch', 'edge'))
- small_first_new: float32 [99, 4096], replicated
- small_second_new: float32 [99, 4096], replicated
- small_weight_new: float32 [99, 4096], replicated
- small_weight_low: bfloat16 [99, 4096], replicated
- norm_first_new: float32 [2432], replicated
- norm_second_new: float32 [2432], replicated
- norm_params_new: float32 [2432], replicated
The draws below stay inside these ranges and needn't reach their ends.
Inputs may be any that keep to these rules, and one draw needn't show every extreme that they name: `dest_device`: in each aligned block of 5760 rows, the edges of one device, no device number appears more than 1440 times. `big_left`: every row, read as a 64 x 64 matrix, is orthogonal. `big_right`: every row, read as a 64 x 64 matrix, is orthogonal. `small_left`: every row, read as a 64 x 64 matrix, is orthogonal. `small_right`: every row, read as a 64 x 64 matrix, is orthogonal. `big_second`: entries are positive. `small_second`: entries are positive. `norm_second`: entries are positive.
All inputs are finite; a program needn't handle non-finite values. No bound on the sum of `node_valid` on one device may be relied on, other than what follows from the above.
Results may differ from the reference program's by a relative error of at most 0.018.
Values may be sent and summed in bfloat16 or wider, within the bound.
No kernel may reach another device: no remote copies, remote signals or barrier semaphores. Data moves between devices by JAX's collectives and lax.ppermute only.
A program may use at most 320 MiB of HBM per device.

```python
import math
import jax
import jax.numpy as jnp
import numpy as np
from jax import lax

D = 512
DE = 192
FF = 2048
K = 60
TILE = 64
STEP = 10
NODE_DEV = 96
NODES = 768
COMPLEXES = 4
MOST = 1440
BIG_TILES = 768
SMALL_TILES = 99
NORM_LEN = 2432
N_EDGE = 8


def big_layout():
    middle = (2 * D + DE) ** (-0.5)
    shapes = [(D, D), (D, D), (D, D), (D, D), (D, FF), (FF, D)]
    spreads = [middle, middle, D ** (-0.5), 2.5 * D ** (-0.5), D ** (-0.5), FF ** (-0.5)]
    backward = math.sqrt(1.0 + 0.07 * K)
    message = backward / 1.3 / math.sqrt(K)
    grad_sizes = [0.13 * message, 0.4 * message, 0.25 * message, 0.2 * message, 0.5 * backward / math.sqrt(K), 0.5 * backward / math.sqrt(K)]
    return (shapes, spreads, grad_sizes)


def small_layout():
    middle = (2 * D + DE) ** (-0.5)
    shapes = [(DE, D), (D, DE), (D, DE), (DE, DE), (DE, DE), (DE, DE)]
    spreads = [middle, middle, middle, middle, DE ** (-0.5), 1.5 * DE ** (-0.5)]
    backward = math.sqrt(1.0 + 0.07 * K)
    message = backward / 1.3 / math.sqrt(K)
    grad_sizes = [0.13 * message, 0.3, 0.3, 0.3, 0.5, 0.55]
    return (shapes, spreads, grad_sizes)


def norm_layout():
    backward = math.sqrt(1.0 + 0.07 * K) / math.sqrt(K)
    lengths = [D, D, D, D, DE, DE]
    grad_sizes = [0.9 * backward, 0.9 * backward, 0.8 * backward, 0.8 * backward, 0.8, 0.8]
    return (lengths, grad_sizes)


def per_tile(shapes, values):
    amounts = [height // TILE * (breadth // TILE) for height, breadth in shapes]
    return jnp.asarray(np.repeat(np.array(values, np.float32), amounts))[:, None, None]


def flatten_tiles(square_tiles):
    return square_tiles.reshape(square_tiles.shape[0], TILE * TILE)


def signed_from(key, scales):
    return flatten_tiles(jax.random.truncated_normal(key, -4.0, 4.0, (scales.shape[0], TILE, TILE), jnp.float32) * scales)


def seconds_from(key, scales):
    factor = jnp.exp(jax.random.uniform(key, (scales.shape[0], TILE, TILE), jnp.float32, 0.0, math.log(4.0)))
    return flatten_tiles(factor * scales * scales)


def bases_from(key, amount):
    sign_key, order_key, column_key = jax.random.split(key, 3)
    row_signs = jax.random.rademacher(sign_key, (amount, TILE), jnp.float32)
    column_signs = jax.random.rademacher(column_key, (amount, TILE), jnp.float32)
    orders = jax.vmap(lambda subkey: jax.random.permutation(subkey, TILE))(jax.random.split(order_key, amount))
    frequency = orders.astype(jnp.float32)[:, :, None]
    position = jnp.arange(TILE, dtype=jnp.float32)[None, None, :]
    cosines = jnp.cos(math.pi * (position + 0.5) * frequency / TILE) * math.sqrt(2.0 / TILE)
    cosines = jnp.where(frequency == 0.0, cosines / math.sqrt(2.0), cosines)
    return flatten_tiles(cosines * row_signs[:, :, None] * column_signs[:, None, :])


def norm_scales():
    lengths, grad_sizes = norm_layout()
    return jnp.asarray(np.repeat(np.array(grad_sizes, np.float32), lengths))


def draw_big_weight(key, part):
    key = jax.random.fold_in(key, 11)
    shapes, spreads, grad_sizes = big_layout()
    return signed_from(key, per_tile(shapes, spreads))


def draw_big_first(key, part):
    key = jax.random.fold_in(key, 12)
    shapes, spreads, grad_sizes = big_layout()
    return signed_from(key, per_tile(shapes, grad_sizes))


def draw_big_second(key, part):
    key = jax.random.fold_in(key, 13)
    shapes, spreads, grad_sizes = big_layout()
    return seconds_from(key, per_tile(shapes, grad_sizes))


def draw_big_left(key, part):
    key = jax.random.fold_in(key, 14)
    return bases_from(key, BIG_TILES)


def draw_big_right(key, part):
    key = jax.random.fold_in(key, 15)
    return bases_from(key, BIG_TILES)


def draw_small_weight(key, part):
    key = jax.random.fold_in(key, 16)
    shapes, spreads, grad_sizes = small_layout()
    return signed_from(key, per_tile(shapes, spreads))


def draw_small_first(key, part):
    key = jax.random.fold_in(key, 17)
    shapes, spreads, grad_sizes = small_layout()
    return signed_from(key, per_tile(shapes, grad_sizes))


def draw_small_second(key, part):
    key = jax.random.fold_in(key, 18)
    shapes, spreads, grad_sizes = small_layout()
    return seconds_from(key, per_tile(shapes, grad_sizes))


def draw_small_left(key, part):
    key = jax.random.fold_in(key, 19)
    return bases_from(key, SMALL_TILES)


def draw_small_right(key, part):
    key = jax.random.fold_in(key, 20)
    return bases_from(key, SMALL_TILES)


def draw_norm_params(key, part):
    key = jax.random.fold_in(key, 21)
    uniform_vals = jax.random.uniform(key, (NORM_LEN,), jnp.float32, -1.0, 1.0)
    gain_mask = jnp.asarray(np.repeat(np.array([1, 0, 1, 0, 1, 0], np.int32), [D, D, D, D, DE, DE]))
    return jnp.where(gain_mask > 0, 1.0 + 0.3 * uniform_vals, 0.4 * uniform_vals)


def draw_norm_first(key, part):
    key = jax.random.fold_in(key, 22)
    return jax.random.truncated_normal(key, -4.0, 4.0, (NORM_LEN,), jnp.float32) * norm_scales()


def draw_norm_second(key, part):
    key = jax.random.fold_in(key, 23)
    scales = norm_scales()
    factor = jnp.exp(jax.random.uniform(key, (NORM_LEN,), jnp.float32, 0.0, math.log(4.0)))
    return factor * scales * scales


def plant(values, own_key, least, high):
    shape = values.shape
    spot = [jax.random.randint(jax.random.fold_in(own_key, axis), (), 0, shape[axis]) for axis in range(len(shape))]
    values = values.at[tuple(spot)].set(least)
    longest = shape.index(max(shape))
    spot[longest] = (spot[longest] + 1) % shape[longest]
    return values.at[tuple(spot)].set(high)


def block_levels(rng, dims, shards, least, top_value):
    def one(dim, parts):
        steps = jax.random.uniform(jax.random.fold_in(jax.random.fold_in(rng, 6), dim), (parts,), jnp.float32, least / len(shards), top_value / len(shards))
        return jnp.repeat(jnp.exp(steps), dims[dim] // parts).reshape((-1,) + (1,) * (len(dims) - dim - 1))

    gain = one(*shards[0])
    for cut in shards[1:]:
        gain = gain * one(*cut)
    return gain


def shared_out(key, own, number, rows, number_of, top, reach, skew):
    order = jax.random.permutation(key, number_of)
    crowded, ordinary = shares(number_of, rows * top, reach, skew, True), shares(number_of, rows * top, reach, skew, False)
    places = jnp.arange(number_of)

    def named(tallies, offset_by):
        used = int((tallies > 0).sum())
        fixed = max(1, used // 4)
        passed = fixed + (places - fixed + offset_by * (used - fixed)) % max(1, number_of - fixed)
        return jnp.zeros((number_of,), jnp.int32).at[order[jnp.where(places < fixed, places, passed)]].set(jnp.asarray(tallies, jnp.int32))

    tallies = jnp.where(number % 4 == 0, named(crowded, number // 4), named(ordinary, number - number // 4 - 1))
    mixed = jax.random.permutation(jax.random.fold_in(own, 3), number_of)
    donor, taker = mixed[0:number_of // 2 * 2:2], mixed[1:number_of // 2 * 2:2]
    slack = jnp.minimum(tallies[donor] - 1, reach - tallies[taker]) // 2
    slack = jnp.where((donor == order[0]) | (taker == order[0]) | (tallies[taker] == 0), 0, jnp.maximum(slack, 0))
    passed = jax.random.randint(jax.random.fold_in(own, 4), (number_of // 2,), 0, 1 << 20) % (slack + 1)
    tallies = tallies.at[donor].add(-passed).at[taker].add(passed)
    members = jnp.searchsorted(jnp.cumsum(tallies), jnp.arange(rows * top), side="right").astype(jnp.int32)
    table = members.reshape(top, rows).T
    table = table[jax.random.permutation(jax.random.fold_in(own, 1), rows)]
    offset_by = jax.random.randint(jax.random.fold_in(own, 2), (rows, 1), 0, top)
    return jnp.take_along_axis(table, (jnp.arange(top)[None, :] + offset_by) % top, axis=1)


def shares(count, total, bound, lean, full):
    weights = [(1 << 20) // math.isqrt(rank ** lean) + 1 for rank in range(1, count + 1)]
    largest = bound if full else min(bound, max(-(-total // count), total * weights[0] // sum(weights)))
    least = 1 if total - largest >= count - 1 else 0
    given, spare = [largest] + [least] * (count - 1), total - largest - least * (count - 1)
    while spare > 0:
        movable = [i for i in range(1, count) if given[i] < largest] or [i for i in range(1, count) if given[i] < bound]
        mass, budget = sum([weights[i] for i in movable]), spare
        for i in movable:
            more = min(bound - given[i], max(1, budget * weights[i] // mass), spare)
            given[i] = given[i] + more
            spare = spare - more
    return np.array(given)


def centred(stream_key, dims, scale, most, cuts=(), kind=jnp.bfloat16):
    result = jax.random.normal(stream_key, dims, jnp.float32) * scale
    if len(cuts) > 0:
        result = block_levels(stream_key, dims, cuts, -0.22, 0.18) * result
    return jnp.clip(result, min=-most, max=most).astype(kind)


def setup_inputs(seed: int = 0) -> dict:
    key_list = jax.random.split(jax.random.key(seed), 21)
    node = centred(key_list[0], (COMPLEXES, NODES, D), 1.0, 6.0, ((0, 4), (1, 8)))
    edge = centred(key_list[1], (COMPLEXES, NODES * K, DE), 1.0, 6.0, ((0, 4), (1, 8)))
    dest_device_keys = jax.random.split(jax.random.fold_in(key_list[2], 1), COMPLEXES * (NODES * K) // (NODE_DEV * K))
    dest_device_turns = jax.random.permutation(jax.random.fold_in(key_list[2], 3), COMPLEXES * (NODES * K) // (NODE_DEV * K))
    dest_device = jax.vmap(lambda own, number: shared_out(jax.random.fold_in(key_list[2], 2), own, number, NODE_DEV * K, N_EDGE, 1, MOST, 2))(dest_device_keys, dest_device_turns).reshape((COMPLEXES, NODES * K, 1))
    dest_local = plant(jax.random.randint(key_list[3], (COMPLEXES, NODES * K), 0, NODE_DEV), jax.random.fold_in(key_list[3], 1), 0, NODE_DEV - 1).astype(jnp.int32)
    node_valid = plant((jax.random.randint(key_list[4], (COMPLEXES, NODES), 0, 8) < 7).astype(jnp.int32), jax.random.fold_in(key_list[4], 1), 0, 1)
    node_cot = centred(key_list[5], (COMPLEXES, NODES, D), 1.0, 6.0, ((0, 4), (1, 8)))
    edge_cot = centred(key_list[6], (COMPLEXES, NODES * K, DE), 1.0, 6.0, ((0, 4), (1, 8)))
    big_weight = draw_big_weight(jax.random.fold_in(key_list[20], 71), 0)
    big_first = draw_big_first(jax.random.fold_in(key_list[20], 71), 0)
    big_second = draw_big_second(jax.random.fold_in(key_list[20], 71), 0)
    big_left = draw_big_left(jax.random.fold_in(key_list[20], 71), 0)
    big_right = draw_big_right(jax.random.fold_in(key_list[20], 71), 0)
    small_weight = draw_small_weight(jax.random.fold_in(key_list[20], 71), 0)
    small_first = draw_small_first(jax.random.fold_in(key_list[20], 71), 0)
    small_second = draw_small_second(jax.random.fold_in(key_list[20], 71), 0)
    small_left = draw_small_left(jax.random.fold_in(key_list[20], 71), 0)
    small_right = draw_small_right(jax.random.fold_in(key_list[20], 71), 0)
    norm_params = draw_norm_params(jax.random.fold_in(key_list[20], 71), 0)
    norm_first = draw_norm_first(jax.random.fold_in(key_list[20], 71), 0)
    norm_second = draw_norm_second(jax.random.fold_in(key_list[20], 71), 0)
    return {"node": node, "edge": edge, "dest_device": dest_device, "dest_local": dest_local, "node_valid": node_valid, "node_cot": node_cot, "edge_cot": edge_cot, "big_weight": big_weight, "big_first": big_first, "big_second": big_second, "big_left": big_left, "big_right": big_right, "small_weight": small_weight, "small_first": small_first, "small_second": small_second, "small_left": small_left, "small_right": small_right, "norm_params": norm_params, "norm_first": norm_first, "norm_second": norm_second}


BETA_ONE = 0.5
BETA_TWO = 0.5
EPS_ADAM = 1e-08
EPS_NORM = 1e-05
DECAY = 0.01
NORM_RATE = 0.4
PRECISION_HIGH = lax.Precision.HIGHEST

@jax.custom_vjp
def low(v):
    return lax.optimization_barrier(v.astype(jnp.bfloat16)).astype(jnp.float32)

@jax.custom_vjp
def low_back(v):
    return v

def low_keep(v):
    return (low(v), None)

def low_pass(kept, grad):
    return (grad,)

def back_keep(v):
    return (v, None)

def back_low(kept, grad):
    return (low(grad),)
low.defvjp(low_keep, low_pass)
low_back.defvjp(back_keep, back_low)

def big_shapes():
    return [(D, D), (D, D), (D, D), (D, D), (D, FF), (FF, D)]

def small_shapes():
    return [(DE, D), (D, DE), (D, DE), (DE, DE), (DE, DE), (DE, DE)]

def big_spreads():
    middle = (2 * D + DE) ** (-0.5)
    return [middle, middle, D ** (-0.5), 2.5 * D ** (-0.5), D ** (-0.5), FF ** (-0.5)]

def small_spreads():
    middle = (2 * D + DE) ** (-0.5)
    return [middle, middle, middle, middle, DE ** (-0.5), 1.5 * DE ** (-0.5)]

def rate_table(shapes, spreads):
    amounts = [height // TILE * (breadth // TILE) for height, breadth in shapes]
    return np.repeat(np.array(spreads, np.float32), amounts)

def as_square(flat_tiles):
    return flat_tiles.reshape(flat_tiles.shape[0], TILE, TILE)

def as_flat(square_tiles):
    return square_tiles.reshape(square_tiles.shape[0], TILE * TILE)

def from_tiles(tile_stack, shapes):
    matrices = []
    offset = 0
    for height, breadth in shapes:
        amount = height // TILE * (breadth // TILE)
        blocked = tile_stack[offset:offset + amount].reshape(height // TILE, breadth // TILE, TILE, TILE)
        matrices.append(blocked.transpose(0, 2, 1, 3).reshape(height, breadth))
        offset += amount
    return matrices

def split_norms(norm_vec):
    return (norm_vec[0:D], norm_vec[D:2 * D], norm_vec[2 * D:3 * D], norm_vec[3 * D:4 * D], norm_vec[4 * D:4 * D + DE], norm_vec[4 * D + DE:4 * D + 2 * DE])

def matmul(left_side, right_side):
    return jnp.dot(left_side, right_side, precision=PRECISION_HIGH, preferred_element_type=jnp.float32)

def layer_norm(values, gain_vec, offset):
    centre = lax.optimization_barrier(jnp.mean(values, axis=-1, keepdims=True))
    centered = values - centre
    spread = lax.optimization_barrier(jnp.mean(centered * centered, axis=-1, keepdims=True))
    return centered * lax.rsqrt(spread + EPS_NORM) * gain_vec + offset

def forward(big_tiles, small_tiles, norm_vec, features, edge_feats, targets, valid_mask):
    w_src, w_dst, w_mid, w_out, w_up, w_down = from_tiles(low(big_tiles), big_shapes())
    w_edge, e_src, e_dst, e_edge, e_mid, e_out = from_tiles(low(small_tiles), small_shapes())
    gain_one, shift_one, gain_two, shift_two, gain_three, shift_three = split_norms(norm_vec)
    group_size = NODES if NODES < 64 else 64
    blocks = NODES // group_size
    flat_targets = targets.reshape(NODES * K)
    flat_edges = edge_feats.reshape(NODES * K, DE)
    from_source = low_back(matmul(features, w_src))
    from_target = low_back(low(matmul(features, w_dst)))

    def message_block(pieces):
        source_rows, edge_rows, target_rows = pieces
        pre_act = jnp.repeat(source_rows, K, axis=0) + from_target[target_rows] + matmul(edge_rows, w_edge)
        pre_act = low_back(pre_act)
        hidden = low(jax.nn.gelu(pre_act))
        second = low_back(matmul(hidden, w_mid))
        hidden_two = low(jax.nn.gelu(second))
        return low_back(low(matmul(hidden_two, w_out)))
    messages = lax.map(jax.checkpoint(message_block), (from_source.reshape(blocks, group_size, D), flat_edges.reshape(blocks, group_size * K, DE), flat_targets.reshape(blocks, group_size * K)))
    edge_ok = jnp.repeat(valid_mask, K)
    msg_totals = jax.ops.segment_sum(messages.reshape(NODES * K, D) * edge_ok[:, None], flat_targets, num_segments=NODES)
    counts = jax.ops.segment_sum(edge_ok, flat_targets, num_segments=NODES) * valid_mask
    denominator = jnp.maximum(counts, 1.0)
    mean_msg = msg_totals * valid_mask[:, None] / denominator[:, None]
    updated = layer_norm(features + mean_msg, gain_one, shift_one)
    widened = low_back(matmul(low(updated), w_up))
    narrowed = low_back(matmul(low(jax.nn.gelu(widened)), w_down))
    node_final = layer_norm(updated + narrowed, gain_two, shift_two)
    node_low = low(node_final)
    to_source = low_back(matmul(node_low, e_src))
    to_target = low_back(low(matmul(node_low, e_dst)))

    def edge_block(pieces):
        source_rows, edge_rows, target_rows = pieces
        pre_act = low_back(jnp.repeat(source_rows, K, axis=0) + to_target[target_rows] + matmul(edge_rows, e_edge))
        hidden = low(jax.nn.gelu(pre_act))
        second = low_back(matmul(hidden, e_mid))
        change = low_back(matmul(low(jax.nn.gelu(second)), e_out))
        return layer_norm(edge_rows + change, gain_three, shift_three)
    edge_final = lax.map(jax.checkpoint(edge_block), (to_source.reshape(blocks, group_size, DE), flat_edges.reshape(blocks, group_size * K, DE), flat_targets.reshape(blocks, group_size * K)))
    return (node_final, edge_final.reshape(NODES * K, DE))

def soap_step(weight, moment_one, moment_two, left_basis, right_basis, gradient, step_rates):
    turned = jnp.einsum('tji,tjk->tik', left_basis, gradient, precision=PRECISION_HIGH)
    turned = jnp.einsum('tik,tkl->til', turned, right_basis, precision=PRECISION_HIGH)
    new_one = BETA_ONE * moment_one + (1.0 - BETA_ONE) * turned
    new_two = BETA_TWO * moment_two + (1.0 - BETA_TWO) * turned * turned
    direction = new_one / (1.0 - BETA_ONE ** STEP) / (jnp.sqrt(new_two / (1.0 - BETA_TWO ** STEP)) + EPS_ADAM)
    restored = jnp.einsum('tij,tjk->tik', left_basis, direction, precision=PRECISION_HIGH)
    restored = jnp.einsum('tik,tlk->til', restored, right_basis, precision=PRECISION_HIGH)
    weight_new = weight - step_rates[:, None, None] * (restored + DECAY * weight)
    return (new_one, new_two, weight_new)

def adam_step(params, moment_one, moment_two, gradient):
    new_one = BETA_ONE * moment_one + (1.0 - BETA_ONE) * gradient
    new_two = BETA_TWO * moment_two + (1.0 - BETA_TWO) * gradient * gradient
    direction = new_one / (1.0 - BETA_ONE ** STEP) / (jnp.sqrt(new_two / (1.0 - BETA_TWO ** STEP)) + EPS_ADAM)
    return (new_one, new_two, params - NORM_RATE * direction)

def reference(node, edge, dest_device, dest_local, node_valid, node_cot, edge_cot, big_weight, big_first, big_second, big_left, big_right, small_weight, small_first, small_second, small_left, small_right, norm_params, norm_first, norm_second):
    big_master = as_square(big_weight)
    small_master = as_square(small_weight)
    targets_all = (dest_device[..., 0] * NODE_DEV + dest_local).astype(jnp.int32)
    valid_all = node_valid.astype(jnp.float32)

    def one_complex(totals, pieces):
        features, edge_feats, targets, valid_mask, node_back, edge_back = pieces

        def forward_one(big_tiles, small_tiles, norm_vec, feats, edge_vals):
            return forward(big_tiles, small_tiles, norm_vec, feats, edge_vals, targets, valid_mask)
        outputs, pullback = jax.vjp(forward_one, big_master, small_master, norm_params, features.astype(jnp.float32), edge_feats.astype(jnp.float32))
        grads_all = pullback((node_back.astype(jnp.float32), edge_back.astype(jnp.float32)))
        totals = (totals[0] + grads_all[0], totals[1] + grads_all[1], totals[2] + grads_all[2])
        return (totals, (outputs[0].astype(jnp.bfloat16), outputs[1].astype(jnp.bfloat16), grads_all[3], grads_all[4]))
    zero_grads = (jnp.zeros_like(big_master), jnp.zeros_like(small_master), jnp.zeros_like(norm_params))
    totals, (node_out, edge_out, node_grad, edge_grad) = lax.scan(one_complex, zero_grads, (node, edge, targets_all, valid_all, node_cot, edge_cot))
    grad_scale = 1.0 / math.sqrt(COMPLEXES * NODES * K)
    big_rates = jnp.asarray(rate_table(big_shapes(), big_spreads()))
    small_rates = jnp.asarray(rate_table(small_shapes(), small_spreads()))
    big_one, big_two, big_new = soap_step(big_master, as_square(big_first), as_square(big_second), as_square(big_left), as_square(big_right), totals[0] * grad_scale, big_rates)
    small_one, small_two, small_new = soap_step(small_master, as_square(small_first), as_square(small_second), as_square(small_left), as_square(small_right), totals[1] * grad_scale, small_rates)
    norm_one, norm_two, norm_new = adam_step(norm_params, norm_first, norm_second, totals[2] * grad_scale)
    return (node_out, edge_out, node_grad, edge_grad, as_flat(big_one), as_flat(big_two), as_flat(big_new), as_flat(big_new).astype(jnp.bfloat16), as_flat(small_one), as_flat(small_two), as_flat(small_new), as_flat(small_new).astype(jnp.bfloat16), norm_one, norm_two, norm_new)
```

```python
import functools
import math

import jax
import jax.numpy as jnp
import numpy as np
from jax import lax
from jax.experimental import pallas as pl
from jax.experimental.pallas import tpu as pltpu
from jax.sharding import Mesh
from jax.sharding import PartitionSpec as P

D = 512
DE = 192
FF = 2048
K = 60
TILE = 64
STEP = 10


BETA_ONE = 0.5
BETA_TWO = 0.5
EPS_ADAM = 1e-08
EPS_NORM = 1e-05
DECAY = 0.01
NORM_RATE = 0.4
PRECISION_HIGH = lax.Precision.HIGHEST


def big_shapes():
    return [(D, D), (D, D), (D, D), (D, D), (D, FF), (FF, D)]


def small_shapes():
    return [(DE, D), (D, DE), (D, DE), (DE, DE), (DE, DE), (DE, DE)]


def big_spreads():
    middle = (2 * D + DE) ** (-0.5)
    return [middle, middle, D ** (-0.5), 2.5 * D ** (-0.5), D ** (-0.5), FF ** (-0.5)]


def small_spreads():
    middle = (2 * D + DE) ** (-0.5)
    return [middle, middle, middle, middle, DE ** (-0.5), 1.5 * DE ** (-0.5)]


def rate_table(shapes, spreads):
    amounts = [height // TILE * (breadth // TILE) for height, breadth in shapes]
    return np.repeat(np.array(spreads, np.float32), amounts)


def as_square(flat_tiles):
    return flat_tiles.reshape(flat_tiles.shape[0], TILE, TILE)


def as_flat(square_tiles):
    return square_tiles.reshape(square_tiles.shape[0], TILE * TILE)


def from_tiles(tile_stack, shapes):
    matrices = []
    offset = 0
    for height, breadth in shapes:
        amount = height // TILE * (breadth // TILE)
        blocked = tile_stack[offset : offset + amount].reshape(
            height // TILE, breadth // TILE, TILE, TILE
        )
        matrices.append(blocked.transpose(0, 2, 1, 3).reshape(height, breadth))
        offset += amount
    return matrices


def to_flat_tiles(matrix):
    height, breadth = matrix.shape
    blocked = matrix.reshape(height // TILE, TILE, breadth // TILE, TILE)
    return blocked.transpose(0, 2, 1, 3).reshape(-1, TILE * TILE)


def adam_step(params, moment_one, moment_two, gradient):
    new_one = BETA_ONE * moment_one + (1.0 - BETA_ONE) * gradient
    new_two = BETA_TWO * moment_two + (1.0 - BETA_TWO) * gradient * gradient
    direction = (
        new_one / (1.0 - BETA_ONE**STEP) / (jnp.sqrt(new_two / (1.0 - BETA_TWO**STEP)) + EPS_ADAM)
    )
    return (new_one, new_two, params - NORM_RATE * direction)


def times_transposed(left_side, right_side):
    return lax.dot_general(
        left_side, right_side, (((1,), (1,)), ((), ())), preferred_element_type=jnp.float32
    )


LOW = jnp.bfloat16
WIDE = 256
GELU_A = math.sqrt(2.0 / math.pi)
GELU_B = GELU_A * 0.044715
OWNED_ROWS = 3 * TILE


def dot(left, right):
    return jnp.dot(left, right, preferred_element_type=jnp.float32)


def dot_rows(left, right):
    return lax.dot_general(
        left, right, (((0,), (0,)), ((), ())), preferred_element_type=jnp.float32
    )


def dot_turned(left, right):
    return lax.dot_general(
        left, right, (((1,), (1,)), ((), ())), preferred_element_type=jnp.float32
    )


def split_low(values):
    high = values.astype(LOW)
    return high, (values - high.astype(jnp.float32)).astype(LOW)


def gelu_pair(v):
    square = v * v
    half = 0.5 * jnp.tanh(v * (GELU_A + GELU_B * square)) + 0.5
    out = v * half
    slope = half + out * (1.0 - half) * (2.0 * GELU_A + 6.0 * GELU_B * square)
    return out, slope


def norm_parts(values, width):
    centre = jnp.sum(values, axis=-1, keepdims=True) * (1.0 / width)
    centered = values - centre
    if values.shape[-1] != width:
        lane = lax.broadcasted_iota(jnp.int32, values.shape, 1)
        centered = jnp.where(lane < width, centered, 0.0)
    spread = jnp.sum(centered * centered, axis=-1, keepdims=True) * (1.0 / width)
    inverse = lax.rsqrt(spread + EPS_NORM)
    return centered * inverse, inverse


def norm_back(scaled, inverse, gain, upstream, width):
    inner = upstream * gain
    mean_inner = jnp.sum(inner, axis=-1, keepdims=True) * (1.0 / width)
    mean_cross = jnp.sum(inner * scaled, axis=-1, keepdims=True) * (1.0 / width)
    return inverse * (inner - mean_inner - scaled * mean_cross)


def whole(shape):
    return pl.BlockSpec(shape, lambda *_: (0,) * len(shape), pipeline_mode=pl.Buffered(1))


def anywhere(values):
    return [pl.BlockSpec(memory_space=pl.ANY)] * len(values)


def kept(shape):
    return pl.BlockSpec(shape, lambda *_: (0,) * len(shape))


def params(limit=58):
    return pltpu.CompilerParams(vmem_limit_bytes=limit * 2**20)


def shaped(shape, dtype):
    return jax.ShapeDtypeStruct(shape, dtype)


def trimmed(kernel, inputs, unread):
    def run(*refs):
        kernel(*refs[:inputs], *refs[inputs + unread :])

    return run


def prepare_kernel(targets, valid, edge, tall, wide, ok_row):
    nodes, block = tall.shape
    group = block // K
    down = lax.broadcasted_iota(jnp.int32, (nodes, block), 0)
    hot = jnp.where(down == targets[...], 1.0, 0.0)
    tall[...] = hot.astype(LOW)
    row = lax.broadcasted_iota(jnp.int32, (WIDE - DE, block), 0)
    source = lax.broadcasted_iota(jnp.int32, (WIDE - DE, block), 1) // K
    picked = jnp.where((row == source) | (row == source + group), 1.0, 0.0)
    wide[0:DE] = edge[...]
    wide[DE:WIDE] = picked.astype(LOW)
    ok = jnp.sum(picked[0:group] * valid[...], axis=0, keepdims=True)
    ok_row[...] = ok


def block_of():
    return 32 * K


def lanes(height, block):
    return pl.BlockSpec((height, block), lambda i: (0, i))


def tall_lanes(nodes, block):
    buffers = pl.Buffered(2 if nodes <= 1024 else 1)
    return pl.BlockSpec((nodes, block), lambda i: (0, i), pipeline_mode=buffers)


def prepare(targets, valid, edge_across, nodes):
    rows = edge_across.shape[1]
    block = block_of()
    return pl.pallas_call(
        prepare_kernel,
        grid=(rows // block,),
        in_specs=[
            lanes(1, block),
            pl.BlockSpec((block // K, 1), lambda i: (i, 0)),
            lanes(DE, block),
        ],
        out_specs=[
            lanes(nodes, block),
            lanes(WIDE, block),
            lanes(1, block),
        ],
        out_shape=[
            shaped((nodes, rows), LOW),
            shaped((WIDE, rows), LOW),
            shaped((1, rows), jnp.float32),
        ],
        compiler_params=params(),
    )(targets, valid, edge_across)


def source_rows(values):
    high = values.astype(LOW).astype(jnp.float32)
    return jnp.concatenate([high, values - high], axis=0).astype(LOW)


def put_halves(halves, total, owned):
    for index in range(total.shape[0] // owned):
        rows = total[index * owned : (index + 1) * owned].astype(LOW)
        halves[index % 2][index // 2, 0:owned, :] = rows


COUNT_ROWS = 16


def message_kernel(
    tall, wide, ok_row, w_rows, w_edge, x_all,
    even, odd, hidden_out, slope_one, slope_two,
    table, mixed, from_source, total, mid, counts,
):
    step = pl.program_id(0)
    owned = from_source.shape[0]

    @pl.when(step == 0)
    def _():
        table[...] = dot(x_all[...], w_rows[D : 2 * D]).astype(LOW).T
        from_source[...] = dot(x_all[0:owned], w_rows[0:D])
        mixed[0:DE] = w_edge[...]
        mid[...] = w_rows[2 * D : 3 * D].T
        total[...] = jnp.zeros_like(total)
        counts[...] = jnp.zeros_like(counts)

    group = hidden_out.shape[1] // K
    mixed[DE:WIDE] = source_rows(from_source[pl.ds(step * group, group), :])
    pre = dot(table[...], tall[...]) + dot_rows(mixed[...], wide[...])
    hidden, slope = gelu_pair(pre)
    hidden = hidden.astype(LOW)
    hidden_out[...] = hidden
    slope_one[...] = slope.astype(LOW)
    second, slope = gelu_pair(dot(mid[...], hidden))
    ok = ok_row[...]
    slope_two[...] = (slope * ok).astype(LOW)
    total[...] += dot_turned(tall[...], (second * ok).astype(LOW))
    ok_rows = jnp.broadcast_to(ok, (COUNT_ROWS, ok.shape[1])).astype(LOW)
    counts[...] += dot_turned(ok_rows, tall[...])

    @pl.when(step == pl.num_programs(0) - 1)
    def _():
        put_halves((even, odd), total, owned)
        for index in range(total.shape[0] // owned):
            amount = counts[:, index * owned : (index + 1) * owned]
            high = jnp.floor(amount * (1.0 / LANES))
            place = (even, odd)[index % 2].at[index // 2]
            rows = pl.ds(owned, COUNT_ROWS)
            place[rows, :] = jnp.zeros((COUNT_ROWS, D), LOW)
            place[rows, 0:owned] = high.astype(LOW)
            place[rows, LANES : LANES + owned] = (amount - high * LANES).astype(LOW)


def message_forward(tall, wide, ok_row, x_all, owned, w_rows, w_edge, after):
    nodes, rows = tall.shape
    block = block_of()
    half = (nodes // owned // 2, owned + COUNT_ROWS, D)
    return pl.pallas_call(
        trimmed(message_kernel, 6, len(after)),
        grid=(rows // block,),
        in_specs=[
            tall_lanes(nodes, block),
            lanes(WIDE, block),
            lanes(1, block),
            whole((3 * D, D)),
            whole((DE, D)),
            whole((nodes, D)),
        ]
        + anywhere(after),
        out_specs=[kept(half), kept(half)] + [lanes(D, block)] * 3,
        out_shape=[shaped(half, LOW)] * 2 + [shaped((D, rows), LOW)] * 3,
        scratch_shapes=[
            pltpu.VMEM((D, nodes), LOW),
            pltpu.VMEM((WIDE, D), LOW),
            pltpu.VMEM((owned, D), jnp.float32),
            pltpu.VMEM((nodes, D), jnp.float32),
            pltpu.VMEM((D, D), LOW),
            pltpu.VMEM((COUNT_ROWS, nodes), jnp.float32),
        ],
        compiler_params=params(),
    )(tall, wide, ok_row, w_rows, w_edge, x_all, *after)


def up_part(blocks, part):
    per, parts = D // TILE, FF // D
    strips = [blocks[4 * per + row * parts + part] for row in range(per)]
    return jnp.concatenate(strips, axis=0)


def out_part(blocks):
    per = D // TILE
    return blocks[3 * per : 4 * per].reshape(D, D)


def down_part(blocks, part):
    per = D // TILE
    first = per * (4 + FF // D + part)
    return blocks[first : first + per].reshape(D, D)


def node_forward_kernel(x, valid, blocks, u_src, u_dst, norms, *refs):
    pieces = refs[:-10]
    (
        low_out, q_src, q_dst, inside_out, one_out, act_out, slope_out, summed_out, scale_out,
        sums_out,
    ) = refs[-10:]
    summed_all = sum(piece[...].astype(jnp.float32) for piece in pieces)
    owned = x.shape[0]
    sums = summed_all[0:owned]
    tally = summed_all[owned : owned + 8, 0:LANES] * float(LANES)
    tally += summed_all[owned : owned + 8, LANES : 2 * LANES]
    amount = tally.T[0:owned, 0:1]
    scale = valid[...] / jnp.maximum(amount * valid[...], 1.0)
    scale_out[...] = scale
    sums_out[...] = sums
    high, low = split_low(sums * scale)
    w_out = out_part(blocks)
    inside = x[...].astype(jnp.float32) + (dot(high, w_out) + dot(low, w_out))
    scaled, _ = norm_parts(inside, D)
    one = scaled * norms[0:1] + norms[1:2]
    one_low = one.astype(LOW)
    narrowed = jnp.zeros_like(one)
    for part in range(FF // D):
        act, slope = gelu_pair(dot(one_low, up_part(blocks, part)))
        act = act.astype(LOW)
        act_out[:, part * D : (part + 1) * D] = act
        slope_out[:, part * D : (part + 1) * D] = slope.astype(LOW)
        narrowed += dot(act, down_part(blocks, part))
    summed = one + narrowed
    scaled, _ = norm_parts(summed, D)
    two = (scaled * norms[2:3] + norms[3:4]).astype(LOW)
    low_out[...] = two
    q_src[...] = dot(two, u_src[...])
    q_dst[...] = dot(two, u_dst[...]).astype(LOW)
    inside_out[...] = inside
    one_out[...] = one
    summed_out[...] = summed


def node_forward(x, valid, blocks, u_src, u_dst, norms, pieces, after):
    owned = x.shape[0]
    wide = shaped((owned, D), jnp.float32)
    operands = [x, valid, blocks, u_src, u_dst, norms, *pieces]
    return pl.pallas_call(
        trimmed(node_forward_kernel, len(operands), len(after)),
        in_specs=[pl.BlockSpec(memory_space=pltpu.VMEM)] * len(operands) + anywhere(after),
        out_shape=[
            shaped((owned, D), LOW),
            shaped((owned, WIDE), jnp.float32),
            shaped((owned, WIDE), LOW),
            wide,
            wide,
            shaped((owned, FF), LOW),
            shaped((owned, FF), LOW),
            wide,
            shaped((owned, 1), jnp.float32),
            wide,
        ],
        compiler_params=params(),
    )(*operands, *after)


def tall_norm(values):
    width = values.shape[0]
    centre = jnp.sum(values, axis=0, keepdims=True) * (1.0 / width)
    centered = values - centre
    spread = jnp.sum(centered * centered, axis=0, keepdims=True) * (1.0 / width)
    inverse = lax.rsqrt(spread + EPS_NORM)
    return centered * inverse, inverse


def tall_norm_back(scaled, inverse, gain, upstream):
    width = scaled.shape[0]
    inner = upstream * gain
    mean_inner = jnp.sum(inner, axis=0, keepdims=True) * (1.0 / width)
    mean_cross = jnp.sum(inner * scaled, axis=0, keepdims=True) * (1.0 / width)
    return inverse * (inner - mean_inner - scaled * mean_cross)


def lane_sums(values):
    return sum(
        values[:, first : first + LANES] for first in range(0, values.shape[1], LANES)
    )


def edge_kernel(count, tall, wide, cot, q_src, u_edge, u_mid, u_out, norms, *refs):
    pieces = refs[0:count]
    (
        edge_out, d_edge, even, odd, d_source, g_edge, g_mid, g_out, g_norms,
        table, mixed, total, mid_turned, out_turned, gain_sum, shift_sum, columns,
    ) = refs[-17:]
    step = pl.program_id(0)
    last = pl.num_programs(0) - 1
    owned = q_src.shape[0]

    @pl.when(step == 0)
    def _():
        table[...] = jnp.concatenate([piece[...] for piece in pieces], axis=0).T
        mixed[0:DE] = u_edge[...]
        mid_turned[...] = u_mid[...].T
        out_turned[...] = u_out[...].T
        columns[...] = norms[...].T
        for ref in (total, gain_sum, shift_sum, g_edge, g_mid, g_out):
            ref[...] = jnp.zeros_like(ref)

    group = edge_out.shape[1] // K
    mixed[DE:WIDE] = source_rows(q_src[pl.ds(step * group, group), :])
    both = wide[...]
    first, slope_one = gelu_pair(
        dot(table[0:DE], tall[...]) + dot(mixed[...].T[0:DE], both)
    )
    first = first.astype(LOW)
    second, slope_two = gelu_pair(dot(mid_turned[0:DE, 0:DE], first))
    second = second.astype(LOW)
    change = dot(out_turned[0:DE, 0:DE], second)
    scaled, inverse = tall_norm(both[0:DE].astype(jnp.float32) + change)
    gain, offset = columns[0:DE, 0:1], columns[0:DE, 1:2]
    edge_out[...] = (scaled * gain + offset).astype(LOW)
    back = cot[...].astype(jnp.float32)
    gain_sum[...] += lane_sums(back * scaled)
    shift_sum[...] += lane_sums(back)
    d_sum = tall_norm_back(scaled, inverse, gain, back)
    d_change = d_sum.astype(LOW)
    g_out[0:DE, 0:DE] += dot_turned(second, d_change)
    d_second = (dot(u_out[:, 0:DE], d_change) * slope_two).astype(LOW)
    g_mid[0:DE, 0:DE] += dot_turned(first, d_second)
    d_first = (dot(u_mid[:, 0:DE], d_second) * slope_one).astype(LOW)
    d_edge[...] = d_sum + dot(u_edge[:, 0:DE], d_first)
    turned = dot_turned(both, d_first)
    g_edge[:, 0:DE] += turned[0:DE]
    d_source[pl.ds(step * group, group), :] = turned[DE : DE + group]
    total[:, 0:DE] += dot_turned(tall[...], d_first)

    @pl.when(step == last)
    def _():
        put_halves((even, odd), total, owned)
        gain_row = jnp.sum(gain_sum[...].T, axis=0, keepdims=True)
        shift_row = jnp.sum(shift_sum[...].T, axis=0, keepdims=True)
        both_rows = jnp.concatenate([gain_row, shift_row], axis=1)
        g_norms[...] = jnp.zeros_like(g_norms)
        for index in range(3):
            g_norms[index : index + 1] = both_rows[:, index * LANES : (index + 1) * LANES]


def edge_phase(tall, wide, cot, pieces, q_src, u_edge, u_mid, u_out, norms, after):
    nodes, rows = tall.shape
    owned = q_src.shape[0]
    block = block_of()
    count = len(pieces)
    half = (count // 2, owned, WIDE)
    square = shaped((DE, WIDE), jnp.float32)
    line = shaped((8, LANES), jnp.float32)
    return pl.pallas_call(
        functools.partial(edge_kernel, count),
        grid=(rows // block,),
        in_specs=[
            tall_lanes(nodes, block),
            lanes(WIDE, block),
            lanes(DE, block),
            whole((owned, WIDE)),
            whole((DE, WIDE)),
            whole((DE, WIDE)),
            whole((DE, WIDE)),
            whole((8, WIDE)),
        ]
        + [whole((owned, WIDE))] * count
        + anywhere(after),
        out_specs=[
            lanes(DE, block),
            lanes(DE, block),
            kept(half),
            kept(half),
            kept((owned, DE)),
            kept((DE, WIDE)),
            kept((DE, WIDE)),
            kept((DE, WIDE)),
            kept((8, LANES)),
        ],
        out_shape=[
            shaped((DE, rows), LOW),
            shaped((DE, rows), jnp.float32),
            shaped(half, LOW),
            shaped(half, LOW),
            shaped((owned, DE), jnp.float32),
            square,
            square,
            square,
            line,
        ],
        scratch_shapes=[
            pltpu.VMEM((WIDE, nodes), LOW),
            pltpu.VMEM((WIDE, WIDE), LOW),
            pltpu.VMEM((nodes, WIDE), jnp.float32),
            pltpu.VMEM((WIDE, DE), LOW),
            pltpu.VMEM((WIDE, DE), LOW),
            pltpu.VMEM((DE, LANES), jnp.float32),
            pltpu.VMEM((DE, LANES), jnp.float32),
            pltpu.VMEM((WIDE, 8), jnp.float32),
        ],
        compiler_params=params(),
    )(tall, wide, cot, q_src, u_edge, u_mid, u_out, norms, *pieces, *after)


def put_blocks(ref, base, matrix, step=1):
    for row in range(matrix.shape[0] // TILE):
        strip = matrix[row * TILE : (row + 1) * TILE].astype(ref.dtype)
        owner, batch, slot = early_place(base + row * step)
        for part in range(4):
            ref[owner, batch, part, slot * TILE : (slot + 1) * TILE, :] = strip[
                :, part * LANES : (part + 1) * LANES
            ]


def put_sides(refs, core, stores):
    for own in range(2):

        @pl.when(core == own)
        def _():
            for side, value, index in stores:
                refs[side ^ own][index] = value


def small_stores(batch, begin, matrix):
    stores = []
    piece = EARLY_ROWS // 8
    end = begin + matrix.shape[0]
    first = begin
    while first < end:
        index, offset = first // piece, first % piece
        amount = min(end - first, piece - offset)
        value = matrix[first - begin : first - begin + amount].astype(LOW)
        place = (index % 4 ^ batch, slice(offset, offset + amount), slice(None))
        stores.append((index // 4, value, place))
        first += amount
    return stores


def put_norm(ref, index, values):
    total = jnp.sum(values, axis=0, keepdims=True)
    for part in range(4):
        row = index * 4 + part
        ref[row : row + 1, 0:LANES] = total[:, part * LANES : (part + 1) * LANES]


def early_place(block):
    batch, rest = block // 24, block % 24
    return rest // 3, batch, rest % 3


def node_backward_kernel(
    place, cot, d_q_src, low, summed, one, inside, act, slope, scale, sums,
    blocks, u_src, u_dst, norms, g_edge, g_mid, g_out, g_edge_norms, *refs,
):
    reply, d_inside_out, g_blocks, g_even, g_odd, g_norms = refs[-6:]
    pieces = refs[:-6]
    core, batch = place[1], place[2]
    stores = []
    d_src = d_q_src[...].astype(LOW)
    d_dst = sum(piece[...].astype(jnp.float32) for piece in pieces).astype(LOW)
    low_now = low[...]
    blank = jnp.zeros((D, WIDE - DE), jnp.float32)
    stores += small_stores(batch, 0, jnp.concatenate([dot_rows(low_now, d_src), blank], axis=1))
    stores += small_stores(batch, D, dot_rows(low_now, d_dst))
    for index, ref in enumerate((g_edge, g_mid, g_out)):
        stores += small_stores(batch, 2 * D + index * DE, ref[...])
    g_norms[...] = jnp.zeros_like(g_norms)
    g_norms[16:24, 0:LANES] = g_edge_norms[...]
    d_final = (
        cot[...].astype(jnp.float32)
        + dot_turned(d_src, u_src[:, 0:DE])
        + dot_turned(d_dst, u_dst[...])
    )
    scaled, inverse = norm_parts(summed[...], D)
    d_summed = norm_back(scaled, inverse, norms[2:3], d_final, D)
    put_norm(g_norms, 2, d_final * scaled)
    put_norm(g_norms, 3, d_final)
    d_narrow = d_summed.astype(LOW)
    one_low = one[...].astype(LOW)
    d_one = d_summed
    first_up = D // TILE
    parts = FF // D
    first_down = first_up + first_up * parts
    for part in range(parts):
        cols = slice(part * D, (part + 1) * D)
        put_blocks(g_blocks, first_down + part * first_up, dot_rows(act[:, cols], d_narrow))
        d_wide = (
            dot_turned(d_narrow, down_part(blocks, part)) * slope[:, cols].astype(jnp.float32)
        ).astype(LOW)
        put_blocks(g_blocks, first_up + part, dot_rows(one_low, d_wide), parts)
        d_one += dot_turned(d_wide, up_part(blocks, part))
    scaled, inverse = norm_parts(inside[...], D)
    d_inside = norm_back(scaled, inverse, norms[0:1], d_one, D)
    put_norm(g_norms, 0, d_one * scaled)
    put_norm(g_norms, 1, d_one)
    d_inside_out[...] = d_inside
    per_target = (d_inside * scale[...]).astype(LOW)
    high, rest = split_low(sums[...])
    put_blocks(g_blocks, 0, dot_rows(high, per_target) + dot_rows(rest, per_target))
    reply[...] = dot_turned(per_target, out_part(blocks)).astype(LOW)
    stores += small_stores(batch, 2 * D + 3 * DE, g_norms[...])
    put_sides((g_even, g_odd), core, stores)


def node_backward(place, operands, pieces, after):
    owned = operands[0].shape[0]
    half = shaped((4, EARLY_ROWS // 8, WIDE), LOW)
    amount = len(operands) + len(pieces)
    return pl.pallas_call(
        trimmed(node_backward_kernel, amount + 1, len(after)),
        in_specs=[pl.BlockSpec(memory_space=pltpu.SMEM)]
        + [pl.BlockSpec(memory_space=pltpu.VMEM)] * amount
        + anywhere(after),
        out_shape=[
            shaped((owned, D), LOW),
            shaped((owned, D), jnp.float32),
            shaped((8, 3, 4, OWNED_ROWS, LANES), LOW),
            half,
            half,
        ],
        scratch_shapes=[pltpu.VMEM((TILE, WIDE), jnp.float32)],
        compiler_params=params(),
    )(place, *operands, *pieces, *after)


def message_back_kernel(
    count, place, tall, wide, hidden, slope_one, slope_two, part_edge, x_all, w_mid, w_edge, *refs
):
    pieces = refs[0:count]
    (
        d_edge, even, odd, d_source, late_even, late_odd, table, total, g_mid, g_edge, from_source,
    ) = refs[-11:]
    step = pl.program_id(0)
    owned = d_source.shape[0]

    @pl.when(step == 0)
    def _():
        table[...] = jnp.concatenate([piece[...] for piece in pieces], axis=0).T
        total[...] = jnp.zeros_like(total)
        g_mid[...] = jnp.zeros_like(g_mid)
        g_edge[...] = jnp.zeros_like(g_edge)

    d_hidden = dot(table[...], tall[...])
    d_second = (d_hidden * slope_two[...].astype(jnp.float32)).astype(LOW)
    g_mid[...] += dot_turned(hidden[...], d_second)
    d_pre = (dot(w_mid[...], d_second) * slope_one[...].astype(jnp.float32)).astype(LOW)
    d_edge[...] = part_edge[...] + dot(w_edge[...], d_pre)
    turned = dot_turned(wide[...], d_pre)
    g_edge[...] += turned[0:DE]
    group = hidden.shape[1] // K
    from_source[pl.ds(step * group, group), :] = turned[DE : DE + group]
    total[...] += dot_turned(tall[...], d_pre)

    @pl.when(step == pl.num_programs(0) - 1)
    def _():
        put_halves((even, odd), total, owned)
        gathered = x_all[...]
        sources_low = from_source[...].astype(LOW)
        d_source[...] = sources_low
        chip, core, batch = place[0], place[1], place[2]
        matrices = (
            dot_rows(gathered[0:owned], sources_low),
            dot_rows(gathered, total[...].astype(LOW)),
            g_mid[...],
        )
        stores = []
        for row in range(3 * (D // TILE)):
            owner, slot = row // 3, row % 3
            strip = matrices[row // (D // TILE)][row % (D // TILE) * TILE :][0:TILE].astype(LOW)
            first = pl.multiple_of((owner // 2 ^ chip) * OWNED_ROWS + slot * TILE, TILE)
            for part in range(4):
                value = strip[:, part * LANES : (part + 1) * LANES]
                stores.append((owner % 2, value, (part ^ batch, pl.ds(first, TILE), slice(None))))
        half = DE // 2
        for side in range(2):
            strip = g_edge[side * half : (side + 1) * half].astype(LOW)
            for part in range(4):
                value = strip[:, part * LANES : (part + 1) * LANES]
                rows = slice(4 * OWNED_ROWS, 4 * OWNED_ROWS + half)
                stores.append((side, value, (part ^ batch, rows, slice(None))))
        put_sides((late_even, late_odd), core, stores)


def message_backward(
    place, tall, wide, hidden, slope_one, slope_two, part_edge, x_all, w_rows, w_edge, pieces, after
):
    nodes, rows = tall.shape
    owned = pieces[0].shape[0]
    block = block_of()
    count = len(pieces)
    half = (count // 2, owned, D)
    feature = tall_lanes(D, block) if nodes <= 1024 else pl.BlockSpec(
        (D, block), lambda i: (0, i), pipeline_mode=pl.Buffered(1)
    )
    late = (4, 4 * OWNED_ROWS + DE // 2, LANES)
    return pl.pallas_call(
        functools.partial(message_back_kernel, count),
        grid=(rows // block,),
        in_specs=[
            pl.BlockSpec(memory_space=pltpu.SMEM),
            tall_lanes(nodes, block),
            lanes(WIDE, block),
            feature,
            feature,
            feature,
            lanes(DE, block),
            whole((nodes, D)),
            pl.BlockSpec((D, D), lambda i: (2, 0), pipeline_mode=pl.Buffered(1)),
            whole((DE, D)),
        ]
        + [whole((owned, D))] * count
        + anywhere(after),
        out_specs=[
            lanes(DE, block),
            kept(half),
            kept(half),
            kept((owned, D)),
            kept(late),
            kept(late),
        ],
        out_shape=[
            shaped((DE, rows), jnp.float32),
            shaped(half, LOW),
            shaped(half, LOW),
            shaped((owned, D), LOW),
            shaped(late, LOW),
            shaped(late, LOW),
        ],
        scratch_shapes=[
            pltpu.VMEM((D, nodes), LOW),
            pltpu.VMEM((nodes, D), jnp.float32),
            pltpu.VMEM((D, D), jnp.float32),
            pltpu.VMEM((DE, D), jnp.float32),
            pltpu.VMEM((owned, D), jnp.float32),
        ],
        compiler_params=params(),
    )(
        place, tall, wide, hidden, slope_one, slope_two, part_edge, x_all, w_rows, w_edge,
        *pieces, *after,
    )


def node_gradient_kernel(inside, d_source, w_rows, *refs):
    pieces, out = refs[:-1], refs[-1]
    d_target = sum(piece[...].astype(jnp.float32) for piece in pieces).astype(LOW)
    out[...] = (
        inside[...]
        + dot_turned(d_source[...], w_rows[0:D])
        + dot_turned(d_target, w_rows[D : 2 * D])
    )


def node_gradient(inside, d_source, w_rows, pieces):
    return pl.pallas_call(
        node_gradient_kernel,
        out_shape=shaped(inside.shape, jnp.float32),
        compiler_params=params(),
    )(inside, d_source, w_rows, *pieces)


def add_halves_kernel(left, right, *outs):
    for index, out in enumerate(outs):
        total = left[index].astype(jnp.float32) + right[index].astype(jnp.float32)
        out[...] = total.astype(out.dtype)


def add_halves(left, right):
    shape = left.shape[1:]
    return pl.pallas_call(
        add_halves_kernel,
        out_shape=[shaped(shape, jnp.float32)] + [shaped(shape, LOW)] * (left.shape[0] - 1),
        compiler_params=params(),
    )(left, right)


def matrices_kernel(narrow, src, dst, rest, w_edge, e_src, e_dst, e_edge, e_mid, e_out):
    for index in range(6):
        block, side = index // 2, index % 2
        w_edge[block * TILE : (block + 1) * TILE, side * QUAD : (side + 1) * QUAD] = narrow[
            index
        ].astype(LOW)
    for ref, groups, first in (
        (e_src, src, 0), (e_dst, dst, 0), (e_edge, rest, 0), (e_mid, rest, 3), (e_out, rest, 6),
    ):
        for block in range(ref.shape[0] // TILE):
            ref[block * TILE : (block + 1) * TILE] = groups[first + block].astype(LOW)


def matrices(groups):
    return pl.pallas_call(
        matrices_kernel,
        out_shape=[shaped((DE, D), LOW)]
        + [shaped((D, WIDE), LOW)] * 2
        + [shaped((DE, WIDE), LOW)] * 3,
        compiler_params=params(),
    )(*groups)


def assemble_kernel(count, place, *refs):
    lines, pieces, rows, x_all = refs[0:8], refs[8:-2], refs[-2], refs[-1]
    chip, core, batch = place[0], place[1], place[2]
    owned = pieces[0].shape[0]
    for index, piece in enumerate(lines):
        side, part = index // 4, index % 4
        for line in range(4):
            row = ((line ^ chip) * 2 + (side ^ core)) * OWNED_ROWS
            lane = (part ^ batch) * LANES
            rows[
                pl.ds(pl.multiple_of(row, TILE), OWNED_ROWS),
                pl.ds(pl.multiple_of(lane, LANES), LANES),
            ] = piece[line]
    for index, piece in enumerate(pieces):
        x_all[index * owned : (index + 1) * owned] = piece[...]


def assemble(place, lines, pieces):
    owned = pieces[0].shape[0]
    amount = len(lines) + len(pieces)
    return pl.pallas_call(
        functools.partial(assemble_kernel, len(pieces)),
        in_specs=[pl.BlockSpec(memory_space=pltpu.SMEM)]
        + [pl.BlockSpec(memory_space=pltpu.VMEM)] * amount,
        out_shape=[shaped((3 * D, D), LOW), shaped((8 * owned, D), LOW)],
        compiler_params=params(),
    )(place, *lines, *pieces)


def own_rows_kernel(tiles, rows, quarters, flat, pair):
    load_flat(tiles, flat)
    for index, group in enumerate(group_list(0, 24, 4)):
        block, side = index // 2, index % 2
        value = group_in(flat, pair, group).astype(LOW)
        rows[block * TILE : (block + 1) * TILE, side * QUAD : (side + 1) * QUAD] = value
        for half in range(2):
            quarters[2 * side + half, block * TILE : (block + 1) * TILE, :] = value[
                :, half * LANES : (half + 1) * LANES
            ]


def own_rows(tiles):
    return pl.pallas_call(
        own_rows_kernel,
        out_shape=[
            shaped((OWNED_ROWS, D), LOW),
            shaped((4, OWNED_ROWS, LANES), LOW),
        ],
        scratch_shapes=[
            pltpu.VMEM((flat_rows(24), LANES), jnp.float32),
            pltpu.VMEM((TILE, LANES), jnp.float32),
        ],
        compiler_params=params(),
    )(tiles)


LANES = 128
QUAD = 4 * TILE
FLAT = TILE * TILE // LANES


def group_list(first, last, size):
    return [list(range(t, min(t + size, last))) for t in range(first, last, size)]


def load_flat(ref, flat):
    amount = ref.shape[0]
    for top in range(0, amount, 8):
        rows = min(8, amount - top)
        for part in range(FLAT):
            flat[pl.ds(top * FLAT + 8 * part, rows), :] = ref[
                top : top + rows, part * LANES : (part + 1) * LANES
            ]


def store_flat(ref, flat, first=0, last=None):
    last = ref.shape[0] if last is None else last
    while first < last:
        rows = min(8 - first % 8, last - first)
        top = first // 8 * 8
        for part in range(FLAT):
            ref[first : first + rows, part * LANES : (part + 1) * LANES] = flat[
                pl.ds(top * FLAT + 8 * part + first - top, rows), :
            ]
        first += rows


def tile_rows(tile):
    return pl.ds(tile // 8 * 8 * FLAT + tile % 8, FLAT, stride=8)


def lower_half(shape):
    return lax.broadcasted_iota(jnp.int32, shape, 1) < TILE


def group_in(flat, pair, tiles):
    left = lower_half((FLAT, LANES))
    halves = []
    for first in range(0, 4, 2):
        here = tiles[first : first + 2]
        one = flat[tile_rows(here[0]), :] if here else jnp.zeros((FLAT, LANES), jnp.float32)
        two = flat[tile_rows(here[1]), :] if len(here) > 1 else jnp.zeros_like(one)
        pair[pl.ds(0, FLAT, stride=2), :] = jnp.where(left, one, pltpu.roll(two, TILE, 1))
        pair[pl.ds(1, FLAT, stride=2), :] = jnp.where(left, pltpu.roll(one, TILE, 1), two)
        halves.append(pair[...])
    return jnp.concatenate(halves, axis=1)


def group_out(value, flat, pair, tiles):
    left = lower_half((FLAT, LANES))
    for first in range(0, 4, 2):
        here = tiles[first : first + 2]
        if not here:
            continue
        pair[...] = value[:, first * TILE : first * TILE + LANES]
        even = pair[pl.ds(0, FLAT, stride=2), :]
        odd = pair[pl.ds(1, FLAT, stride=2), :]
        flat[tile_rows(here[0]), :] = jnp.where(left, even, pltpu.roll(odd, TILE, 1))
        if len(here) > 1:
            flat[tile_rows(here[1]), :] = jnp.where(left, pltpu.roll(even, TILE, 1), odd)


def flat_rows(amount):
    return -(-amount // 8) * 8 * FLAT


def regroup_kernel(plan, tiles, *refs):
    outs = refs[:-2]
    flat, pair = refs[-2:]
    load_flat(tiles, flat)
    for out, spec in zip(outs, plan):
        for index, group in enumerate(group_list(*spec)):
            out[index] = group_in(flat, pair, group)


def regroup(tiles, plan, after=()):
    return pl.pallas_call(
        trimmed(functools.partial(regroup_kernel, plan), 1, len(after)),
        in_specs=[pl.BlockSpec(memory_space=pltpu.VMEM)] + anywhere(after),
        out_shape=[
            shaped((len(group_list(*spec)), TILE, QUAD), jnp.float32) for spec in plan
        ],
        scratch_shapes=[
            pltpu.VMEM((flat_rows(tiles.shape[0]), LANES), jnp.float32),
            pltpu.VMEM((TILE, LANES), jnp.float32),
        ],
        compiler_params=params(),
    )(tiles, *after)


def soap_groups(grads, weights, firsts, seconds, lefts, rights, rates):
    count = range(len(grads))
    lane = lax.broadcasted_iota(jnp.int32, (TILE, QUAD), 1) // TILE
    masks = [jnp.where(lane == k, 1.0, 0.0) for k in range(4)]
    low_masks = [mask.astype(LOW) for mask in masks]

    def diagonal(values):
        return jnp.concatenate([values * mask for mask in low_masks], axis=0)

    def thrice(product_of, values, sides):
        parts = [split_low(v) for v in values]
        both = [product_of(jnp.concatenate(parts[i], axis=0), sides[i][0]) for i in count]
        rest = [product_of(parts[i][0], sides[i][1]) for i in count]
        return [both[i][0:TILE] + both[i][TILE:] + rest[i] for i in count]

    right_sides = [[diagonal(part) for part in split_low(v)] for v in rights]
    left_parts = [split_low(v) for v in lefts]
    left_sides = [jnp.concatenate([high, low, high], axis=0) for high, low in left_parts]
    half = [split_low(v) for v in thrice(dot, grads, right_sides)]
    half = [jnp.concatenate([high, high, low], axis=0) for high, low in half]
    full = [dot_rows(left_sides[i], half[i]) for i in count]
    turned = [sum(v[TILE * k : TILE * (k + 1)] * masks[k] for k in range(4)) for v in full]
    new_one = [BETA_ONE * firsts[i] + (1.0 - BETA_ONE) * turned[i] for i in count]
    new_two = [
        BETA_TWO * seconds[i] + (1.0 - BETA_TWO) * turned[i] * turned[i] for i in count
    ]
    fix_one = 1.0 / (1.0 - BETA_ONE**STEP)
    fix_two = 1.0 / (1.0 - BETA_TWO**STEP)
    steps = [
        new_one[i] * fix_one / (jnp.sqrt(new_two[i] * fix_two) + EPS_ADAM) for i in count
    ]
    sides = [[diagonal(part) for part in split_low(v)] for v in steps]
    half = thrice(dot, lefts, sides)
    restored = thrice(dot_turned, half, right_sides)
    new = [
        weights[i] - rates[i] * (restored[i] + DECAY * weights[i]) for i in count
    ]
    return new_one, new_two, new


TOGETHER = 5
EARLY_ROWS = 1664


def block_rate(block):
    middle = (2 * D + DE) ** (-0.5)
    return jnp.where(
        block < 16,
        middle,
        jnp.where(
            block < 24,
            D ** (-0.5),
            jnp.where(block < 32, 2.5 * D ** (-0.5), jnp.where(block < 64, D ** (-0.5), FF ** (-0.5))),
        ),
    )


def small_rates():
    middle = (2 * D + DE) ** (-0.5)
    return [middle] * 19 + [DE ** (-0.5)] * 3 + [1.5 * DE ** (-0.5)] * 3


NORM_ROWS = 24


def soap_early_kernel(scale, span, place, grads, weight, first, second, left, right, *refs):
    norms, outs = refs[0:3], refs[-10:-4]
    flats, pairs = refs[-4:-1], refs[-1]
    step = pl.program_id(0)

    @pl.when(step == 0)
    def _():
        core, batch = place[1], place[2]
        piece = EARLY_ROWS // 8

        def rows_of(begin, end):
            parts = []
            while begin < end:
                index, offset = begin // piece, begin % piece
                amount = min(end - begin, piece - offset)
                parts.append(grads[index // 4 ^ core, index % 4 ^ batch, offset : offset + amount, :])
                begin += amount
            value = parts[0] if len(parts) == 1 else jnp.concatenate(parts, axis=0)
            return value.astype(jnp.float32) * scale

        groups = group_list(24, 99, 3)
        rates = small_rates()
        for start in range(span[0], span[1], TOGETHER):
            here = range(start, min(start + TOGETHER, span[1]))
            state = [[ref[i - span[0]] for i in here] for ref in (weight, first, second, left, right)]
            results = soap_groups(
                [rows_of(i * TILE, (i + 1) * TILE) for i in here], *state, [rates[i] for i in here]
            )
            for spot, index in enumerate(here):
                tiles = [tile - 24 - span[0] * 3 for tile in groups[index]]
                for kind, flat in enumerate(flats):
                    group_out(results[kind][spot], flat, pairs.at[kind * TOGETHER + spot], tiles)
        rows = rows_of(25 * TILE, 25 * TILE + 32)[0:NORM_ROWS, 0:LANES]
        results = adam_step(*(ref[...] for ref in norms), rows)
        for ref, value in zip(outs[3:6], (results[2], results[0], results[1])):
            ref[...] = value

    for ref, flat in zip(outs[0:3], flats):
        for part in range(FLAT):
            first_row = pl.multiple_of(step * (8 * FLAT) + 8 * part, 8)
            ref[:, part * LANES : (part + 1) * LANES] = flat[pl.ds(first_row, 8), :]


def soap_early(scale, span, place, grads, state, norms, held):
    amount = (span[1] - span[0]) * 3
    first = 3 + span[0] * 3 // 8
    out = shaped((99, TILE * TILE), jnp.float32)
    line = shaped((NORM_ROWS, LANES), jnp.float32)
    return pl.pallas_call(
        trimmed(functools.partial(soap_early_kernel, scale, span), 10, len(held)),
        grid=(-(-amount // 8),),
        in_specs=[pl.BlockSpec(memory_space=pltpu.SMEM), whole(grads.shape)]
        + [whole(v.shape) for v in state]
        + [whole(line.shape)] * 3
        + anywhere(held),
        out_specs=[pl.BlockSpec((8, TILE * TILE), lambda i: (first + i, 0))] * 3
        + [kept(line.shape)] * 3,
        out_shape=[out, out, out, line, line, line],
        scratch_shapes=[pltpu.VMEM((flat_rows(amount), LANES), jnp.float32)] * 3
        + [pltpu.VMEM((3 * TOGETHER, TILE, LANES), jnp.float32)],
        input_output_aliases={10 + i: i for i in range(len(held))},
        compiler_params=params(),
    )(place, grads, *state, *norms, *held)


def soap_late_kernel(scale, place, own, other_one, other_two, other_three, pieces, *refs):
    state, v_state = refs[0:5], refs[5:10]
    older = refs[12]
    one, two, new, low, v_one, v_two, v_new, v_low = refs[13:21]
    flats, v_flats, pairs = refs[21:24], refs[24:27], refs[27]
    chip, core, batch = place[0], place[1], place[2]
    groups = group_list(0, 24, 4)
    received = (own, other_one, other_two, other_three)

    def v_block(block, side):
        parts = []
        for part in (2 * side, 2 * side + 1):
            rows = []
            for begin in range(block * TILE, (block + 1) * TILE, TILE // 2):
                half, offset = begin // (DE // 2), begin % (DE // 2)
                rows.append(pieces[half ^ core, part ^ batch, offset : offset + TILE // 2, :])
            parts.append(jnp.concatenate(rows, axis=0))
        return jnp.concatenate(parts, axis=1).astype(jnp.float32)

    def own_part(block, part):
        rows = slice(block * TILE, (block + 1) * TILE)
        shifted = slice(part * OWNED_ROWS + rows.start, part * OWNED_ROWS + rows.stop)
        total = tree_sum([ref[shifted, :].astype(jnp.float32) for ref in received])
        return jnp.where(batch == 0, received[part][rows, :].astype(jnp.float32), total)

    def own_block(block, side):
        return jnp.concatenate([own_part(block, 2 * side), own_part(block, 2 * side + 1)], axis=1)

    first = batch * 24 + (chip * 2 + core) * 3
    own_rates = [block_rate(first + i // 2) for i in range(6)]
    v_rates = [(2 * D + DE) ** (-0.5)] * 6
    for grad_of, values, rates, targets, base in (
        (own_block, state, own_rates, flats, 0),
        (v_block, v_state, v_rates, v_flats, 18),
    ):
        here = range(6)
        grads = [grad_of(i // 2, i % 2) * scale for i in here]
        results = soap_groups(grads, *[[ref[i] for i in here] for ref in values], rates)
        for index in here:
            for kind, flat in enumerate(targets):
                group_out(results[kind][index], flat, pairs.at[base + kind * 6 + index], groups[index])
    for ref, flat in zip((one, two, new, v_one, v_two, v_new), (*flats, *v_flats)):
        store_flat(ref, flat)
    low[...] = new[...].astype(LOW)
    v_low[...] = jnp.concatenate([v_new[...], older[24:]], axis=0).astype(LOW)


def soap_late(scale, place, received, pieces, state, v_state, early):
    out = shaped((24, TILE * TILE), jnp.float32)
    small = shaped(early[0].shape, jnp.float32)
    front = pl.BlockSpec((24, TILE * TILE), lambda i: (0, 0))
    group = whole((6, TILE, QUAD))
    flat = pltpu.VMEM((flat_rows(24), LANES), jnp.float32)
    return pl.pallas_call(
        functools.partial(soap_late_kernel, scale),
        grid=(1,),
        in_specs=[
            pl.BlockSpec(memory_space=pltpu.SMEM),
        ]
        + [whole(v.shape) for v in received]
        + [whole(pieces.shape)]
        + [group] * 10
        + [pl.BlockSpec(memory_space=pl.ANY)] * 2
        + [whole(small.shape)],
        out_specs=[front] * 7 + [whole(small.shape)],
        out_shape=[out, out, out, shaped((24, TILE * TILE), LOW), small, small, small]
        + [shaped(small.shape, LOW)],
        scratch_shapes=[flat] * 6 + [pltpu.VMEM((36, TILE, LANES), jnp.float32)],
        input_output_aliases={16: 4, 17: 5, 18: 6},
        compiler_params=params(),
    )(place, *received, pieces, *state, *v_state, *early)


def swap_core(values):
    return lax.ppermute(values, "core", [(0, 1), (1, 0)])


def swap_chip(values, shift):
    chips = lax.axis_size("chip")
    return lax.ppermute(values, "chip", [(i, i ^ shift) for i in range(chips)])


def gate(values, others):
    return lax.optimization_barrier((values, others))[0]


def gather_pieces(values, fill=()):
    chips = lax.axis_size("chip")
    parts = [values] + [swap_chip(values, shift) for shift in range(1, chips)]
    parts = gate(parts, fill)
    return [half for part in parts for half in (part, swap_core(part))]


def reduce_pieces(even, odd):
    near = add_halves(even, swap_core(odd))
    return [near[0]] + [swap_chip(near[shift], shift) for shift in range(1, len(near))]


def swap_batch(values, shift):
    return lax.ppermute(values, "batch", [(i, i ^ shift) for i in range(4)])


def pick(values, index):
    return lax.dynamic_index_in_dim(values, index, 0, keepdims=False)


def tree_sum(parts):
    while len(parts) > 1:
        parts = [parts[i] + parts[i + 1] for i in range(0, len(parts), 2)]
    return parts[0]


def wide_values(values):
    return values.astype(jnp.float32)


def gather_first(place, quarters, x, batch, fill):
    pieces = [x] + [swap_chip(x, shift) for shift in range(1, 4)]
    sent = [
        lax.ppermute(quarters[index], "batch", [(0, index)]) for index in range(1, 4)
    ]
    quarter = jnp.where(batch == 0, quarters[0], sent[0] + sent[1] + sent[2])
    quarter = gate(quarter, fill[0])
    lines = jnp.stack([quarter] + [swap_chip(quarter, shift) for shift in range(1, 4)])
    lines = gate(lines, fill[1])
    parts = [lines] + [swap_batch(lines, shift) for shift in range(1, 4)]
    parts, pieces = gate((parts, pieces), fill[2])
    pieces = [half for piece in pieces for half in (piece, swap_core(piece))]
    return assemble(place, parts + [swap_core(part) for part in parts], pieces)


def reduce_small(even, odd):
    near = add_halves(even, swap_core(odd))
    total = near[0]
    for shift in range(1, 4):
        total = total + wide_values(swap_batch(near[shift], shift))
    return total.astype(LOW)


def share_small(total):
    others = [total] + [swap_chip(total, shift) for shift in range(1, 4)]
    total = tree_sum([wide_values(v) for v in others]).astype(LOW)
    parts = jnp.stack([total] + [swap_batch(total, shift) for shift in range(1, 4)])
    return jnp.stack([parts, swap_core(parts)])


def reduce_late(even, odd, early, batch, fill):
    near = add_halves(even, swap_core(odd))
    received = [swap_batch(near[shift], shift) for shift in range(1, 4)]
    received = gate(received, fill(near[0]))
    total = near[0] + sum(wide_values(part) for part in received)
    shared = total[4 * OWNED_ROWS :]
    lines = [total[OWNED_ROWS * i : OWNED_ROWS * (i + 1)] for i in range(4)]
    sent = [
        jnp.concatenate([lines[shift], shared], axis=0).astype(LOW) for shift in range(1, 4)
    ]
    received = [swap_chip(part, shift) for shift, part in enumerate(sent, 1)]
    quarter = lines[0]
    shares = [wide_values(shared.astype(LOW))]
    for part in gate(received, fill(sent)):
        got = wide_values(part)
        quarter = quarter + got[0:OWNED_ROWS]
        shares.append(got[OWNED_ROWS:])
    shared = tree_sum(shares).astype(LOW)
    quarter = jnp.pad(quarter.astype(LOW)[None], ((0, 3), (0, 0), (0, 0)))

    def outgoing(target):
        block = jnp.where(target == 0, quarter, pick(early, jnp.maximum(target - 1, 0)))
        return jnp.concatenate([block.reshape(4 * OWNED_ROWS, LANES), shared], axis=0)

    sent = [outgoing(batch ^ shift) for shift in range(4)]
    received = [swap_batch(part, shift) for shift, part in enumerate(sent) if shift]
    received = gate([sent[0]] + received, fill(sent))
    edges = jnp.stack([part[4 * OWNED_ROWS :] for part in received])
    edges = jnp.stack([edges, swap_core(edges)])
    return received, edges


def flat_list(groups):
    return [value for group in groups for value in group]


def pad_to(matrix, height, breadth):
    return jnp.pad(matrix, ((0, height - matrix.shape[0]), (0, breadth - matrix.shape[1])))


def norm_rows(vector):
    return pad_to(vector.reshape(19, LANES), NORM_ROWS, LANES)


def norm_vector(rows):
    return rows[0:19].reshape(-1)


def gather_plain(tiles, every):
    amount = tiles.shape[0]
    unit = math.gcd(amount, D // TILE)
    local = tiles.astype(LOW).reshape(amount // unit, unit, TILE, TILE)
    local = local.transpose(0, 2, 1, 3).reshape(amount // unit, TILE, unit * TILE)
    units = lax.all_gather(local, every, axis=0, tiled=True)
    blocks = units.reshape(-1, D // TILE // unit, TILE, unit * TILE).transpose(0, 2, 1, 3)
    blocks = blocks.reshape(-1, TILE, D)
    return blocks[0:24].reshape(3 * D, D), blocks


def soap_plain(weight, moment_one, moment_two, left, right, gradient, rates):
    left, right = as_square(left), as_square(right)
    high = lax.Precision.HIGHEST
    turned = jnp.einsum("tji,tjk->tik", left, gradient, precision=high)
    turned = jnp.einsum("tik,tkl->til", turned, right, precision=high)
    new_one = BETA_ONE * as_square(moment_one) + (1.0 - BETA_ONE) * turned
    new_two = BETA_TWO * as_square(moment_two) + (1.0 - BETA_TWO) * turned * turned
    direction = (
        new_one / (1.0 - BETA_ONE**STEP) / (jnp.sqrt(new_two / (1.0 - BETA_TWO**STEP)) + EPS_ADAM)
    )
    restored = jnp.einsum("tij,tjk->tik", left, direction, precision=high)
    restored = jnp.einsum("tik,tlk->til", restored, right, precision=high)
    weight = as_square(weight)
    new = weight - rates[:, None, None] * (restored + DECAY * weight)
    return as_flat(new_one), as_flat(new_two), as_flat(new)


def update_plain(g_late, g_early, g_small, every, scale, big, small, norms):
    amount = big[0].shape[0]
    unit = math.gcd(amount, D // TILE)
    g_late, g_small = jnp.stack(g_late), jnp.stack(g_small).reshape(EARLY_ROWS, WIDE)
    late = g_late[:, :, 0 : 4 * OWNED_ROWS].reshape(2, 4, 4, OWNED_ROWS, LANES)
    late = late.transpose(2, 0, 3, 1, 4).reshape(24, TILE, D)
    w_edge = g_late[:, :, 4 * OWNED_ROWS :].transpose(0, 2, 1, 3).reshape(DE, D)
    early = g_early.reshape(8, 3, 4, 3, TILE, LANES).transpose(1, 0, 3, 4, 2, 5)
    early = early.reshape(72, TILE, D)
    grads = jnp.concatenate([late, early], axis=0)
    grads = grads.reshape(-1, TILE, D // TILE // unit, unit * TILE).transpose(0, 2, 1, 3)
    own = lax.psum_scatter(
        grads.reshape(-1, TILE, unit * TILE), every, scatter_dimension=0, tiled=True
    )
    own = wide_values(own).reshape(amount // unit, TILE, unit, TILE).transpose(0, 2, 1, 3)
    own = own.reshape(amount, TILE, TILE) * scale
    w_edge, g_small = lax.psum((wide_values(w_edge), wide_values(g_small)), every)
    strips = g_small[0:1600, 0:DE].reshape(25, TILE, 3, TILE).transpose(0, 2, 1, 3)
    tiles = jnp.concatenate(
        [as_square(to_flat_tiles(w_edge)), strips.reshape(75, TILE, TILE)], axis=0
    )
    first = lax.axis_index(every) * amount
    rates = lax.dynamic_slice_in_dim(
        jnp.asarray(rate_table(big_shapes(), big_spreads())), first, amount
    )
    big_new = soap_plain(*big, own, rates)
    rates = jnp.asarray(rate_table(small_shapes(), small_spreads()))
    small_new = soap_plain(*small, tiles * scale, rates)
    norm_new = adam_step(*norms, norm_vector(g_small[1600:, 0:LANES]) * scale)
    return big_new, small_new, norm_new


def body(
    node,
    edge,
    dest_device,
    dest_local,
    node_valid,
    node_cot,
    edge_cot,
    big_weight,
    big_first,
    big_second,
    big_left,
    big_right,
    small_weight,
    small_first,
    small_second,
    small_left,
    small_right,
    norm_params,
    norm_first,
    norm_second,
):
    chips = lax.axis_size("chip")
    every = ("batch", "chip", "core")
    shards = 2 * chips
    owned = node.shape[1]
    nodes = owned * shards
    rows = owned * K
    complexes = node.shape[0] * lax.axis_size("batch")
    tuned = chips == 4 and lax.axis_size("batch") == 4 and big_weight.shape[0] == 24
    chip, core, batch = (lax.axis_index(axis) for axis in ("chip", "core", "batch"))
    grad_scale = 1.0 / math.sqrt(complexes * nodes * K)
    x = node[0]
    big_state = (big_weight, big_first, big_second, big_left, big_right)
    small_state = (small_weight, small_first, small_second, small_left, small_right)
    norm_state = (norm_params, norm_first, norm_second)

    place = jnp.stack([chip, core, batch]).astype(jnp.int32) * int(tuned)
    plan = ((0, 24, 4), (24, 48, 3), (48, 72, 3), (72, 99, 3))
    small_groups = [regroup(small_weight, plan)]
    w_edge, e_src, e_dst, e_edge, e_mid, e_out = matrices(small_groups[0])
    norms = norm_params[0 : 4 * D].reshape(4, D)
    edge_norms = pad_to(norm_params[4 * D :].reshape(2, DE), 8, WIDE)
    valid = node_valid[0].astype(jnp.float32).reshape(owned, 1)
    me = chip * 2 + core
    relative = (dest_device[0].reshape(1, rows) ^ me) * owned + dest_local
    tall, wide, ok_row = prepare(relative, valid, edge[0].T, nodes)
    if tuned:
        own, quarters = own_rows(big_weight)
        blocks = lax.all_gather(own, every, axis=0, tiled=True).reshape(-1, TILE, D)
        w_rows, x_all = gather_first(
            place, quarters, x, batch, (small_groups[0], (w_edge, e_src), (tall, wide))
        )
    else:
        w_rows, blocks = gather_plain(big_weight, every)
        x_all = jnp.concatenate(gather_pieces(x), axis=0)

    def fillers(states, plans, token):
        return [regroup(v, plans, (token,)) for v in states] if tuned else []

    even, odd, hidden, slope_one, slope_two = message_forward(
        tall, wide, ok_row, x_all, owned, w_rows, w_edge, ()
    )
    sums = reduce_pieces(even, odd)
    small_groups += fillers(small_state[1:3], plan, even)
    node_low, q_src, q_dst, inside, one, act, slope, summed, scale, sums = node_forward(
        x, valid, blocks, e_src, e_dst, norms, sums, flat_list(small_groups[1:3])
    )
    big_groups = fillers(big_state[0:3], plan[0:1], q_dst)
    q_pieces = gather_pieces(q_dst, flat_list(big_groups))
    (
        edge_new, part_edge, even, odd, d_q_src, g_e_edge, g_e_mid, g_e_out, g_e_norms,
    ) = edge_phase(
        tall, wide, edge_cot[0].T, q_pieces, q_src, e_edge, e_mid, e_out, edge_norms, (),
    )
    d_q_dst = reduce_pieces(even, odd)
    big_groups += fillers(big_state[3:5], plan[0:1], even)
    reply, d_inside, g_early, *g_small = node_backward(
        place,
        [
            node_cot[0], d_q_src, node_low, summed, one, inside, act, slope, scale, sums,
            blocks, e_src, e_dst, norms, g_e_edge, g_e_mid, g_e_out, g_e_norms,
        ],
        d_q_dst,
        flat_list(big_groups[3:5]),
    )
    small_groups += fillers(small_state[3:5], plan, reply)
    replies = gather_pieces(reply, flat_list(small_groups[3:5]))
    d_edges, even, odd, d_p_src, *g_late = message_backward(
        place, tall, wide, hidden, slope_one, slope_two, part_edge, x_all, w_rows, w_edge, replies, (),
    )
    d_p_dst = reduce_pieces(even, odd)
    d_features = node_gradient(d_inside, d_p_src, w_rows, d_p_dst)

    if tuned:
        norm_groups = [norm_rows(v) for v in norm_state]
        big_groups = [v[0] for v in big_groups]
        late_groups = [v[0] for v in small_groups]
        early = lax.psum_scatter(
            gate(g_early, replies), ("chip", "core"), scatter_dimension=0, tiled=True
        )
        early = early.reshape(3, 4, OWNED_ROWS, LANES)
        small_sum = share_small(reduce_small(*g_small))
        spans = [(0, 8), (8, 16), (16, 25)]
        early_new, norm_new = [], []

        def fill(token):
            index = len(norm_new)
            outs = soap_early(
                grad_scale, spans[index], place, gate(small_sum, token),
                [v[index + 1] for v in small_groups], norm_groups, early_new[-3:],
            )
            early_new.extend(outs[0:3])
            norm_new.append(outs[3:6])
            return outs[0]

        mine, edges = reduce_late(*g_late, early, batch, fill)
        early_new = early_new[-3:]
        norm_new, norm_one, norm_two = norm_new[-1]
        big_one, big_two, big_new, big_low, small_one, small_two, small_new, small_low = soap_late(
            grad_scale, place, mine, edges, big_groups, late_groups, early_new
        )
        norm_one, norm_two, norm_new = (norm_vector(v) for v in (norm_one, norm_two, norm_new))
    else:
        (
            (big_one, big_two, big_new),
            (small_one, small_two, small_new),
            (norm_one, norm_two, norm_new),
        ) = update_plain(
            g_late, g_early, g_small, every, grad_scale, big_state, small_state, norm_state
        )
        big_low = big_new.astype(LOW)
        small_low = small_new.astype(LOW)
    return (
        node_low[None],
        edge_new.T[None],
        d_features[None],
        d_edges.T[None],
        big_one,
        big_two,
        big_new,
        big_low,
        small_one,
        small_two,
        small_new,
        small_low,
        norm_one,
        norm_two,
        norm_new,
    )


def solution(mesh):
    batch, shards = mesh.devices.shape
    fine = Mesh(mesh.devices.reshape(batch, shards // 2, 2), ("batch", "chip", "core"))
    edge = ("chip", "core")
    every = ("batch", "chip", "core")
    placed = (
        P("batch", edge, None),
        P("batch", edge, None),
        P("batch", edge, None),
        P("batch", edge),
        P("batch", edge),
        P("batch", edge, None),
        P("batch", edge, None),
        P(every, None),
        P(every, None),
        P(every, None),
        P(every, None),
        P(every, None),
        P(),
        P(),
        P(),
        P(),
        P(),
        P(),
        P(),
        P(),
    )
    return jax.shard_map(
        body,
        mesh=fine,
        in_specs=placed,
        out_specs=(
            P("batch", edge, None),
            P("batch", edge, None),
            P("batch", edge, None),
            P("batch", edge, None),
            P(every, None),
            P(every, None),
            P(every, None),
            P(every, None),
            P(),
            P(),
            P(),
            P(),
            P(),
            P(),
            P(),
        ),
        check_vma=False,
    )
```

```python
import functools
import math

import jax
import jax.numpy as jnp
import numpy as np
from jax import lax
from jax.experimental import pallas as pl
from jax.experimental.pallas import tpu as pltpu
from jax.sharding import Mesh
from jax.sharding import PartitionSpec as P

D = 512
DE = 192
FF = 2048
K = 60
TILE = 64
STEP = 10


BETA_ONE = 0.5
BETA_TWO = 0.5
EPS_ADAM = 1e-08
EPS_NORM = 1e-05
DECAY = 0.01
NORM_RATE = 0.4
PRECISION_HIGH = lax.Precision.HIGHEST


def big_shapes():
    return [(D, D), (D, D), (D, D), (D, D), (D, FF), (FF, D)]


def small_shapes():
    return [(DE, D), (D, DE), (D, DE), (DE, DE), (DE, DE), (DE, DE)]


def big_spreads():
    middle = (2 * D + DE) ** (-0.5)
    return [middle, middle, D ** (-0.5), 2.5 * D ** (-0.5), D ** (-0.5), FF ** (-0.5)]


def small_spreads():
    middle = (2 * D + DE) ** (-0.5)
    return [middle, middle, middle, middle, DE ** (-0.5), 1.5 * DE ** (-0.5)]


def rate_table(shapes, spreads):
    amounts = [height // TILE * (breadth // TILE) for height, breadth in shapes]
    return np.repeat(np.array(spreads, np.float32), amounts)


def as_square(flat_tiles):
    return flat_tiles.reshape(flat_tiles.shape[0], TILE, TILE)


def as_flat(square_tiles):
    return square_tiles.reshape(square_tiles.shape[0], TILE * TILE)


def from_tiles(tile_stack, shapes):
    matrices = []
    offset = 0
    for height, breadth in shapes:
        amount = height // TILE * (breadth // TILE)
        blocked = tile_stack[offset : offset + amount].reshape(
            height // TILE, breadth // TILE, TILE, TILE
        )
        matrices.append(blocked.transpose(0, 2, 1, 3).reshape(height, breadth))
        offset += amount
    return matrices


def to_flat_tiles(matrix):
    height, breadth = matrix.shape
    blocked = matrix.reshape(height // TILE, TILE, breadth // TILE, TILE)
    return blocked.transpose(0, 2, 1, 3).reshape(-1, TILE * TILE)


def adam_step(params, moment_one, moment_two, gradient):
    new_one = BETA_ONE * moment_one + (1.0 - BETA_ONE) * gradient
    new_two = BETA_TWO * moment_two + (1.0 - BETA_TWO) * gradient * gradient
    direction = (
        new_one / (1.0 - BETA_ONE**STEP) / (jnp.sqrt(new_two / (1.0 - BETA_TWO**STEP)) + EPS_ADAM)
    )
    return (new_one, new_two, params - NORM_RATE * direction)


def times_transposed(left_side, right_side):
    return lax.dot_general(
        left_side, right_side, (((1,), (1,)), ((), ())), preferred_element_type=jnp.float32
    )


LOW = jnp.bfloat16
WIDE = 256
GELU_A = math.sqrt(2.0 / math.pi)
GELU_B = GELU_A * 0.044715
OWNED_ROWS = 3 * TILE


def dot(left, right):
    return jnp.dot(left, right, preferred_element_type=jnp.float32)


def dot_rows(left, right):
    return lax.dot_general(
        left, right, (((0,), (0,)), ((), ())), preferred_element_type=jnp.float32
    )


def dot_turned(left, right):
    return lax.dot_general(
        left, right, (((1,), (1,)), ((), ())), preferred_element_type=jnp.float32
    )


def split_low(values):
    high = values.astype(LOW)
    return high, (values - high.astype(jnp.float32)).astype(LOW)


def gelu_pair(v):
    square = v * v
    half = 0.5 * jnp.tanh(v * (GELU_A + GELU_B * square)) + 0.5
    out = v * half
    slope = half + out * (1.0 - half) * (2.0 * GELU_A + 6.0 * GELU_B * square)
    return out, slope


def norm_parts(values, width):
    centre = jnp.sum(values, axis=-1, keepdims=True) * (1.0 / width)
    centered = values - centre
    if values.shape[-1] != width:
        lane = lax.broadcasted_iota(jnp.int32, values.shape, 1)
        centered = jnp.where(lane < width, centered, 0.0)
    spread = jnp.sum(centered * centered, axis=-1, keepdims=True) * (1.0 / width)
    inverse = lax.rsqrt(spread + EPS_NORM)
    return centered * inverse, inverse


def norm_back(scaled, inverse, gain, upstream, width):
    inner = upstream * gain
    mean_inner = jnp.sum(inner, axis=-1, keepdims=True) * (1.0 / width)
    mean_cross = jnp.sum(inner * scaled, axis=-1, keepdims=True) * (1.0 / width)
    return inverse * (inner - mean_inner - scaled * mean_cross)


def whole(shape):
    return pl.BlockSpec(shape, lambda *_: (0,) * len(shape), pipeline_mode=pl.Buffered(1))


def anywhere(values):
    return [pl.BlockSpec(memory_space=pl.ANY)] * len(values)


def kept(shape):
    return pl.BlockSpec(shape, lambda *_: (0,) * len(shape))


def params(limit=58):
    return pltpu.CompilerParams(vmem_limit_bytes=limit * 2**20)


def shaped(shape, dtype):
    return jax.ShapeDtypeStruct(shape, dtype)


def trimmed(kernel, inputs, unread):
    def run(*refs):
        kernel(*refs[:inputs], *refs[inputs + unread :])

    return run


def prepare_kernel(targets, valid, edge, tall, wide, ok_row):
    nodes, block = tall.shape
    group = block // K
    down = lax.broadcasted_iota(jnp.int32, (nodes, block), 0)
    hot = jnp.where(down == targets[...], 1.0, 0.0)
    tall[...] = hot.astype(LOW)
    row = lax.broadcasted_iota(jnp.int32, (WIDE - DE, block), 0)
    source = lax.broadcasted_iota(jnp.int32, (WIDE - DE, block), 1) // K
    picked = jnp.where((row == source) | (row == source + group), 1.0, 0.0)
    wide[0:DE] = edge[...]
    wide[DE:WIDE] = picked.astype(LOW)
    ok = jnp.sum(picked[0:group] * valid[...], axis=0, keepdims=True)
    ok_row[...] = ok


def block_of():
    return 32 * K


def lanes(height, block):
    return pl.BlockSpec((height, block), lambda i: (0, i))


def tall_lanes(nodes, block):
    buffers = pl.Buffered(2 if nodes <= 1024 else 1)
    return pl.BlockSpec((nodes, block), lambda i: (0, i), pipeline_mode=buffers)


def prepare(targets, valid, edge_across, nodes):
    rows = edge_across.shape[1]
    block = block_of()
    return pl.pallas_call(
        prepare_kernel,
        grid=(rows // block,),
        in_specs=[
            lanes(1, block),
            pl.BlockSpec((block // K, 1), lambda i: (i, 0)),
            lanes(DE, block),
        ],
        out_specs=[
            lanes(nodes, block),
            lanes(WIDE, block),
            lanes(1, block),
        ],
        out_shape=[
            shaped((nodes, rows), LOW),
            shaped((WIDE, rows), LOW),
            shaped((1, rows), jnp.float32),
        ],
        compiler_params=params(),
    )(targets, valid, edge_across)


def source_rows(values):
    high = values.astype(LOW).astype(jnp.float32)
    return jnp.concatenate([high, values - high], axis=0).astype(LOW)


def put_halves(halves, total, owned):
    for index in range(total.shape[0] // owned):
        rows = total[index * owned : (index + 1) * owned].astype(LOW)
        halves[index % 2][index // 2, 0:owned, :] = rows


COUNT_ROWS = 16


def message_kernel(
    tall, wide, ok_row, w_rows, w_edge, x_all,
    even, odd, hidden_out, slope_one, slope_two,
    table, mixed, from_source, total, mid, counts,
):
    step = pl.program_id(0)
    owned = from_source.shape[0]

    @pl.when(step == 0)
    def _():
        table[...] = dot(x_all[...], w_rows[D : 2 * D]).astype(LOW).T
        from_source[...] = dot(x_all[0:owned], w_rows[0:D])
        mixed[0:DE] = w_edge[...]
        mid[...] = w_rows[2 * D : 3 * D].T
        total[...] = jnp.zeros_like(total)
        counts[...] = jnp.zeros_like(counts)

    group = hidden_out.shape[1] // K
    mixed[DE:WIDE] = source_rows(from_source[pl.ds(step * group, group), :])
    pre = dot(table[...], tall[...]) + dot_rows(mixed[...], wide[...])
    hidden, slope = gelu_pair(pre)
    hidden = hidden.astype(LOW)
    hidden_out[...] = hidden
    slope_one[...] = slope.astype(LOW)
    second, slope = gelu_pair(dot(mid[...], hidden))
    ok = ok_row[...]
    slope_two[...] = (slope * ok).astype(LOW)
    total[...] += dot_turned(tall[...], (second * ok).astype(LOW))
    ok_rows = jnp.broadcast_to(ok, (COUNT_ROWS, ok.shape[1])).astype(LOW)
    counts[...] += dot_turned(ok_rows, tall[...])

    @pl.when(step == pl.num_programs(0) - 1)
    def _():
        put_halves((even, odd), total, owned)
        for index in range(total.shape[0] // owned):
            amount = counts[:, index * owned : (index + 1) * owned]
            high = jnp.floor(amount * (1.0 / LANES))
            place = (even, odd)[index % 2].at[index // 2]
            rows = pl.ds(owned, COUNT_ROWS)
            place[rows, :] = jnp.zeros((COUNT_ROWS, D), LOW)
            place[rows, 0:owned] = high.astype(LOW)
            place[rows, LANES : LANES + owned] = (amount - high * LANES).astype(LOW)


def message_forward(tall, wide, ok_row, x_all, owned, w_rows, w_edge, after):
    nodes, rows = tall.shape
    block = block_of()
    half = (nodes // owned // 2, owned + COUNT_ROWS, D)
    return pl.pallas_call(
        trimmed(message_kernel, 6, len(after)),
        grid=(rows // block,),
        in_specs=[
            tall_lanes(nodes, block),
            lanes(WIDE, block),
            lanes(1, block),
            whole((3 * D, D)),
            whole((DE, D)),
            whole((nodes, D)),
        ]
        + anywhere(after),
        out_specs=[kept(half), kept(half)] + [lanes(D, block)] * 3,
        out_shape=[shaped(half, LOW)] * 2 + [shaped((D, rows), LOW)] * 3,
        scratch_shapes=[
            pltpu.VMEM((D, nodes), LOW),
            pltpu.VMEM((WIDE, D), LOW),
            pltpu.VMEM((owned, D), jnp.float32),
            pltpu.VMEM((nodes, D), jnp.float32),
            pltpu.VMEM((D, D), LOW),
            pltpu.VMEM((COUNT_ROWS, nodes), jnp.float32),
        ],
        compiler_params=params(),
    )(tall, wide, ok_row, w_rows, w_edge, x_all, *after)


def up_part(blocks, part):
    per, parts = D // TILE, FF // D
    strips = [blocks[4 * per + row * parts + part] for row in range(per)]
    return jnp.concatenate(strips, axis=0)


def out_part(blocks):
    per = D // TILE
    return blocks[3 * per : 4 * per].reshape(D, D)


def down_part(blocks, part):
    per = D // TILE
    first = per * (4 + FF // D + part)
    return blocks[first : first + per].reshape(D, D)


def node_forward_kernel(x, valid, blocks, u_src, u_dst, norms, *refs):
    pieces = refs[:-10]
    (
        low_out, q_src, q_dst, inside_out, one_out, act_out, slope_out, summed_out, scale_out,
        sums_out,
    ) = refs[-10:]
    summed_all = sum(piece[...].astype(jnp.float32) for piece in pieces)
    owned = x.shape[0]
    sums = summed_all[0:owned]
    tally = summed_all[owned : owned + 8, 0:LANES] * float(LANES)
    tally += summed_all[owned : owned + 8, LANES : 2 * LANES]
    amount = tally.T[0:owned, 0:1]
    scale = valid[...] / jnp.maximum(amount * valid[...], 1.0)
    scale_out[...] = scale
    sums_out[...] = sums
    high, low = split_low(sums * scale)
    w_out = out_part(blocks)
    inside = x[...].astype(jnp.float32) + (dot(high, w_out) + dot(low, w_out))
    scaled, _ = norm_parts(inside, D)
    one = scaled * norms[0:1] + norms[1:2]
    one_low = one.astype(LOW)
    narrowed = jnp.zeros_like(one)
    for part in range(FF // D):
        act, slope = gelu_pair(dot(one_low, up_part(blocks, part)))
        act = act.astype(LOW)
        act_out[:, part * D : (part + 1) * D] = act
        slope_out[:, part * D : (part + 1) * D] = slope.astype(LOW)
        narrowed += dot(act, down_part(blocks, part))
    summed = one + narrowed
    scaled, _ = norm_parts(summed, D)
    two = (scaled * norms[2:3] + norms[3:4]).astype(LOW)
    low_out[...] = two
    q_src[...] = dot(two, u_src[...])
    q_dst[...] = dot(two, u_dst[...]).astype(LOW)
    inside_out[...] = inside
    one_out[...] = one
    summed_out[...] = summed


def node_forward(x, valid, blocks, u_src, u_dst, norms, pieces, after):
    owned = x.shape[0]
    wide = shaped((owned, D), jnp.float32)
    operands = [x, valid, blocks, u_src, u_dst, norms, *pieces]
    return pl.pallas_call(
        trimmed(node_forward_kernel, len(operands), len(after)),
        in_specs=[pl.BlockSpec(memory_space=pltpu.VMEM)] * len(operands) + anywhere(after),
        out_shape=[
            shaped((owned, D), LOW),
            shaped((owned, WIDE), jnp.float32),
            shaped((owned, WIDE), LOW),
            wide,
            wide,
            shaped((owned, FF), LOW),
            shaped((owned, FF), LOW),
            wide,
            shaped((owned, 1), jnp.float32),
            wide,
        ],
        compiler_params=params(),
    )(*operands, *after)


def tall_norm(values):
    width = values.shape[0]
    centre = jnp.sum(values, axis=0, keepdims=True) * (1.0 / width)
    centered = values - centre
    spread = jnp.sum(centered * centered, axis=0, keepdims=True) * (1.0 / width)
    inverse = lax.rsqrt(spread + EPS_NORM)
    return centered * inverse, inverse


def tall_norm_back(scaled, inverse, gain, upstream):
    width = scaled.shape[0]
    inner = upstream * gain
    mean_inner = jnp.sum(inner, axis=0, keepdims=True) * (1.0 / width)
    mean_cross = jnp.sum(inner * scaled, axis=0, keepdims=True) * (1.0 / width)
    return inverse * (inner - mean_inner - scaled * mean_cross)


def lane_sums(values):
    return sum(
        values[:, first : first + LANES] for first in range(0, values.shape[1], LANES)
    )


def edge_kernel(count, tall, wide, cot, q_src, u_edge, u_mid, u_out, norms, *refs):
    pieces = refs[0:count]
    (
        edge_out, d_edge, even, odd, d_source, g_edge, g_mid, g_out, g_norms,
        table, mixed, total, mid_turned, out_turned, gain_sum, shift_sum, columns,
    ) = refs[-17:]
    step = pl.program_id(0)
    last = pl.num_programs(0) - 1
    owned = q_src.shape[0]

    @pl.when(step == 0)
    def _():
        table[...] = jnp.concatenate([piece[...] for piece in pieces], axis=0).T
        mixed[0:DE] = u_edge[...]
        mid_turned[...] = u_mid[...].T
        out_turned[...] = u_out[...].T
        columns[...] = norms[...].T
        for ref in (total, gain_sum, shift_sum, g_edge, g_mid, g_out):
            ref[...] = jnp.zeros_like(ref)

    group = edge_out.shape[1] // K
    mixed[DE:WIDE] = source_rows(q_src[pl.ds(step * group, group), :])
    both = wide[...]
    first, slope_one = gelu_pair(
        dot(table[0:DE], tall[...]) + dot(mixed[...].T[0:DE], both)
    )
    first = first.astype(LOW)
    second, slope_two = gelu_pair(dot(mid_turned[0:DE, 0:DE], first))
    second = second.astype(LOW)
    change = dot(out_turned[0:DE, 0:DE], second)
    scaled, inverse = tall_norm(both[0:DE].astype(jnp.float32) + change)
    gain, offset = columns[0:DE, 0:1], columns[0:DE, 1:2]
    edge_out[...] = (scaled * gain + offset).astype(LOW)
    back = cot[...].astype(jnp.float32)
    gain_sum[...] += lane_sums(back * scaled)
    shift_sum[...] += lane_sums(back)
    d_sum = tall_norm_back(scaled, inverse, gain, back)
    d_change = d_sum.astype(LOW)
    g_out[0:DE, 0:DE] += dot_turned(second, d_change)
    d_second = (dot(u_out[:, 0:DE], d_change) * slope_two).astype(LOW)
    g_mid[0:DE, 0:DE] += dot_turned(first, d_second)
    d_first = (dot(u_mid[:, 0:DE], d_second) * slope_one).astype(LOW)
    d_edge[...] = d_sum + dot(u_edge[:, 0:DE], d_first)
    turned = dot_turned(both, d_first)
    g_edge[:, 0:DE] += turned[0:DE]
    d_source[pl.ds(step * group, group), :] = turned[DE : DE + group]
    total[:, 0:DE] += dot_turned(tall[...], d_first)

    @pl.when(step == last)
    def _():
        put_halves((even, odd), total, owned)
        gain_row = jnp.sum(gain_sum[...].T, axis=0, keepdims=True)
        shift_row = jnp.sum(shift_sum[...].T, axis=0, keepdims=True)
        both_rows = jnp.concatenate([gain_row, shift_row], axis=1)
        g_norms[...] = jnp.zeros_like(g_norms)
        for index in range(3):
            g_norms[index : index + 1] = both_rows[:, index * LANES : (index + 1) * LANES]


def edge_phase(tall, wide, cot, pieces, q_src, u_edge, u_mid, u_out, norms, after):
    nodes, rows = tall.shape
    owned = q_src.shape[0]
    block = block_of()
    count = len(pieces)
    half = (count // 2, owned, WIDE)
    square = shaped((DE, WIDE), jnp.float32)
    line = shaped((8, LANES), jnp.float32)
    return pl.pallas_call(
        functools.partial(edge_kernel, count),
        grid=(rows // block,),
        in_specs=[
            tall_lanes(nodes, block),
            lanes(WIDE, block),
            lanes(DE, block),
            whole((owned, WIDE)),
            whole((DE, WIDE)),
            whole((DE, WIDE)),
            whole((DE, WIDE)),
            whole((8, WIDE)),
        ]
        + [whole((owned, WIDE))] * count
        + anywhere(after),
        out_specs=[
            lanes(DE, block),
            lanes(DE, block),
            kept(half),
            kept(half),
            kept((owned, DE)),
            kept((DE, WIDE)),
            kept((DE, WIDE)),
            kept((DE, WIDE)),
            kept((8, LANES)),
        ],
        out_shape=[
            shaped((DE, rows), LOW),
            shaped((DE, rows), jnp.float32),
            shaped(half, LOW),
            shaped(half, LOW),
            shaped((owned, DE), jnp.float32),
            square,
            square,
            square,
            line,
        ],
        scratch_shapes=[
            pltpu.VMEM((WIDE, nodes), LOW),
            pltpu.VMEM((WIDE, WIDE), LOW),
            pltpu.VMEM((nodes, WIDE), jnp.float32),
            pltpu.VMEM((WIDE, DE), LOW),
            pltpu.VMEM((WIDE, DE), LOW),
            pltpu.VMEM((DE, LANES), jnp.float32),
            pltpu.VMEM((DE, LANES), jnp.float32),
            pltpu.VMEM((WIDE, 8), jnp.float32),
        ],
        compiler_params=params(),
    )(tall, wide, cot, q_src, u_edge, u_mid, u_out, norms, *pieces, *after)


def put_blocks(ref, base, matrix, step=1):
    for row in range(matrix.shape[0] // TILE):
        strip = matrix[row * TILE : (row + 1) * TILE].astype(ref.dtype)
        owner, batch, slot = early_place(base + row * step)
        for part in range(4):
            ref[owner, batch, part, slot * TILE : (slot + 1) * TILE, :] = strip[
                :, part * LANES : (part + 1) * LANES
            ]


def put_sides(refs, core, stores):
    for own in range(2):

        @pl.when(core == own)
        def _():
            for side, value, index in stores:
                refs[side ^ own][index] = value


def small_stores(batch, begin, matrix):
    stores = []
    piece = EARLY_ROWS // 8
    end = begin + matrix.shape[0]
    first = begin
    while first < end:
        index, offset = first // piece, first % piece
        amount = min(end - first, piece - offset)
        value = matrix[first - begin : first - begin + amount].astype(LOW)
        place = (index % 4 ^ batch, slice(offset, offset + amount), slice(None))
        stores.append((index // 4, value, place))
        first += amount
    return stores


def put_norm(ref, index, values):
    total = jnp.sum(values, axis=0, keepdims=True)
    for part in range(4):
        row = index * 4 + part
        ref[row : row + 1, 0:LANES] = total[:, part * LANES : (part + 1) * LANES]


def early_place(block):
    batch, rest = block // 24, block % 24
    return rest // 3, batch, rest % 3


def node_backward_kernel(
    place, cot, d_q_src, low, summed, one, inside, act, slope, scale, sums,
    blocks, u_src, u_dst, norms, g_edge, g_mid, g_out, g_edge_norms, *refs,
):
    reply, d_inside_out, g_blocks, g_even, g_odd, g_norms = refs[-6:]
    pieces = refs[:-6]
    core, batch = place[1], place[2]
    stores = []
    d_src = d_q_src[...].astype(LOW)
    d_dst = sum(piece[...].astype(jnp.float32) for piece in pieces).astype(LOW)
    low_now = low[...]
    blank = jnp.zeros((D, WIDE - DE), jnp.float32)
    stores += small_stores(batch, 0, jnp.concatenate([dot_rows(low_now, d_src), blank], axis=1))
    stores += small_stores(batch, D, dot_rows(low_now, d_dst))
    for index, ref in enumerate((g_edge, g_mid, g_out)):
        stores += small_stores(batch, 2 * D + index * DE, ref[...])
    g_norms[...] = jnp.zeros_like(g_norms)
    g_norms[16:24, 0:LANES] = g_edge_norms[...]
    d_final = (
        cot[...].astype(jnp.float32)
        + dot_turned(d_src, u_src[:, 0:DE])
        + dot_turned(d_dst, u_dst[...])
    )
    scaled, inverse = norm_parts(summed[...], D)
    d_summed = norm_back(scaled, inverse, norms[2:3], d_final, D)
    put_norm(g_norms, 2, d_final * scaled)
    put_norm(g_norms, 3, d_final)
    d_narrow = d_summed.astype(LOW)
    one_low = one[...].astype(LOW)
    d_one = d_summed
    first_up = D // TILE
    parts = FF // D
    first_down = first_up + first_up * parts
    for part in range(parts):
        cols = slice(part * D, (part + 1) * D)
        put_blocks(g_blocks, first_down + part * first_up, dot_rows(act[:, cols], d_narrow))
        d_wide = (
            dot_turned(d_narrow, down_part(blocks, part)) * slope[:, cols].astype(jnp.float32)
        ).astype(LOW)
        put_blocks(g_blocks, first_up + part, dot_rows(one_low, d_wide), parts)
        d_one += dot_turned(d_wide, up_part(blocks, part))
    scaled, inverse = norm_parts(inside[...], D)
    d_inside = norm_back(scaled, inverse, norms[0:1], d_one, D)
    put_norm(g_norms, 0, d_one * scaled)
    put_norm(g_norms, 1, d_one)
    d_inside_out[...] = d_inside
    per_target = (d_inside * scale[...]).astype(LOW)
    high, rest = split_low(sums[...])
    put_blocks(g_blocks, 0, dot_rows(high, per_target) + dot_rows(rest, per_target))
    reply[...] = dot_turned(per_target, out_part(blocks)).astype(LOW)
    stores += small_stores(batch, 2 * D + 3 * DE, g_norms[...])
    put_sides((g_even, g_odd), core, stores)


def node_backward(place, operands, pieces, after):
    owned = operands[0].shape[0]
    half = shaped((4, EARLY_ROWS // 8, WIDE), LOW)
    amount = len(operands) + len(pieces)
    return pl.pallas_call(
        trimmed(node_backward_kernel, amount + 1, len(after)),
        in_specs=[pl.BlockSpec(memory_space=pltpu.SMEM)]
        + [pl.BlockSpec(memory_space=pltpu.VMEM)] * amount
        + anywhere(after),
        out_shape=[
            shaped((owned, D), LOW),
            shaped((owned, D), jnp.float32),
            shaped((8, 3, 4, OWNED_ROWS, LANES), LOW),
            half,
            half,
        ],
        scratch_shapes=[pltpu.VMEM((TILE, WIDE), jnp.float32)],
        compiler_params=params(),
    )(place, *operands, *pieces, *after)


def message_back_kernel(
    count, place, tall, wide, hidden, slope_one, slope_two, part_edge, x_all, w_mid, w_edge, *refs
):
    pieces = refs[0:count]
    (
        d_edge, even, odd, d_source, late_even, late_odd, table, total, g_mid, g_edge, from_source,
    ) = refs[-11:]
    step = pl.program_id(0)
    owned = d_source.shape[0]

    @pl.when(step == 0)
    def _():
        table[...] = jnp.concatenate([piece[...] for piece in pieces], axis=0).T
        total[...] = jnp.zeros_like(total)
        g_mid[...] = jnp.zeros_like(g_mid)
        g_edge[...] = jnp.zeros_like(g_edge)

    d_hidden = dot(table[...], tall[...])
    d_second = (d_hidden * slope_two[...].astype(jnp.float32)).astype(LOW)
    g_mid[...] += dot_turned(hidden[...], d_second)
    d_pre = (dot(w_mid[...], d_second) * slope_one[...].astype(jnp.float32)).astype(LOW)
    d_edge[...] = part_edge[...] + dot(w_edge[...], d_pre)
    turned = dot_turned(wide[...], d_pre)
    g_edge[...] += turned[0:DE]
    group = hidden.shape[1] // K
    from_source[pl.ds(step * group, group), :] = turned[DE : DE + group]
    total[...] += dot_turned(tall[...], d_pre)

    @pl.when(step == pl.num_programs(0) - 1)
    def _():
        put_halves((even, odd), total, owned)
        gathered = x_all[...]
        sources_low = from_source[...].astype(LOW)
        d_source[...] = sources_low
        chip, core, batch = place[0], place[1], place[2]
        matrices = (
            dot_rows(gathered[0:owned], sources_low),
            dot_rows(gathered, total[...].astype(LOW)),
            g_mid[...],
        )
        stores = []
        for row in range(3 * (D // TILE)):
            owner, slot = row // 3, row % 3
            strip = matrices[row // (D // TILE)][row % (D // TILE) * TILE :][0:TILE].astype(LOW)
            first = pl.multiple_of((owner // 2 ^ chip) * OWNED_ROWS + slot * TILE, TILE)
            for part in range(4):
                value = strip[:, part * LANES : (part + 1) * LANES]
                stores.append((owner % 2, value, (part ^ batch, pl.ds(first, TILE), slice(None))))
        half = DE // 2
        for side in range(2):
            strip = g_edge[side * half : (side + 1) * half].astype(LOW)
            for part in range(4):
                value = strip[:, part * LANES : (part + 1) * LANES]
                rows = slice(4 * OWNED_ROWS, 4 * OWNED_ROWS + half)
                stores.append((side, value, (part ^ batch, rows, slice(None))))
        put_sides((late_even, late_odd), core, stores)


def message_backward(
    place, tall, wide, hidden, slope_one, slope_two, part_edge, x_all, w_rows, w_edge, pieces, after
):
    nodes, rows = tall.shape
    owned = pieces[0].shape[0]
    block = block_of()
    count = len(pieces)
    half = (count // 2, owned, D)
    feature = tall_lanes(D, block) if nodes <= 1024 else pl.BlockSpec(
        (D, block), lambda i: (0, i), pipeline_mode=pl.Buffered(1)
    )
    late = (4, 4 * OWNED_ROWS + DE // 2, LANES)
    return pl.pallas_call(
        functools.partial(message_back_kernel, count),
        grid=(rows // block,),
        in_specs=[
            pl.BlockSpec(memory_space=pltpu.SMEM),
            tall_lanes(nodes, block),
            lanes(WIDE, block),
            feature,
            feature,
            feature,
            lanes(DE, block),
            whole((nodes, D)),
            pl.BlockSpec((D, D), lambda i: (2, 0), pipeline_mode=pl.Buffered(1)),
            whole((DE, D)),
        ]
        + [whole((owned, D))] * count
        + anywhere(after),
        out_specs=[
            lanes(DE, block),
            kept(half),
            kept(half),
            kept((owned, D)),
            kept(late),
            kept(late),
        ],
        out_shape=[
            shaped((DE, rows), jnp.float32),
            shaped(half, LOW),
            shaped(half, LOW),
            shaped((owned, D), LOW),
            shaped(late, LOW),
            shaped(late, LOW),
        ],
        scratch_shapes=[
            pltpu.VMEM((D, nodes), LOW),
            pltpu.VMEM((nodes, D), jnp.float32),
            pltpu.VMEM((D, D), jnp.float32),
            pltpu.VMEM((DE, D), jnp.float32),
            pltpu.VMEM((owned, D), jnp.float32),
        ],
        compiler_params=params(),
    )(
        place, tall, wide, hidden, slope_one, slope_two, part_edge, x_all, w_rows, w_edge,
        *pieces, *after,
    )


def node_gradient_kernel(inside, d_source, w_rows, *refs):
    pieces, out = refs[:-1], refs[-1]
    d_target = sum(piece[...].astype(jnp.float32) for piece in pieces).astype(LOW)
    out[...] = (
        inside[...]
        + dot_turned(d_source[...], w_rows[0:D])
        + dot_turned(d_target, w_rows[D : 2 * D])
    )


def node_gradient(inside, d_source, w_rows, pieces):
    return pl.pallas_call(
        node_gradient_kernel,
        out_shape=shaped(inside.shape, jnp.float32),
        compiler_params=params(),
    )(inside, d_source, w_rows, *pieces)


def add_halves_kernel(left, right, *outs):
    for index, out in enumerate(outs):
        total = left[index].astype(jnp.float32) + right[index].astype(jnp.float32)
        out[...] = total.astype(out.dtype)


def add_halves(left, right):
    shape = left.shape[1:]
    return pl.pallas_call(
        add_halves_kernel,
        out_shape=[shaped(shape, jnp.float32)] + [shaped(shape, LOW)] * (left.shape[0] - 1),
        compiler_params=params(),
    )(left, right)


def matrices_kernel(groups, w_edge, e_src, e_dst, e_edge, e_mid, e_out):
    for index in range(6):
        block, side = index // 2, index % 2
        w_edge[block * TILE : (block + 1) * TILE, side * QUAD : (side + 1) * QUAD] = groups[
            index
        ].astype(LOW)
    for ref, first in (
        (e_src, SPAN_GROUPS), (e_dst, 2 * SPAN_GROUPS), (e_edge, 3 * SPAN_GROUPS),
        (e_mid, 3 * SPAN_GROUPS + 3), (e_out, 3 * SPAN_GROUPS + 6),
    ):
        for block in range(ref.shape[0] // TILE):
            ref[block * TILE : (block + 1) * TILE] = groups[first + block].astype(LOW)


def matrices(groups):
    return pl.pallas_call(
        matrices_kernel,
        out_shape=[shaped((DE, D), LOW)]
        + [shaped((D, WIDE), LOW)] * 2
        + [shaped((DE, WIDE), LOW)] * 3,
        compiler_params=params(),
    )(groups)


def assemble_kernel(count, place, *refs):
    lines, pieces, rows, x_all = refs[0:8], refs[8:-2], refs[-2], refs[-1]
    chip, core, batch = place[0], place[1], place[2]
    owned = pieces[0].shape[0]
    for index, piece in enumerate(lines):
        side, part = index // 4, index % 4
        for line in range(4):
            row = ((line ^ chip) * 2 + (side ^ core)) * OWNED_ROWS
            lane = (part ^ batch) * LANES
            rows[
                pl.ds(pl.multiple_of(row, TILE), OWNED_ROWS),
                pl.ds(pl.multiple_of(lane, LANES), LANES),
            ] = piece[line]
    for index, piece in enumerate(pieces):
        x_all[index * owned : (index + 1) * owned] = piece[...]


def assemble(place, lines, pieces):
    owned = pieces[0].shape[0]
    amount = len(lines) + len(pieces)
    return pl.pallas_call(
        functools.partial(assemble_kernel, len(pieces)),
        in_specs=[pl.BlockSpec(memory_space=pltpu.SMEM)]
        + [pl.BlockSpec(memory_space=pltpu.VMEM)] * amount,
        out_shape=[shaped((3 * D, D), LOW), shaped((8 * owned, D), LOW)],
        compiler_params=params(),
    )(place, *lines, *pieces)


def own_rows_kernel(tiles, rows, quarters, flat, pair):
    load_flat(tiles, flat)
    for index, group in enumerate(group_list(0, 24, 4)):
        block, side = index // 2, index % 2
        value = group_in(flat, pair, group).astype(LOW)
        rows[block * TILE : (block + 1) * TILE, side * QUAD : (side + 1) * QUAD] = value
        for half in range(2):
            quarters[2 * side + half, block * TILE : (block + 1) * TILE, :] = value[
                :, half * LANES : (half + 1) * LANES
            ]


def own_rows(tiles):
    return pl.pallas_call(
        own_rows_kernel,
        out_shape=[
            shaped((OWNED_ROWS, D), LOW),
            shaped((4, OWNED_ROWS, LANES), LOW),
        ],
        scratch_shapes=[
            pltpu.VMEM((flat_rows(24), LANES), jnp.float32),
            pltpu.VMEM((TILE, LANES), jnp.float32),
        ],
        compiler_params=params(),
    )(tiles)


LANES = 128
QUAD = 4 * TILE
FLAT = TILE * TILE // LANES


def group_list(first, last, size):
    return [list(range(t, min(t + size, last))) for t in range(first, last, size)]


def load_flat(ref, flat):
    amount = ref.shape[0]
    for top in range(0, amount, 8):
        rows = min(8, amount - top)
        for part in range(FLAT):
            flat[pl.ds(top * FLAT + 8 * part, rows), :] = ref[
                top : top + rows, part * LANES : (part + 1) * LANES
            ]


def store_flat(ref, flat, first=0, last=None):
    last = ref.shape[0] if last is None else last
    while first < last:
        rows = min(8 - first % 8, last - first)
        top = first // 8 * 8
        for part in range(FLAT):
            ref[first : first + rows, part * LANES : (part + 1) * LANES] = flat[
                pl.ds(top * FLAT + 8 * part + first - top, rows), :
            ]
        first += rows


def tile_rows(tile):
    return pl.ds(tile // 8 * 8 * FLAT + tile % 8, FLAT, stride=8)


def lower_half(shape):
    return lax.broadcasted_iota(jnp.int32, shape, 1) < TILE


def group_in(flat, pair, tiles):
    left = lower_half((FLAT, LANES))
    halves = []
    for first in range(0, 4, 2):
        here = tiles[first : first + 2]
        one = flat[tile_rows(here[0]), :] if here else jnp.zeros((FLAT, LANES), jnp.float32)
        two = flat[tile_rows(here[1]), :] if len(here) > 1 else jnp.zeros_like(one)
        pair[pl.ds(0, FLAT, stride=2), :] = jnp.where(left, one, pltpu.roll(two, TILE, 1))
        pair[pl.ds(1, FLAT, stride=2), :] = jnp.where(left, pltpu.roll(one, TILE, 1), two)
        halves.append(pair[...])
    return jnp.concatenate(halves, axis=1)


def group_out(value, flat, pair, tiles):
    left = lower_half((FLAT, LANES))
    for first in range(0, 4, 2):
        here = tiles[first : first + 2]
        if not here:
            continue
        pair[...] = value[:, first * TILE : first * TILE + LANES]
        even = pair[pl.ds(0, FLAT, stride=2), :]
        odd = pair[pl.ds(1, FLAT, stride=2), :]
        flat[tile_rows(here[0]), :] = jnp.where(left, even, pltpu.roll(odd, TILE, 1))
        if len(here) > 1:
            flat[tile_rows(here[1]), :] = jnp.where(left, pltpu.roll(even, TILE, 1), odd)


def flat_rows(amount):
    return -(-amount // 8) * 8 * FLAT


SPAN_GROUPS = 8


def regroup_small_kernel(count, *refs):
    tiles, outs = refs[0:count], refs[count : 2 * count]
    flat, pair = refs[-2:]
    step = pl.program_id(0)
    for condition, amount, size, spot in (
        (step == 0, 24, 4, 0),
        ((step > 0) & (step < 4), 24, 3, 0),
        (step == 4, 3, 3, 0),
    ):

        @pl.when(condition)
        def _():
            for ref, out in zip(tiles, outs):
                load_flat(ref, flat)
                for index, group in enumerate(group_list(0, amount, size)):
                    out[spot + index] = group_in(flat, pair, group)


def regroup_small(arrays, after=()):
    count = len(arrays)
    shape = (5 * SPAN_GROUPS, TILE, QUAD)
    out_spec = pl.BlockSpec((SPAN_GROUPS, TILE, QUAD), lambda i: (i, 0, 0))
    return pl.pallas_call(
        trimmed(functools.partial(regroup_small_kernel, count), count, len(after)),
        grid=(5,),
        in_specs=[pl.BlockSpec((24, TILE * TILE), lambda i: (i, 0))] * count + anywhere(after),
        out_specs=[out_spec] * count,
        out_shape=[shaped(shape, jnp.float32)] * count,
        scratch_shapes=[
            pltpu.VMEM((flat_rows(24), LANES), jnp.float32),
            pltpu.VMEM((TILE, LANES), jnp.float32),
        ],
        compiler_params=params(),
    )(*arrays, *after)


def regroup_big_kernel(count, *refs):
    tiles, outs = refs[0:count], refs[count : 2 * count]
    flat, pair = refs[-2:]
    for ref, out in zip(tiles, outs):
        load_flat(ref, flat)
        for index, group in enumerate(group_list(0, 24, 4)):
            out[index] = group_in(flat, pair, group)


def regroup_big(arrays, after=()):
    count = len(arrays)
    return pl.pallas_call(
        trimmed(functools.partial(regroup_big_kernel, count), count, len(after)),
        in_specs=[pl.BlockSpec(memory_space=pltpu.VMEM)] * count + anywhere(after),
        out_shape=[shaped((6, TILE, QUAD), jnp.float32)] * count,
        scratch_shapes=[
            pltpu.VMEM((flat_rows(24), LANES), jnp.float32),
            pltpu.VMEM((TILE, LANES), jnp.float32),
        ],
        compiler_params=params(),
    )(*arrays, *after)


def soap_groups(grads, weights, firsts, seconds, lefts, rights, rates):
    count = range(len(grads))
    lane = lax.broadcasted_iota(jnp.int32, (TILE, QUAD), 1) // TILE
    masks = [jnp.where(lane == k, 1.0, 0.0) for k in range(4)]
    low_masks = [mask.astype(LOW) for mask in masks]

    def diagonal(values):
        return jnp.concatenate([values * mask for mask in low_masks], axis=0)

    def thrice(product_of, values, sides):
        parts = [split_low(v) for v in values]
        both = [product_of(jnp.concatenate(parts[i], axis=0), sides[i][0]) for i in count]
        rest = [product_of(parts[i][0], sides[i][1]) for i in count]
        return [both[i][0:TILE] + both[i][TILE:] + rest[i] for i in count]

    right_sides = [[diagonal(part) for part in split_low(v)] for v in rights]
    left_parts = [split_low(v) for v in lefts]
    left_sides = [jnp.concatenate([high, low, high], axis=0) for high, low in left_parts]
    half = [split_low(v) for v in thrice(dot, grads, right_sides)]
    half = [jnp.concatenate([high, high, low], axis=0) for high, low in half]
    full = [dot_rows(left_sides[i], half[i]) for i in count]
    turned = [sum(v[TILE * k : TILE * (k + 1)] * masks[k] for k in range(4)) for v in full]
    new_one = [BETA_ONE * firsts[i] + (1.0 - BETA_ONE) * turned[i] for i in count]
    new_two = [
        BETA_TWO * seconds[i] + (1.0 - BETA_TWO) * turned[i] * turned[i] for i in count
    ]
    fix_one = 1.0 / (1.0 - BETA_ONE**STEP)
    fix_two = 1.0 / (1.0 - BETA_TWO**STEP)
    steps = [
        new_one[i] * fix_one / (jnp.sqrt(new_two[i] * fix_two) + EPS_ADAM) for i in count
    ]
    sides = [diagonal(v.astype(LOW)) for v in steps]
    half = [dot(left_parts[i][0], sides[i]).astype(LOW) for i in count]
    restored = [dot_turned(half[i], right_sides[i][0]) for i in count]
    new = [
        weights[i] - rates[i] * (restored[i] + DECAY * weights[i]) for i in count
    ]
    return new_one, new_two, new


TOGETHER = 5
EARLY_ROWS = 1664


def block_rate(block):
    middle = (2 * D + DE) ** (-0.5)
    return jnp.where(
        block < 16,
        middle,
        jnp.where(
            block < 24,
            D ** (-0.5),
            jnp.where(block < 32, 2.5 * D ** (-0.5), jnp.where(block < 64, D ** (-0.5), FF ** (-0.5))),
        ),
    )


def small_rates():
    middle = (2 * D + DE) ** (-0.5)
    return [middle] * 19 + [DE ** (-0.5)] * 3 + [1.5 * DE ** (-0.5)] * 3


NORM_ROWS = 19


def soap_early_kernel(scale, place, grads, rates, weight, first, second, left, right, *refs):
    norms, outs = refs[0:3], refs[3:9]
    flats, pairs = refs[9:12], refs[12]
    step = pl.program_id(0)
    core, batch = place[1], place[2]
    piece = EARLY_ROWS // 8

    def rows_of(begin, end):
        parts = []
        while begin < end:
            index, offset = begin // piece, begin % piece
            amount = min(end - begin, piece - offset)
            parts.append(grads[index // 4 ^ core, index % 4 ^ batch, offset : offset + amount, :])
            begin += amount
        value = parts[0] if len(parts) == 1 else jnp.concatenate(parts, axis=0)
        return value.astype(jnp.float32) * scale

    def groups(start, amount):
        here = range(amount)
        state = [[ref[i] for i in here] for ref in (weight, first, second, left, right)]
        results = soap_groups(
            [rows_of((start + i) * TILE, (start + i + 1) * TILE) for i in here],
            *state,
            [rates[start + i : start + i + 1] for i in here],
        )
        for spot in here:
            tiles = list(range(spot * 3, spot * 3 + 3))
            for kind, flat in enumerate(flats):
                group_out(results[kind][spot], flat, pairs.at[kind * SPAN_GROUPS + spot], tiles)

    for index, amount in enumerate((8, 8, 8, 1)):

        @pl.when(step == index)
        def _():
            groups(8 * index, amount)

    @pl.when(step == 0)
    def _():
        rows = rows_of(25 * TILE, 25 * TILE + 32)[0:NORM_ROWS, 0:LANES]
        results = adam_step(*(ref[...] for ref in norms), rows)
        for ref, value in zip(outs[3:6], (results[2], results[0], results[1])):
            ref[...] = value

    for ref, flat in zip(outs[0:3], flats):
        store_flat(ref, flat)


def soap_early(scale, place, grads, state, norms):
    out = shaped((99, TILE * TILE), jnp.float32)
    line = shaped((NORM_ROWS, LANES), jnp.float32)
    rates = jnp.asarray(np.repeat(np.array(small_rates(), np.float32)[:, None], QUAD, axis=1))
    return pl.pallas_call(
        functools.partial(soap_early_kernel, scale),
        grid=(4,),
        in_specs=[pl.BlockSpec(memory_space=pltpu.SMEM), whole(grads.shape), whole(rates.shape)]
        + [pl.BlockSpec((SPAN_GROUPS, TILE, QUAD), lambda i: (1 + i, 0, 0))] * 5
        + [whole(line.shape)] * 3,
        out_specs=[pl.BlockSpec((24, TILE * TILE), lambda i: (1 + i, 0))] * 3
        + [kept(line.shape)] * 3,
        out_shape=[out, out, out, line, line, line],
        scratch_shapes=[pltpu.VMEM((flat_rows(24), LANES), jnp.float32)] * 3
        + [pltpu.VMEM((3 * SPAN_GROUPS, TILE, LANES), jnp.float32)],
        compiler_params=params(),
    )(place, grads, rates, *state, *norms)


def soap_late_kernel(scale, place, own, other_one, other_two, other_three, pieces, *refs):
    state, v_state = refs[0:5], refs[5:10]
    older = refs[12]
    one, two, new, low, v_one, v_two, v_new, v_low = refs[13:21]
    flats, v_flats, pairs = refs[21:24], refs[24:27], refs[27]
    chip, core, batch = place[0], place[1], place[2]
    groups = group_list(0, 24, 4)
    received = (own, other_one, other_two, other_three)

    def v_block(block, side):
        parts = []
        for part in (2 * side, 2 * side + 1):
            rows = []
            for begin in range(block * TILE, (block + 1) * TILE, TILE // 2):
                half, offset = begin // (DE // 2), begin % (DE // 2)
                rows.append(pieces[half ^ core, part ^ batch, offset : offset + TILE // 2, :])
            parts.append(jnp.concatenate(rows, axis=0))
        return jnp.concatenate(parts, axis=1).astype(jnp.float32)

    def own_part(block, part):
        rows = slice(block * TILE, (block + 1) * TILE)
        shifted = slice(part * OWNED_ROWS + rows.start, part * OWNED_ROWS + rows.stop)
        total = tree_sum([ref[shifted, :].astype(jnp.float32) for ref in received])
        return jnp.where(batch == 0, received[part][rows, :].astype(jnp.float32), total)

    def own_block(block, side):
        return jnp.concatenate([own_part(block, 2 * side), own_part(block, 2 * side + 1)], axis=1)

    first = batch * 24 + (chip * 2 + core) * 3
    own_rates = [block_rate(first + i // 2) for i in range(6)]
    v_rates = [(2 * D + DE) ** (-0.5)] * 6
    for grad_of, values, rates, targets, base in (
        (own_block, state, own_rates, flats, 0),
        (v_block, v_state, v_rates, v_flats, 18),
    ):
        here = range(6)
        grads = [grad_of(i // 2, i % 2) * scale for i in here]
        results = soap_groups(grads, *[[ref[i] for i in here] for ref in values], rates)
        for index in here:
            for kind, flat in enumerate(targets):
                group_out(results[kind][index], flat, pairs.at[base + kind * 6 + index], groups[index])
    for ref, flat in zip((one, two, new, v_one, v_two, v_new), (*flats, *v_flats)):
        store_flat(ref, flat)
    low[...] = new[...].astype(LOW)
    v_low[...] = jnp.concatenate([v_new[...], older[24:]], axis=0).astype(LOW)


def soap_late(scale, place, received, pieces, state, v_state, early):
    out = shaped((24, TILE * TILE), jnp.float32)
    small = shaped(early[0].shape, jnp.float32)
    front = pl.BlockSpec((24, TILE * TILE), lambda i: (0, 0))
    group = whole((6, TILE, QUAD))
    flat = pltpu.VMEM((flat_rows(24), LANES), jnp.float32)
    return pl.pallas_call(
        functools.partial(soap_late_kernel, scale),
        grid=(1,),
        in_specs=[
            pl.BlockSpec(memory_space=pltpu.SMEM),
        ]
        + [whole(v.shape) for v in received]
        + [whole(pieces.shape)]
        + [group] * 10
        + [pl.BlockSpec(memory_space=pl.ANY)] * 2
        + [whole(small.shape)],
        out_specs=[front] * 7 + [whole(small.shape)],
        out_shape=[out, out, out, shaped((24, TILE * TILE), LOW), small, small, small]
        + [shaped(small.shape, LOW)],
        scratch_shapes=[flat] * 6 + [pltpu.VMEM((36, TILE, LANES), jnp.float32)],
        input_output_aliases={16: 4, 17: 5, 18: 6},
        compiler_params=params(),
    )(place, *received, pieces, *state, *v_state, *early)


def swap_core(values):
    return lax.ppermute(values, "core", [(0, 1), (1, 0)])


def swap_chip(values, shift):
    chips = lax.axis_size("chip")
    return lax.ppermute(values, "chip", [(i, i ^ shift) for i in range(chips)])


def gate(values, others):
    return lax.optimization_barrier((values, others))[0]


def send_pieces(values):
    chips = lax.axis_size("chip")
    return [values] + [swap_chip(values, shift) for shift in range(1, chips)]


def gather_pieces(values, fill=()):
    return swap_pieces(send_pieces(values), fill)


def swap_pieces(parts, fill=()):
    parts = gate(parts, fill)
    return [half for part in parts for half in (part, swap_core(part))]


def reduce_pieces(even, odd):
    return send_near(add_halves(even, swap_core(odd)))


def send_near(near):
    return [near[0]] + [swap_chip(near[shift], shift) for shift in range(1, len(near))]


def swap_batch(values, shift):
    return lax.ppermute(values, "batch", [(i, i ^ shift) for i in range(4)])


def pick(values, index):
    return lax.dynamic_index_in_dim(values, index, 0, keepdims=False)


def tree_sum(parts):
    while len(parts) > 1:
        parts = [parts[i] + parts[i + 1] for i in range(0, len(parts), 2)]
    return parts[0]


def wide_values(values):
    return values.astype(jnp.float32)


def gather_first(place, quarters, x, batch, fill):
    pieces = [x] + [swap_chip(x, shift) for shift in range(1, 4)]
    sent = [
        lax.ppermute(quarters[index], "batch", [(0, index)]) for index in range(1, 4)
    ]
    quarter = jnp.where(batch == 0, quarters[0], sent[0] + sent[1] + sent[2])
    quarter = gate(quarter, fill[0])
    lines = jnp.stack([quarter] + [swap_chip(quarter, shift) for shift in range(1, 4)])
    lines = gate(lines, fill[1])
    parts = [lines] + [swap_batch(lines, shift) for shift in range(1, 4)]
    parts, pieces = gate((parts, pieces), fill[2])
    pieces = [half for piece in pieces for half in (piece, swap_core(piece))]
    return assemble(place, parts + [swap_core(part) for part in parts], pieces)


def reduce_small(near):
    total = near[0]
    for shift in range(1, 4):
        total = total + wide_values(swap_batch(near[shift], shift))
    total = total.astype(LOW)
    others = [total] + [swap_chip(total, shift) for shift in range(1, 4)]
    return total, tree_sum([wide_values(v) for v in others]).astype(LOW)


def share_small(total, token):
    others = [total] + gate([swap_batch(total, shift) for shift in range(1, 4)], token)
    parts = jnp.stack(others)
    return jnp.stack([parts, swap_core(parts)])


def reduce_late(near, early, batch, fill, third, other):
    received = [swap_batch(near[shift], shift) for shift in range(1, 4)]
    received = gate(received, fill)
    total = near[0] + sum(wide_values(part) for part in received)
    shared = total[4 * OWNED_ROWS :]
    lines = [total[OWNED_ROWS * i : OWNED_ROWS * (i + 1)] for i in range(4)]
    sent = [
        jnp.concatenate([lines[shift], shared], axis=0).astype(LOW) for shift in range(1, 4)
    ]
    received = [swap_chip(part, shift) for shift, part in enumerate(sent, 1)]
    quarter = lines[0]
    shares = [wide_values(shared.astype(LOW))]
    for part in received:
        got = wide_values(part)
        quarter = quarter + got[0:OWNED_ROWS]
        shares.append(got[OWNED_ROWS:])
    shared = tree_sum(shares).astype(LOW)
    quarter = jnp.pad(quarter.astype(LOW)[None], ((0, 3), (0, 0), (0, 0)))

    def outgoing(target):
        block = jnp.where(target == 0, quarter, pick(early, jnp.maximum(target - 1, 0)))
        return jnp.concatenate([block.reshape(4 * OWNED_ROWS, LANES), shared], axis=0)

    sent = gate([outgoing(batch ^ shift) for shift in range(4)], third)
    received = [swap_batch(part, shift) for shift, part in enumerate(sent) if shift]
    received = gate([sent[0]] + received, other)
    edges = jnp.stack([part[4 * OWNED_ROWS :] for part in received])
    edges = jnp.stack([edges, swap_core(edges)])
    return received, edges


def pad_to(matrix, height, breadth):
    return jnp.pad(matrix, ((0, height - matrix.shape[0]), (0, breadth - matrix.shape[1])))


def norm_rows(vector):
    return vector.reshape(NORM_ROWS, LANES)


def norm_vector(rows):
    return rows.reshape(-1)


def gather_plain(tiles, every):
    amount = tiles.shape[0]
    unit = math.gcd(amount, D // TILE)
    local = tiles.astype(LOW).reshape(amount // unit, unit, TILE, TILE)
    local = local.transpose(0, 2, 1, 3).reshape(amount // unit, TILE, unit * TILE)
    units = lax.all_gather(local, every, axis=0, tiled=True)
    blocks = units.reshape(-1, D // TILE // unit, TILE, unit * TILE).transpose(0, 2, 1, 3)
    blocks = blocks.reshape(-1, TILE, D)
    return blocks[0:24].reshape(3 * D, D), blocks


def soap_plain(weight, moment_one, moment_two, left, right, gradient, rates):
    left, right = as_square(left), as_square(right)
    high = lax.Precision.HIGHEST
    turned = jnp.einsum("tji,tjk->tik", left, gradient, precision=high)
    turned = jnp.einsum("tik,tkl->til", turned, right, precision=high)
    new_one = BETA_ONE * as_square(moment_one) + (1.0 - BETA_ONE) * turned
    new_two = BETA_TWO * as_square(moment_two) + (1.0 - BETA_TWO) * turned * turned
    direction = (
        new_one / (1.0 - BETA_ONE**STEP) / (jnp.sqrt(new_two / (1.0 - BETA_TWO**STEP)) + EPS_ADAM)
    )
    restored = jnp.einsum("tij,tjk->tik", left, direction, precision=high)
    restored = jnp.einsum("tik,tlk->til", restored, right, precision=high)
    weight = as_square(weight)
    new = weight - rates[:, None, None] * (restored + DECAY * weight)
    return as_flat(new_one), as_flat(new_two), as_flat(new)


def update_plain(g_late, g_early, g_small, every, scale, big, small, norms):
    amount = big[0].shape[0]
    unit = math.gcd(amount, D // TILE)
    g_late, g_small = jnp.stack(g_late), jnp.stack(g_small).reshape(EARLY_ROWS, WIDE)
    late = g_late[:, :, 0 : 4 * OWNED_ROWS].reshape(2, 4, 4, OWNED_ROWS, LANES)
    late = late.transpose(2, 0, 3, 1, 4).reshape(24, TILE, D)
    w_edge = g_late[:, :, 4 * OWNED_ROWS :].transpose(0, 2, 1, 3).reshape(DE, D)
    early = g_early.reshape(8, 3, 4, 3, TILE, LANES).transpose(1, 0, 3, 4, 2, 5)
    early = early.reshape(72, TILE, D)
    grads = jnp.concatenate([late, early], axis=0)
    grads = grads.reshape(-1, TILE, D // TILE // unit, unit * TILE).transpose(0, 2, 1, 3)
    own = lax.psum_scatter(
        grads.reshape(-1, TILE, unit * TILE), every, scatter_dimension=0, tiled=True
    )
    own = wide_values(own).reshape(amount // unit, TILE, unit, TILE).transpose(0, 2, 1, 3)
    own = own.reshape(amount, TILE, TILE) * scale
    w_edge, g_small = lax.psum((wide_values(w_edge), wide_values(g_small)), every)
    strips = g_small[0:1600, 0:DE].reshape(25, TILE, 3, TILE).transpose(0, 2, 1, 3)
    tiles = jnp.concatenate(
        [as_square(to_flat_tiles(w_edge)), strips.reshape(75, TILE, TILE)], axis=0
    )
    first = lax.axis_index(every) * amount
    rates = lax.dynamic_slice_in_dim(
        jnp.asarray(rate_table(big_shapes(), big_spreads())), first, amount
    )
    big_new = soap_plain(*big, own, rates)
    rates = jnp.asarray(rate_table(small_shapes(), small_spreads()))
    small_new = soap_plain(*small, tiles * scale, rates)
    norm_new = adam_step(*norms, norm_vector(g_small[1600:1619, 0:LANES]) * scale)
    return big_new, small_new, norm_new


def body(
    node,
    edge,
    dest_device,
    dest_local,
    node_valid,
    node_cot,
    edge_cot,
    big_weight,
    big_first,
    big_second,
    big_left,
    big_right,
    small_weight,
    small_first,
    small_second,
    small_left,
    small_right,
    norm_params,
    norm_first,
    norm_second,
):
    chips = lax.axis_size("chip")
    every = ("batch", "chip", "core")
    shards = 2 * chips
    owned = node.shape[1]
    nodes = owned * shards
    rows = owned * K
    complexes = node.shape[0] * lax.axis_size("batch")
    tuned = chips == 4 and lax.axis_size("batch") == 4 and big_weight.shape[0] == 24
    chip, core, batch = (lax.axis_index(axis) for axis in ("chip", "core", "batch"))
    grad_scale = 1.0 / math.sqrt(complexes * nodes * K)
    x = node[0]
    big_state = (big_weight, big_first, big_second, big_left, big_right)
    small_state = (small_weight, small_first, small_second, small_left, small_right)
    norm_state = (norm_params, norm_first, norm_second)

    place = jnp.stack([chip, core, batch]).astype(jnp.int32) * int(tuned)
    small_groups = list(regroup_small([small_weight]))
    w_edge, e_src, e_dst, e_edge, e_mid, e_out = matrices(small_groups[0])
    norms = norm_params[0 : 4 * D].reshape(4, D)
    edge_norms = pad_to(norm_params[4 * D :].reshape(2, DE), 8, WIDE)
    valid = node_valid[0].astype(jnp.float32).reshape(owned, 1)
    me = chip * 2 + core
    relative = (dest_device[0].reshape(1, rows) ^ me) * owned + dest_local
    tall, wide, ok_row = prepare(relative, valid, edge[0].T, nodes)
    if tuned:
        own, quarters = own_rows(big_weight)
        blocks = lax.all_gather(own, every, axis=0, tiled=True).reshape(-1, TILE, D)
        w_rows, x_all = gather_first(
            place, quarters, x, batch, (small_groups[0], (w_edge, e_src), (tall, wide))
        )
    else:
        w_rows, blocks = gather_plain(big_weight, every)
        x_all = jnp.concatenate(gather_pieces(x), axis=0)

    even, odd, hidden, slope_one, slope_two = message_forward(
        tall, wide, ok_row, x_all, owned, w_rows, w_edge, ()
    )
    sums = reduce_pieces(even, odd)
    if tuned:
        small_groups += regroup_small(small_state[1:5], (even,))
    node_low, q_src, q_dst, inside, one, act, slope, summed, scale, sums = node_forward(
        x, valid, blocks, e_src, e_dst, norms, sums, small_groups[1:2]
    )
    big_groups = list(regroup_big(big_state, (q_dst,))) if tuned else []
    q_pieces = gather_pieces(q_dst, big_groups[0:1])
    (
        edge_new, part_edge, even, odd, d_q_src, g_e_edge, g_e_mid, g_e_out, g_e_norms,
    ) = edge_phase(
        tall, wide, edge_cot[0].T, q_pieces, q_src, e_edge, e_mid, e_out, edge_norms, (),
    )
    d_q_dst = reduce_pieces(even, odd)
    reply, d_inside, g_early, *g_small = node_backward(
        place,
        [
            node_cot[0], d_q_src, node_low, summed, one, inside, act, slope, scale, sums,
            blocks, e_src, e_dst, norms, g_e_edge, g_e_mid, g_e_out, g_e_norms,
        ],
        d_q_dst,
        (),
    )
    replies = send_pieces(reply)
    held = ()
    if tuned:
        near_small = gate(add_halves(g_small[0], swap_core(g_small[1])), replies[1])
        part_small, small_sum = reduce_small(near_small)
        held = (part_small,)
    replies = swap_pieces(replies, held)
    d_edges, even, odd, d_p_src, *g_late = message_backward(
        place, tall, wide, hidden, slope_one, slope_two, part_edge, x_all, w_rows, w_edge, replies, held,
    )
    near_p = add_halves(even, swap_core(odd))
    d_p_dst = send_near(near_p)
    d_features = node_gradient(d_inside, d_p_src, w_rows, d_p_dst)

    if tuned:
        norm_groups = [norm_rows(v) for v in norm_state]
        late_groups = small_groups
        early = lax.psum_scatter(
            gate(g_early, replies), ("chip", "core"), scatter_dimension=0, tiled=True
        )
        early = early.reshape(3, 4, OWNED_ROWS, LANES)
        near_late = add_halves(g_late[0], swap_core(gate(g_late[1], small_sum)))
        small_sum = share_small(small_sum, near_late[0])
        *early_new, norm_new, norm_one, norm_two = soap_early(
            grad_scale, place, small_sum, small_groups, norm_groups
        )
        mine, edges = reduce_late(near_late, early, batch, early_new[0], near_p, d_features)
        big_one, big_two, big_new, big_low, small_one, small_two, small_new, small_low = soap_late(
            grad_scale, place, mine, edges, big_groups, late_groups, early_new
        )
        norm_one, norm_two, norm_new = (norm_vector(v) for v in (norm_one, norm_two, norm_new))
    else:
        (
            (big_one, big_two, big_new),
            (small_one, small_two, small_new),
            (norm_one, norm_two, norm_new),
        ) = update_plain(
            g_late, g_early, g_small, every, grad_scale, big_state, small_state, norm_state
        )
        big_low = big_new.astype(LOW)
        small_low = small_new.astype(LOW)
    return (
        node_low[None],
        edge_new.T[None],
        d_features[None],
        d_edges.T[None],
        big_one,
        big_two,
        big_new,
        big_low,
        small_one,
        small_two,
        small_new,
        small_low,
        norm_one,
        norm_two,
        norm_new,
    )


def solution(mesh):
    batch, shards = mesh.devices.shape
    fine = Mesh(mesh.devices.reshape(batch, shards // 2, 2), ("batch", "chip", "core"))
    edge = ("chip", "core")
    every = ("batch", "chip", "core")
    placed = (
        P("batch", edge, None),
        P("batch", edge, None),
        P("batch", edge, None),
        P("batch", edge),
        P("batch", edge),
        P("batch", edge, None),
        P("batch", edge, None),
        P(every, None),
        P(every, None),
        P(every, None),
        P(every, None),
        P(every, None),
        P(),
        P(),
        P(),
        P(),
        P(),
        P(),
        P(),
        P(),
    )
    return jax.shard_map(
        body,
        mesh=fine,
        in_specs=placed,
        out_specs=(
            P("batch", edge, None),
            P("batch", edge, None),
            P("batch", edge, None),
            P("batch", edge, None),
            P(every, None),
            P(every, None),
            P(every, None),
            P(every, None),
            P(),
            P(),
            P(),
            P(),
            P(),
            P(),
            P(),
        ),
        check_vma=False,
    )
```

```python
import functools
import math

import jax
import jax.numpy as jnp
import numpy as np
from jax import lax
from jax.experimental import pallas as pl
from jax.experimental.pallas import tpu as pltpu
from jax.sharding import Mesh
from jax.sharding import PartitionSpec as P

D = 512
DE = 192
FF = 2048
K = 60
TILE = 64
STEP = 10


BETA_ONE = 0.5
BETA_TWO = 0.5
EPS_ADAM = 1e-08
EPS_NORM = 1e-05
DECAY = 0.01
NORM_RATE = 0.4
PRECISION_HIGH = lax.Precision.HIGHEST


def big_shapes():
    return [(D, D), (D, D), (D, D), (D, D), (D, FF), (FF, D)]


def small_shapes():
    return [(DE, D), (D, DE), (D, DE), (DE, DE), (DE, DE), (DE, DE)]


def big_spreads():
    middle = (2 * D + DE) ** (-0.5)
    return [middle, middle, D ** (-0.5), 2.5 * D ** (-0.5), D ** (-0.5), FF ** (-0.5)]


def small_spreads():
    middle = (2 * D + DE) ** (-0.5)
    return [middle, middle, middle, middle, DE ** (-0.5), 1.5 * DE ** (-0.5)]


def rate_table(shapes, spreads):
    amounts = [height // TILE * (breadth // TILE) for height, breadth in shapes]
    return np.repeat(np.array(spreads, np.float32), amounts)


def as_square(flat_tiles):
    return flat_tiles.reshape(flat_tiles.shape[0], TILE, TILE)


def as_flat(square_tiles):
    return square_tiles.reshape(square_tiles.shape[0], TILE * TILE)


def from_tiles(tile_stack, shapes):
    matrices = []
    offset = 0
    for height, breadth in shapes:
        amount = height // TILE * (breadth // TILE)
        blocked = tile_stack[offset : offset + amount].reshape(
            height // TILE, breadth // TILE, TILE, TILE
        )
        matrices.append(blocked.transpose(0, 2, 1, 3).reshape(height, breadth))
        offset += amount
    return matrices


def to_flat_tiles(matrix):
    height, breadth = matrix.shape
    blocked = matrix.reshape(height // TILE, TILE, breadth // TILE, TILE)
    return blocked.transpose(0, 2, 1, 3).reshape(-1, TILE * TILE)


def adam_step(params, moment_one, moment_two, gradient):
    new_one = BETA_ONE * moment_one + (1.0 - BETA_ONE) * gradient
    new_two = BETA_TWO * moment_two + (1.0 - BETA_TWO) * gradient * gradient
    direction = (
        new_one / (1.0 - BETA_ONE**STEP) / (jnp.sqrt(new_two / (1.0 - BETA_TWO**STEP)) + EPS_ADAM)
    )
    return (new_one, new_two, params - NORM_RATE * direction)


def times_transposed(left_side, right_side):
    return lax.dot_general(
        left_side, right_side, (((1,), (1,)), ((), ())), preferred_element_type=jnp.float32
    )


LOW = jnp.bfloat16
WIDE = 256
GELU_A = math.sqrt(2.0 / math.pi)
GELU_B = GELU_A * 0.044715
OWNED_ROWS = 3 * TILE


def dot(left, right):
    return jnp.dot(left, right, preferred_element_type=jnp.float32)


def dot_rows(left, right):
    return lax.dot_general(
        left, right, (((0,), (0,)), ((), ())), preferred_element_type=jnp.float32
    )


def dot_turned(left, right):
    return lax.dot_general(
        left, right, (((1,), (1,)), ((), ())), preferred_element_type=jnp.float32
    )


def split_low(values):
    high = values.astype(LOW)
    return high, (values - high.astype(jnp.float32)).astype(LOW)


def gelu_pair(v):
    square = v * v
    half = 0.5 * jnp.tanh(v * (GELU_A + GELU_B * square)) + 0.5
    out = v * half
    slope = half + out * (1.0 - half) * (2.0 * GELU_A + 6.0 * GELU_B * square)
    return out, slope


def norm_parts(values, width):
    centre = jnp.sum(values, axis=-1, keepdims=True) * (1.0 / width)
    centered = values - centre
    if values.shape[-1] != width:
        lane = lax.broadcasted_iota(jnp.int32, values.shape, 1)
        centered = jnp.where(lane < width, centered, 0.0)
    spread = jnp.sum(centered * centered, axis=-1, keepdims=True) * (1.0 / width)
    inverse = lax.rsqrt(spread + EPS_NORM)
    return centered * inverse, inverse


def norm_back(scaled, inverse, gain, upstream, width):
    inner = upstream * gain
    mean_inner = jnp.sum(inner, axis=-1, keepdims=True) * (1.0 / width)
    mean_cross = jnp.sum(inner * scaled, axis=-1, keepdims=True) * (1.0 / width)
    return inverse * (inner - mean_inner - scaled * mean_cross)


def whole(shape):
    return pl.BlockSpec(shape, lambda *_: (0,) * len(shape), pipeline_mode=pl.Buffered(1))


def anywhere(values):
    return [pl.BlockSpec(memory_space=pl.ANY)] * len(values)


def kept(shape):
    return pl.BlockSpec(shape, lambda *_: (0,) * len(shape))


def params(limit=58):
    return pltpu.CompilerParams(vmem_limit_bytes=limit * 2**20)


def shaped(shape, dtype):
    return jax.ShapeDtypeStruct(shape, dtype)


def trimmed(kernel, inputs, unread):
    def run(*refs):
        kernel(*refs[:inputs], *refs[inputs + unread :])

    return run


def target_columns(targets, nodes):
    down = lax.broadcasted_iota(jnp.int32, (nodes, targets.shape[1]), 0)
    return jnp.where(down == targets, 1.0, 0.0).astype(LOW)


def source_mask(block):
    row = lax.broadcasted_iota(jnp.int32, (WIDE - DE, block), 0)
    source = lax.broadcasted_iota(jnp.int32, (WIDE - DE, block), 1) // K
    return jnp.where((row == source) | (row == source + block // K), 1.0, 0.0)


def block_of():
    return 32 * K


def lanes(height, block):
    return pl.BlockSpec((height, block), lambda i: (0, i))


def tall_lanes(nodes, block):
    buffers = pl.Buffered(2 if nodes <= 1024 else 1)
    return pl.BlockSpec((nodes, block), lambda i: (0, i), pipeline_mode=buffers)


def source_rows(values):
    high = values.astype(LOW).astype(jnp.float32)
    return jnp.concatenate([high, values - high], axis=0).astype(LOW)


def put_halves(halves, total, owned):
    for index in range(total.shape[0] // owned):
        rows = total[index * owned : (index + 1) * owned].astype(LOW)
        halves[index % 2][index // 2, 0:owned, :] = rows


COUNT_ROWS = 16


def message_kernel(
    targets, edge, valid, w_rows, w_edge, x_all,
    even, odd, hidden_out, slope_one, slope_two, tall,
    table, mixed, from_source, total, mid, counts, wide,
):
    step = pl.program_id(0)
    owned = from_source.shape[0]

    @pl.when(step == 0)
    def _():
        table[...] = dot(x_all[...], w_rows[D : 2 * D]).astype(LOW).T
        from_source[...] = dot(x_all[0:owned], w_rows[0:D])
        mixed[0:DE] = w_edge[...]
        mid[...] = w_rows[2 * D : 3 * D].T
        wide[DE:WIDE] = source_mask(edge.shape[1]).astype(LOW)
        total[...] = jnp.zeros_like(total)
        counts[...] = jnp.zeros_like(counts)

    nodes, block = tall.shape
    group = block // K
    wide[0:DE] = edge[...]
    tall[...] = target_columns(targets[...], nodes)
    mixed[DE:WIDE] = source_rows(from_source[pl.ds(step * group, group), :])
    pre = dot(table[...], tall[...]) + dot_rows(mixed[...], wide[...])
    hidden, slope = gelu_pair(pre)
    hidden = hidden.astype(LOW)
    hidden_out[...] = hidden
    slope_one[...] = slope.astype(LOW)
    second, slope = gelu_pair(dot(mid[...], hidden))
    ok = jnp.sum(source_mask(block)[0:group] * valid[...], axis=0, keepdims=True)
    slope_two[...] = (slope * ok).astype(LOW)
    total[...] += dot_turned(tall[...], (second * ok).astype(LOW))
    ok_rows = jnp.broadcast_to(ok, (COUNT_ROWS, ok.shape[1])).astype(LOW)
    counts[...] += dot_turned(ok_rows, tall[...])

    @pl.when(step == pl.num_programs(0) - 1)
    def _():
        put_halves((even, odd), total, owned)
        for index in range(total.shape[0] // owned):
            amount = counts[:, index * owned : (index + 1) * owned]
            high = jnp.floor(amount * (1.0 / LANES))
            place = (even, odd)[index % 2].at[index // 2]
            rows = pl.ds(owned, COUNT_ROWS)
            place[rows, :] = jnp.zeros((COUNT_ROWS, D), LOW)
            place[rows, 0:owned] = high.astype(LOW)
            place[rows, LANES : LANES + owned] = (amount - high * LANES).astype(LOW)


def message_forward(targets, edge, valid, x_all, owned, w_rows, w_edge, after):
    nodes, rows = x_all.shape[0], targets.shape[1]
    block = block_of()
    half = (nodes // owned // 2, owned + COUNT_ROWS, D)
    return pl.pallas_call(
        trimmed(message_kernel, 6, len(after)),
        grid=(rows // block,),
        in_specs=[
            lanes(1, block),
            lanes(DE, block),
            pl.BlockSpec((block // K, 1), lambda i: (i, 0)),
            whole((3 * D, D)),
            whole((DE, D)),
            whole((nodes, D)),
        ]
        + anywhere(after),
        out_specs=[kept(half), kept(half)] + [lanes(D, block)] * 3 + [tall_lanes(nodes, block)],
        out_shape=[shaped(half, LOW)] * 2
        + [shaped((D, rows), LOW)] * 3
        + [shaped((nodes, rows), LOW)],
        scratch_shapes=[
            pltpu.VMEM((D, nodes), LOW),
            pltpu.VMEM((WIDE, D), LOW),
            pltpu.VMEM((owned, D), jnp.float32),
            pltpu.VMEM((nodes, D), jnp.float32),
            pltpu.VMEM((D, D), LOW),
            pltpu.VMEM((COUNT_ROWS, nodes), jnp.float32),
            pltpu.VMEM((WIDE, block), LOW),
        ],
        compiler_params=params(),
    )(targets, edge, valid, w_rows, w_edge, x_all, *after)


def up_part(blocks, part):
    per, parts = D // TILE, FF // D
    strips = [blocks[4 * per + row * parts + part] for row in range(per)]
    return jnp.concatenate(strips, axis=0)


def out_part(blocks):
    per = D // TILE
    return blocks[3 * per : 4 * per].reshape(D, D)


def down_part(blocks, part):
    per = D // TILE
    first = per * (4 + FF // D + part)
    return blocks[first : first + per].reshape(D, D)


def node_forward_kernel(x, valid, blocks, u_src, u_dst, norms, *refs):
    pieces = refs[:-10]
    (
        low_out, q_src, q_dst, inside_out, one_out, act_out, slope_out, summed_out, scale_out,
        sums_out,
    ) = refs[-10:]
    summed_all = sum(piece[...].astype(jnp.float32) for piece in pieces)
    owned = x.shape[0]
    sums = summed_all[0:owned]
    tally = summed_all[owned : owned + 8, 0:LANES] * float(LANES)
    tally += summed_all[owned : owned + 8, LANES : 2 * LANES]
    amount = tally.T[0:owned, 0:1]
    scale = valid[...] / jnp.maximum(amount * valid[...], 1.0)
    scale_out[...] = scale
    sums_out[...] = sums
    high, low = split_low(sums * scale)
    w_out = out_part(blocks)
    inside = x[...].astype(jnp.float32) + (dot(high, w_out) + dot(low, w_out))
    scaled, _ = norm_parts(inside, D)
    one = scaled * norms[0:1] + norms[1:2]
    one_low = one.astype(LOW)
    narrowed = jnp.zeros_like(one)
    for part in range(FF // D):
        act, slope = gelu_pair(dot(one_low, up_part(blocks, part)))
        act = act.astype(LOW)
        act_out[:, part * D : (part + 1) * D] = act
        slope_out[:, part * D : (part + 1) * D] = slope.astype(LOW)
        narrowed += dot(act, down_part(blocks, part))
    summed = one + narrowed
    scaled, _ = norm_parts(summed, D)
    two = (scaled * norms[2:3] + norms[3:4]).astype(LOW)
    low_out[...] = two
    q_src[...] = dot(two, u_src[...])
    q_dst[...] = dot(two, u_dst[...]).astype(LOW)
    inside_out[...] = inside
    one_out[...] = one
    summed_out[...] = summed


def node_forward(x, valid, blocks, u_src, u_dst, norms, pieces, after):
    owned = x.shape[0]
    wide = shaped((owned, D), jnp.float32)
    operands = [x, valid, blocks, u_src, u_dst, norms, *pieces]
    return pl.pallas_call(
        trimmed(node_forward_kernel, len(operands), len(after)),
        in_specs=[pl.BlockSpec(memory_space=pltpu.VMEM)] * len(operands) + anywhere(after),
        out_shape=[
            shaped((owned, D), LOW),
            shaped((owned, WIDE), jnp.float32),
            shaped((owned, WIDE), LOW),
            wide,
            wide,
            shaped((owned, FF), LOW),
            shaped((owned, FF), LOW),
            wide,
            shaped((owned, 1), jnp.float32),
            wide,
        ],
        compiler_params=params(),
    )(*operands, *after)


def tall_norm(values):
    width = values.shape[0]
    centre = jnp.sum(values, axis=0, keepdims=True) * (1.0 / width)
    centered = values - centre
    spread = jnp.sum(centered * centered, axis=0, keepdims=True) * (1.0 / width)
    inverse = lax.rsqrt(spread + EPS_NORM)
    return centered * inverse, inverse


def tall_norm_back(scaled, inverse, gain, upstream):
    width = scaled.shape[0]
    inner = upstream * gain
    mean_inner = jnp.sum(inner, axis=0, keepdims=True) * (1.0 / width)
    mean_cross = jnp.sum(inner * scaled, axis=0, keepdims=True) * (1.0 / width)
    return inverse * (inner - mean_inner - scaled * mean_cross)


def lane_sums(values):
    return sum(
        values[:, first : first + LANES] for first in range(0, values.shape[1], LANES)
    )


def edge_kernel(count, tall, edge, cot, q_src, u_edge, u_mid, u_out, norms, *refs):
    pieces = refs[0:count]
    (
        edge_out, d_edge, even, odd, d_source, g_edge, g_mid, g_out, g_norms,
        table, mixed, total, mid_turned, out_turned, gain_sum, shift_sum, columns, wide,
    ) = refs[-18:]
    step = pl.program_id(0)
    last = pl.num_programs(0) - 1
    owned = q_src.shape[0]

    @pl.when(step == 0)
    def _():
        table[...] = jnp.concatenate([piece[...] for piece in pieces], axis=0).T
        mixed[0:DE] = u_edge[...]
        mid_turned[...] = u_mid[...].T
        out_turned[...] = u_out[...].T
        columns[...] = norms[...].T
        wide[DE:WIDE] = source_mask(edge.shape[1]).astype(LOW)
        for ref in (total, gain_sum, shift_sum, g_edge, g_mid, g_out):
            ref[...] = jnp.zeros_like(ref)

    group = edge_out.shape[1] // K
    mixed[DE:WIDE] = source_rows(q_src[pl.ds(step * group, group), :])
    wide[0:DE] = edge[...]
    both = wide[...]
    first, slope_one = gelu_pair(
        dot(table[0:DE], tall[...]) + dot(mixed[...].T[0:DE], both)
    )
    first = first.astype(LOW)
    second, slope_two = gelu_pair(dot(mid_turned[0:DE, 0:DE], first))
    second = second.astype(LOW)
    change = dot(out_turned[0:DE, 0:DE], second)
    scaled, inverse = tall_norm(both[0:DE].astype(jnp.float32) + change)
    gain, offset = columns[0:DE, 0:1], columns[0:DE, 1:2]
    edge_out[...] = (scaled * gain + offset).astype(LOW)
    back = cot[...].astype(jnp.float32)
    gain_sum[...] += lane_sums(back * scaled)
    shift_sum[...] += lane_sums(back)
    d_sum = tall_norm_back(scaled, inverse, gain, back)
    d_change = d_sum.astype(LOW)
    g_out[0:DE, 0:DE] += dot_turned(second, d_change)
    d_second = (dot(u_out[:, 0:DE], d_change) * slope_two).astype(LOW)
    g_mid[0:DE, 0:DE] += dot_turned(first, d_second)
    d_first = (dot(u_mid[:, 0:DE], d_second) * slope_one).astype(LOW)
    d_edge[...] = d_sum + dot(u_edge[:, 0:DE], d_first)
    turned = dot_turned(both, d_first)
    g_edge[:, 0:DE] += turned[0:DE]
    d_source[pl.ds(step * group, group), :] = turned[DE : DE + group]
    total[:, 0:DE] += dot_turned(tall[...], d_first)

    @pl.when(step == last)
    def _():
        put_halves((even, odd), total, owned)
        gain_row = jnp.sum(gain_sum[...].T, axis=0, keepdims=True)
        shift_row = jnp.sum(shift_sum[...].T, axis=0, keepdims=True)
        both_rows = jnp.concatenate([gain_row, shift_row], axis=1)
        g_norms[...] = jnp.zeros_like(g_norms)
        for index in range(3):
            g_norms[index : index + 1] = both_rows[:, index * LANES : (index + 1) * LANES]


def edge_phase(tall, edge, cot, pieces, q_src, u_edge, u_mid, u_out, norms, after):
    nodes, rows = tall.shape
    owned = q_src.shape[0]
    block = block_of()
    count = len(pieces)
    half = (count // 2, owned, WIDE)
    square = shaped((DE, WIDE), jnp.float32)
    line = shaped((8, LANES), jnp.float32)
    return pl.pallas_call(
        functools.partial(edge_kernel, count),
        grid=(rows // block,),
        in_specs=[
            tall_lanes(nodes, block),
            lanes(DE, block),
            lanes(DE, block),
            whole((owned, WIDE)),
            whole((DE, WIDE)),
            whole((DE, WIDE)),
            whole((DE, WIDE)),
            whole((8, WIDE)),
        ]
        + [whole((owned, WIDE))] * count
        + anywhere(after),
        out_specs=[
            lanes(DE, block),
            lanes(DE, block),
            kept(half),
            kept(half),
            kept((owned, DE)),
            kept((DE, WIDE)),
            kept((DE, WIDE)),
            kept((DE, WIDE)),
            kept((8, LANES)),
        ],
        out_shape=[
            shaped((DE, rows), LOW),
            shaped((DE, rows), jnp.float32),
            shaped(half, LOW),
            shaped(half, LOW),
            shaped((owned, DE), jnp.float32),
            square,
            square,
            square,
            line,
        ],
        scratch_shapes=[
            pltpu.VMEM((WIDE, nodes), LOW),
            pltpu.VMEM((WIDE, WIDE), LOW),
            pltpu.VMEM((nodes, WIDE), jnp.float32),
            pltpu.VMEM((WIDE, DE), LOW),
            pltpu.VMEM((WIDE, DE), LOW),
            pltpu.VMEM((DE, LANES), jnp.float32),
            pltpu.VMEM((DE, LANES), jnp.float32),
            pltpu.VMEM((WIDE, 8), jnp.float32),
            pltpu.VMEM((WIDE, block), LOW),
        ],
        compiler_params=params(),
    )(tall, edge, cot, q_src, u_edge, u_mid, u_out, norms, *pieces, *after)


def put_blocks(ref, base, matrix, step=1):
    for row in range(matrix.shape[0] // TILE):
        strip = matrix[row * TILE : (row + 1) * TILE].astype(ref.dtype)
        owner, batch, slot = early_place(base + row * step)
        for part in range(4):
            ref[owner, batch, part, slot * TILE : (slot + 1) * TILE, :] = strip[
                :, part * LANES : (part + 1) * LANES
            ]


def put_sides(refs, core, stores):
    for own in range(2):

        @pl.when(core == own)
        def _():
            for side, value, index in stores:
                refs[side ^ own][index] = value


def small_stores(batch, begin, matrix):
    stores = []
    piece = EARLY_ROWS // 8
    end = begin + matrix.shape[0]
    first = begin
    while first < end:
        index, offset = first // piece, first % piece
        amount = min(end - first, piece - offset)
        value = matrix[first - begin : first - begin + amount].astype(LOW)
        place = (index % 4 ^ batch, slice(offset, offset + amount), slice(None))
        stores.append((index // 4, value, place))
        first += amount
    return stores


def put_norm(ref, index, values):
    total = jnp.sum(values, axis=0, keepdims=True)
    for part in range(4):
        row = index * 4 + part
        ref[row : row + 1, 0:LANES] = total[:, part * LANES : (part + 1) * LANES]


def early_place(block):
    batch, rest = block // 24, block % 24
    return rest // 3, batch, rest % 3


def node_backward_kernel(
    place, cot, d_q_src, low, summed, one, inside, act, slope, scale, sums,
    blocks, u_src, u_dst, norms, g_edge, g_mid, g_out, g_edge_norms, *refs,
):
    reply, d_inside_out, g_blocks, g_even, g_odd, g_norms = refs[-6:]
    pieces = refs[:-6]
    core, batch = place[1], place[2]
    stores = []
    d_src = d_q_src[...].astype(LOW)
    d_dst = sum(piece[...].astype(jnp.float32) for piece in pieces).astype(LOW)
    low_now = low[...]
    blank = jnp.zeros((D, WIDE - DE), jnp.float32)
    stores += small_stores(batch, 0, jnp.concatenate([dot_rows(low_now, d_src), blank], axis=1))
    stores += small_stores(batch, D, dot_rows(low_now, d_dst))
    for index, ref in enumerate((g_edge, g_mid, g_out)):
        stores += small_stores(batch, 2 * D + index * DE, ref[...])
    g_norms[...] = jnp.zeros_like(g_norms)
    g_norms[16:24, 0:LANES] = g_edge_norms[...]
    d_final = (
        cot[...].astype(jnp.float32)
        + dot_turned(d_src, u_src[:, 0:DE])
        + dot_turned(d_dst, u_dst[...])
    )
    scaled, inverse = norm_parts(summed[...], D)
    d_summed = norm_back(scaled, inverse, norms[2:3], d_final, D)
    put_norm(g_norms, 2, d_final * scaled)
    put_norm(g_norms, 3, d_final)
    d_narrow = d_summed.astype(LOW)
    one_low = one[...].astype(LOW)
    d_one = d_summed
    first_up = D // TILE
    parts = FF // D
    first_down = first_up + first_up * parts
    for part in range(parts):
        cols = slice(part * D, (part + 1) * D)
        put_blocks(g_blocks, first_down + part * first_up, dot_rows(act[:, cols], d_narrow))
        d_wide = (
            dot_turned(d_narrow, down_part(blocks, part)) * slope[:, cols].astype(jnp.float32)
        ).astype(LOW)
        put_blocks(g_blocks, first_up + part, dot_rows(one_low, d_wide), parts)
        d_one += dot_turned(d_wide, up_part(blocks, part))
    scaled, inverse = norm_parts(inside[...], D)
    d_inside = norm_back(scaled, inverse, norms[0:1], d_one, D)
    put_norm(g_norms, 0, d_one * scaled)
    put_norm(g_norms, 1, d_one)
    d_inside_out[...] = d_inside
    per_target = (d_inside * scale[...]).astype(LOW)
    high, rest = split_low(sums[...])
    put_blocks(g_blocks, 0, dot_rows(high, per_target) + dot_rows(rest, per_target))
    reply[...] = dot_turned(per_target, out_part(blocks)).astype(LOW)
    stores += small_stores(batch, 2 * D + 3 * DE, g_norms[...])
    put_sides((g_even, g_odd), core, stores)


def node_backward(place, operands, pieces, after):
    owned = operands[0].shape[0]
    half = shaped((4, EARLY_ROWS // 8, WIDE), LOW)
    amount = len(operands) + len(pieces)
    return pl.pallas_call(
        trimmed(node_backward_kernel, amount + 1, len(after)),
        in_specs=[pl.BlockSpec(memory_space=pltpu.SMEM)]
        + [pl.BlockSpec(memory_space=pltpu.VMEM)] * amount
        + anywhere(after),
        out_shape=[
            shaped((owned, D), LOW),
            shaped((owned, D), jnp.float32),
            shaped((8, 3, 4, OWNED_ROWS, LANES), LOW),
            half,
            half,
        ],
        scratch_shapes=[pltpu.VMEM((TILE, WIDE), jnp.float32)],
        compiler_params=params(),
    )(place, *operands, *pieces, *after)


def message_back_kernel(
    count, place, tall, edge, hidden, slope_one, slope_two, part_edge, x_all, w_mid, w_edge, *refs
):
    pieces = refs[0:count]
    (
        d_edge, even, odd, d_source, late_even, late_odd, table, total, g_mid, g_edge, from_source, wide,
    ) = refs[-12:]
    step = pl.program_id(0)
    owned = d_source.shape[0]

    @pl.when(step == 0)
    def _():
        table[...] = jnp.concatenate([piece[...] for piece in pieces], axis=0).T
        wide[DE:WIDE] = source_mask(edge.shape[1]).astype(LOW)
        total[...] = jnp.zeros_like(total)
        g_mid[...] = jnp.zeros_like(g_mid)
        g_edge[...] = jnp.zeros_like(g_edge)

    wide[0:DE] = edge[...]
    d_hidden = dot(table[...], tall[...])
    d_second = (d_hidden * slope_two[...].astype(jnp.float32)).astype(LOW)
    g_mid[...] += dot_turned(hidden[...], d_second)
    d_pre = (dot(w_mid[...], d_second) * slope_one[...].astype(jnp.float32)).astype(LOW)
    d_edge[...] = part_edge[...] + dot(w_edge[...], d_pre)
    turned = dot_turned(wide[...], d_pre)
    g_edge[...] += turned[0:DE]
    group = hidden.shape[1] // K
    from_source[pl.ds(step * group, group), :] = turned[DE : DE + group]
    total[...] += dot_turned(tall[...], d_pre)

    @pl.when(step == pl.num_programs(0) - 1)
    def _():
        put_halves((even, odd), total, owned)
        gathered = x_all[...]
        sources_low = from_source[...].astype(LOW)
        d_source[...] = sources_low
        chip, core, batch = place[0], place[1], place[2]
        matrices = (
            dot_rows(gathered[0:owned], sources_low),
            dot_rows(gathered, total[...].astype(LOW)),
            g_mid[...],
        )
        stores = []
        for row in range(3 * (D // TILE)):
            owner, slot = row // 3, row % 3
            strip = matrices[row // (D // TILE)][row % (D // TILE) * TILE :][0:TILE].astype(LOW)
            first = pl.multiple_of((owner // 2 ^ chip) * OWNED_ROWS + slot * TILE, TILE)
            for part in range(4):
                value = strip[:, part * LANES : (part + 1) * LANES]
                stores.append((owner % 2, value, (part ^ batch, pl.ds(first, TILE), slice(None))))
        half = DE // 2
        for side in range(2):
            strip = g_edge[side * half : (side + 1) * half].astype(LOW)
            for part in range(4):
                value = strip[:, part * LANES : (part + 1) * LANES]
                rows = slice(4 * OWNED_ROWS, 4 * OWNED_ROWS + half)
                stores.append((side, value, (part ^ batch, rows, slice(None))))
        put_sides((late_even, late_odd), core, stores)


def message_backward(
    place, tall, edge, hidden, slope_one, slope_two, part_edge, x_all, w_rows, w_edge, pieces, after
):
    nodes, rows = tall.shape
    owned = pieces[0].shape[0]
    block = block_of()
    count = len(pieces)
    half = (count // 2, owned, D)
    feature = tall_lanes(D, block) if nodes <= 1024 else pl.BlockSpec(
        (D, block), lambda i: (0, i), pipeline_mode=pl.Buffered(1)
    )
    late = (4, 4 * OWNED_ROWS + DE // 2, LANES)
    return pl.pallas_call(
        functools.partial(message_back_kernel, count),
        grid=(rows // block,),
        in_specs=[
            pl.BlockSpec(memory_space=pltpu.SMEM),
            tall_lanes(nodes, block),
            lanes(DE, block),
            feature,
            feature,
            feature,
            lanes(DE, block),
            whole((nodes, D)),
            pl.BlockSpec((D, D), lambda i: (2, 0), pipeline_mode=pl.Buffered(1)),
            whole((DE, D)),
        ]
        + [whole((owned, D))] * count
        + anywhere(after),
        out_specs=[
            lanes(DE, block),
            kept(half),
            kept(half),
            kept((owned, D)),
            kept(late),
            kept(late),
        ],
        out_shape=[
            shaped((DE, rows), jnp.float32),
            shaped(half, LOW),
            shaped(half, LOW),
            shaped((owned, D), LOW),
            shaped(late, LOW),
            shaped(late, LOW),
        ],
        scratch_shapes=[
            pltpu.VMEM((D, nodes), LOW),
            pltpu.VMEM((nodes, D), jnp.float32),
            pltpu.VMEM((D, D), jnp.float32),
            pltpu.VMEM((DE, D), jnp.float32),
            pltpu.VMEM((owned, D), jnp.float32),
            pltpu.VMEM((WIDE, block), LOW),
        ],
        compiler_params=params(),
    )(
        place, tall, edge, hidden, slope_one, slope_two, part_edge, x_all, w_rows, w_edge,
        *pieces, *after,
    )


def node_gradient_kernel(inside, d_source, w_rows, *refs):
    pieces, out = refs[:-1], refs[-1]
    d_target = sum(piece[...].astype(jnp.float32) for piece in pieces).astype(LOW)
    out[...] = (
        inside[...]
        + dot_turned(d_source[...], w_rows[0:D])
        + dot_turned(d_target, w_rows[D : 2 * D])
    )


def node_gradient(inside, d_source, w_rows, pieces):
    return pl.pallas_call(
        node_gradient_kernel,
        out_shape=shaped(inside.shape, jnp.float32),
        compiler_params=params(),
    )(inside, d_source, w_rows, *pieces)


def add_halves_kernel(left, right, *outs):
    for index, out in enumerate(outs):
        total = left[index].astype(jnp.float32) + right[index].astype(jnp.float32)
        out[...] = total.astype(out.dtype)


def add_halves(left, right):
    shape = left.shape[1:]
    return pl.pallas_call(
        add_halves_kernel,
        out_shape=[shaped(shape, jnp.float32)] + [shaped(shape, LOW)] * (left.shape[0] - 1),
        compiler_params=params(8),
    )(left, right)


def assemble_kernel(count, place, *refs):
    lines, pieces, rows, x_all = refs[0:8], refs[8:-2], refs[-2], refs[-1]
    chip, core, batch = place[0], place[1], place[2]
    owned = pieces[0].shape[0]
    for index, piece in enumerate(lines):
        side, part = index // 4, index % 4
        for line in range(4):
            row = ((line ^ chip) * 2 + (side ^ core)) * OWNED_ROWS
            lane = (part ^ batch) * LANES
            rows[
                pl.ds(pl.multiple_of(row, TILE), OWNED_ROWS),
                pl.ds(pl.multiple_of(lane, LANES), LANES),
            ] = piece[line]
    for index, piece in enumerate(pieces):
        x_all[index * owned : (index + 1) * owned] = piece[...]


def assemble(place, lines, pieces):
    owned = pieces[0].shape[0]
    amount = len(lines) + len(pieces)
    return pl.pallas_call(
        functools.partial(assemble_kernel, len(pieces)),
        in_specs=[pl.BlockSpec(memory_space=pltpu.SMEM)]
        + [pl.BlockSpec(memory_space=pltpu.VMEM)] * amount,
        out_shape=[shaped((3 * D, D), LOW), shaped((8 * owned, D), LOW)],
        compiler_params=params(),
    )(place, *lines, *pieces)


def own_rows_kernel(tiles, rows, *refs):
    quarters, (flat, pair) = refs[0:4], refs[4:]
    load_flat(tiles, flat)
    for index, group in enumerate(group_list(0, 24, 4)):
        block, side = index // 2, index % 2
        value = group_in(flat, pair, group).astype(LOW)
        rows[block * TILE : (block + 1) * TILE, side * QUAD : (side + 1) * QUAD] = value
        for half in range(2):
            quarters[2 * side + half][block * TILE : (block + 1) * TILE, :] = value[
                :, half * LANES : (half + 1) * LANES
            ]


def own_rows(tiles):
    return pl.pallas_call(
        own_rows_kernel,
        out_shape=[
            shaped((OWNED_ROWS, D), LOW),
        ] + [shaped((OWNED_ROWS, LANES), LOW)] * 4 + [
        ],
        scratch_shapes=[
            pltpu.VMEM((flat_rows(24), LANES), jnp.float32),
            pltpu.VMEM((TILE, LANES), jnp.float32),
        ],
        compiler_params=params(),
    )(tiles)


LANES = 128
QUAD = 4 * TILE
FLAT = TILE * TILE // LANES


def group_list(first, last, size):
    return [list(range(t, min(t + size, last))) for t in range(first, last, size)]


def load_flat(ref, flat):
    amount = ref.shape[0]
    for top in range(0, amount, 8):
        rows = min(8, amount - top)
        for part in range(FLAT):
            flat[pl.ds(top * FLAT + 8 * part, rows), :] = ref[
                top : top + rows, part * LANES : (part + 1) * LANES
            ]


def store_flat(ref, flat, first=0, last=None):
    last = ref.shape[0] if last is None else last
    while first < last:
        rows = min(8 - first % 8, last - first)
        top = first // 8 * 8
        for part in range(FLAT):
            ref[first : first + rows, part * LANES : (part + 1) * LANES] = flat[
                pl.ds(top * FLAT + 8 * part + first - top, rows), :
            ]
        first += rows


def tile_rows(tile):
    return pl.ds(tile // 8 * 8 * FLAT + tile % 8, FLAT, stride=8)


def lower_half(shape):
    return lax.broadcasted_iota(jnp.int32, shape, 1) < TILE


def group_in(flat, pair, tiles):
    left = lower_half((FLAT, LANES))
    halves = []
    for first in range(0, 4, 2):
        here = tiles[first : first + 2]
        one = flat[tile_rows(here[0]), :] if here else jnp.zeros((FLAT, LANES), jnp.float32)
        two = flat[tile_rows(here[1]), :] if len(here) > 1 else jnp.zeros_like(one)
        pair[pl.ds(0, FLAT, stride=2), :] = jnp.where(left, one, pltpu.roll(two, TILE, 1))
        pair[pl.ds(1, FLAT, stride=2), :] = jnp.where(left, pltpu.roll(one, TILE, 1), two)
        halves.append(pair[...])
    return jnp.concatenate(halves, axis=1)


def group_out(value, flat, pair, tiles):
    left = lower_half((FLAT, LANES))
    for first in range(0, 4, 2):
        here = tiles[first : first + 2]
        if not here:
            continue
        pair[...] = value[:, first * TILE : first * TILE + LANES]
        even = pair[pl.ds(0, FLAT, stride=2), :]
        odd = pair[pl.ds(1, FLAT, stride=2), :]
        flat[tile_rows(here[0]), :] = jnp.where(left, even, pltpu.roll(odd, TILE, 1))
        if len(here) > 1:
            flat[tile_rows(here[1]), :] = jnp.where(left, pltpu.roll(even, TILE, 1), odd)


def flat_rows(amount):
    return -(-amount // 8) * 8 * FLAT


SPAN_GROUPS = 8


def regroup_small_kernel(count, *refs):
    tiles, outs = refs[0:count], refs[count : 2 * count]
    flat, pair = refs[-2:]
    step = pl.program_id(0)
    for condition, amount, size, spot in (
        (step == 0, 24, 4, 0),
        ((step > 0) & (step < 4), 24, 3, 0),
        (step == 4, 3, 3, 0),
    ):

        @pl.when(condition)
        def _():
            for ref, out in zip(tiles, outs):
                load_flat(ref, flat)
                for index, group in enumerate(group_list(0, amount, size)):
                    out[spot + index] = group_in(flat, pair, group)


def regroup_small(arrays, after=()):
    count = len(arrays)
    shape = (5 * SPAN_GROUPS, TILE, QUAD)
    out_spec = pl.BlockSpec((SPAN_GROUPS, TILE, QUAD), lambda i: (i, 0, 0))
    return pl.pallas_call(
        trimmed(functools.partial(regroup_small_kernel, count), count, len(after)),
        grid=(5,),
        in_specs=[pl.BlockSpec((24, TILE * TILE), lambda i: (i, 0))] * count + anywhere(after),
        out_specs=[out_spec] * count,
        out_shape=[shaped(shape, jnp.float32)] * count,
        scratch_shapes=[
            pltpu.VMEM((flat_rows(24), LANES), jnp.float32),
            pltpu.VMEM((TILE, LANES), jnp.float32),
        ],
        compiler_params=params(),
    )(*arrays, *after)


def regroup_weights_kernel(tiles, out, w_edge, e_src, e_dst, e_edge, e_mid, e_out, flat, pair):
    regroup_small_kernel(1, tiles, out, flat, pair)
    step = pl.program_id(0)

    @pl.when(step == 0)
    def _():
        for index in range(6):
            block, side = index // 2, index % 2
            w_edge[block * TILE : (block + 1) * TILE, side * QUAD : (side + 1) * QUAD] = out[
                index
            ].astype(LOW)

    for condition, ref, first, amount, start in (
        (step == 1, e_src, 0, 8, 0), (step == 2, e_dst, 0, 8, 0), (step == 3, e_edge, 0, 3, 0),
        (step == 3, e_mid, 3, 3, 0), (step == 3, e_out, 6, 2, 0), (step == 4, e_out, 0, 1, 2),
    ):

        @pl.when(condition)
        def _():
            for index in range(amount):
                here = slice((start + index) * TILE, (start + index + 1) * TILE)
                ref[here] = out[first + index].astype(LOW)


def regroup_weights(weights):
    shapes = [(DE, D), (D, WIDE), (D, WIDE)] + [(DE, WIDE)] * 3
    return pl.pallas_call(
        regroup_weights_kernel,
        grid=(5,),
        in_specs=[pl.BlockSpec((24, TILE * TILE), lambda i: (i, 0))],
        out_specs=[pl.BlockSpec((SPAN_GROUPS, TILE, QUAD), lambda i: (i, 0, 0))]
        + [kept(shape) for shape in shapes],
        out_shape=[shaped((5 * SPAN_GROUPS, TILE, QUAD), jnp.float32)]
        + [shaped(shape, LOW) for shape in shapes],
        scratch_shapes=[
            pltpu.VMEM((flat_rows(24), LANES), jnp.float32),
            pltpu.VMEM((TILE, LANES), jnp.float32),
        ],
        compiler_params=params(),
    )(weights)


def regroup_big_kernel(count, *refs):
    tiles, outs = refs[0:count], refs[count : 2 * count]
    flat, pair = refs[-2:]
    for ref, out in zip(tiles, outs):
        load_flat(ref, flat)
        for index, group in enumerate(group_list(0, 24, 4)):
            out[index] = group_in(flat, pair, group)


def regroup_big(arrays, after=()):
    count = len(arrays)
    return pl.pallas_call(
        trimmed(functools.partial(regroup_big_kernel, count), count, len(after)),
        in_specs=[pl.BlockSpec(memory_space=pltpu.VMEM)] * count + anywhere(after),
        out_shape=[shaped((6, TILE, QUAD), jnp.float32)] * count,
        scratch_shapes=[
            pltpu.VMEM((flat_rows(24), LANES), jnp.float32),
            pltpu.VMEM((TILE, LANES), jnp.float32),
        ],
        compiler_params=params(),
    )(*arrays, *after)


def soap_groups(grads, weights, firsts, seconds, lefts, rights, rates):
    count = range(len(grads))
    lane = lax.broadcasted_iota(jnp.int32, (TILE, QUAD), 1) // TILE
    masks = [jnp.where(lane == k, 1.0, 0.0) for k in range(4)]
    low_masks = [mask.astype(LOW) for mask in masks]

    def diagonal(values):
        return jnp.concatenate([values * mask for mask in low_masks], axis=0)

    def thrice(product_of, values, sides):
        parts = [split_low(v) for v in values]
        both = [product_of(jnp.concatenate(parts[i], axis=0), sides[i][0]) for i in count]
        rest = [product_of(parts[i][0], sides[i][1]) for i in count]
        return [both[i][0:TILE] + both[i][TILE:] + rest[i] for i in count]

    right_sides = [[diagonal(part) for part in split_low(v)] for v in rights]
    left_parts = [split_low(v) for v in lefts]
    left_sides = [jnp.concatenate([high, low, high], axis=0) for high, low in left_parts]
    half = [split_low(v) for v in thrice(dot, grads, right_sides)]
    half = [jnp.concatenate([high, high, low], axis=0) for high, low in half]
    full = [dot_rows(left_sides[i], half[i]) for i in count]
    turned = [sum(v[TILE * k : TILE * (k + 1)] * masks[k] for k in range(4)) for v in full]
    new_one = [BETA_ONE * firsts[i] + (1.0 - BETA_ONE) * turned[i] for i in count]
    new_two = [
        BETA_TWO * seconds[i] + (1.0 - BETA_TWO) * turned[i] * turned[i] for i in count
    ]
    fix_one = 1.0 / (1.0 - BETA_ONE**STEP)
    fix_two = 1.0 / (1.0 - BETA_TWO**STEP)
    steps = [
        new_one[i] * fix_one / (jnp.sqrt(new_two[i] * fix_two) + EPS_ADAM) for i in count
    ]
    sides = [diagonal(v.astype(LOW)) for v in steps]
    half = [dot(left_parts[i][0], sides[i]).astype(LOW) for i in count]
    restored = [dot_turned(half[i], right_sides[i][0]) for i in count]
    new = [
        weights[i] - rates[i] * (restored[i] + DECAY * weights[i]) for i in count
    ]
    return new_one, new_two, new


TOGETHER = 5
EARLY_ROWS = 1664


def block_rate(block):
    middle = (2 * D + DE) ** (-0.5)
    return jnp.where(
        block < 16,
        middle,
        jnp.where(
            block < 24,
            D ** (-0.5),
            jnp.where(block < 32, 2.5 * D ** (-0.5), jnp.where(block < 64, D ** (-0.5), FF ** (-0.5))),
        ),
    )


def small_rates():
    middle = (2 * D + DE) ** (-0.5)
    return [middle] * 19 + [DE ** (-0.5)] * 3 + [1.5 * DE ** (-0.5)] * 3


NORM_ROWS = 19


def soap_early_kernel(scale, place, grads, rates, weight, first, second, left, right, *refs):
    norms, outs = refs[0:3], refs[3:9]
    flats, pairs = refs[9:12], refs[12]
    step = pl.program_id(0)
    core, batch = place[1], place[2]
    piece = EARLY_ROWS // 8

    def rows_of(begin, end):
        parts = []
        while begin < end:
            index, offset = begin // piece, begin % piece
            amount = min(end - begin, piece - offset)
            parts.append(grads[index // 4 ^ core, index % 4 ^ batch, offset : offset + amount, :])
            begin += amount
        value = parts[0] if len(parts) == 1 else jnp.concatenate(parts, axis=0)
        return value.astype(jnp.float32) * scale

    def groups(start, amount):
        here = range(amount)
        state = [[ref[i] for i in here] for ref in (weight, first, second, left, right)]
        results = soap_groups(
            [rows_of((start + i) * TILE, (start + i + 1) * TILE) for i in here],
            *state,
            [rates[start + i : start + i + 1] for i in here],
        )
        for spot in here:
            tiles = list(range(spot * 3, spot * 3 + 3))
            for kind, flat in enumerate(flats):
                group_out(results[kind][spot], flat, pairs.at[kind * SPAN_GROUPS + spot], tiles)

    for index, amount in enumerate((8, 8, 8, 1)):

        @pl.when(step == index)
        def _():
            groups(8 * index, amount)

    @pl.when(step == 0)
    def _():
        rows = rows_of(25 * TILE, 25 * TILE + 32)[0:NORM_ROWS, 0:LANES]
        results = adam_step(*(ref[...] for ref in norms), rows)
        for ref, value in zip(outs[3:6], (results[2], results[0], results[1])):
            ref[...] = value

    for ref, flat in zip(outs[0:3], flats):
        store_flat(ref, flat)


def soap_early(scale, place, grads, state, norms):
    out = shaped((99, TILE * TILE), jnp.float32)
    line = shaped((NORM_ROWS, LANES), jnp.float32)
    rates = jnp.asarray(np.repeat(np.array(small_rates(), np.float32)[:, None], QUAD, axis=1))
    return pl.pallas_call(
        functools.partial(soap_early_kernel, scale),
        grid=(4,),
        in_specs=[pl.BlockSpec(memory_space=pltpu.SMEM), whole(grads.shape), whole(rates.shape)]
        + [pl.BlockSpec((SPAN_GROUPS, TILE, QUAD), lambda i: (1 + i, 0, 0))] * 5
        + [whole(line.shape)] * 3,
        out_specs=[pl.BlockSpec((24, TILE * TILE), lambda i: (1 + i, 0))] * 3
        + [kept(line.shape)] * 3,
        out_shape=[out, out, out, line, line, line],
        scratch_shapes=[pltpu.VMEM((flat_rows(24), LANES), jnp.float32)] * 3
        + [pltpu.VMEM((3 * SPAN_GROUPS, TILE, LANES), jnp.float32)],
        compiler_params=params(),
    )(place, grads, rates, *state, *norms)


def soap_late_kernel(scale, place, own, other_one, other_two, other_three, *refs):
    state, v_state = refs[0:5], refs[5:10]
    older = refs[12]
    one, two, new, low, v_one, v_two, v_new, v_low = refs[13:21]
    flats, v_flats, pairs, shared_of = refs[21:24], refs[24:27], refs[27], refs[28]
    chip, core, batch = place[0], place[1], place[2]
    groups = group_list(0, 24, 4)
    received = (own, other_one, other_two, other_three)
    for shift, ref in enumerate(received):
        shared_of[shift, 4 * OWNED_ROWS :, :] = ref[4 * OWNED_ROWS :, :]

    def v_block(block, side):
        parts = []
        for part in (2 * side, 2 * side + 1):
            rows = []
            for begin in range(block * TILE, (block + 1) * TILE, TILE // 2):
                half, offset = begin // (DE // 2), begin % (DE // 2)
                first = 4 * OWNED_ROWS + (half ^ core) * (DE // 2) + offset
                rows.append(shared_of[part ^ batch, pl.ds(pl.multiple_of(first, 32), TILE // 2), :])
            parts.append(jnp.concatenate(rows, axis=0))
        return jnp.concatenate(parts, axis=1).astype(jnp.float32)

    def own_part(block, part):
        rows = slice(block * TILE, (block + 1) * TILE)
        shifted = slice(part * OWNED_ROWS + rows.start, part * OWNED_ROWS + rows.stop)
        total = tree_sum([ref[shifted, :].astype(jnp.float32) for ref in received])
        return jnp.where(batch == 0, received[part][rows, :].astype(jnp.float32), total)

    def own_block(block, side):
        return jnp.concatenate([own_part(block, 2 * side), own_part(block, 2 * side + 1)], axis=1)

    first = batch * 24 + (chip * 2 + core) * 3
    own_rates = [block_rate(first + i // 2) for i in range(6)]
    v_rates = [(2 * D + DE) ** (-0.5)] * 6
    for grad_of, values, rates, targets, base in (
        (own_block, state, own_rates, flats, 0),
        (v_block, v_state, v_rates, v_flats, 18),
    ):
        here = range(6)
        grads = [grad_of(i // 2, i % 2) * scale for i in here]
        results = soap_groups(grads, *[[ref[i] for i in here] for ref in values], rates)
        for index in here:
            for kind, flat in enumerate(targets):
                group_out(results[kind][index], flat, pairs.at[base + kind * 6 + index], groups[index])
    for ref, flat in zip((one, two, new, v_one, v_two, v_new), (*flats, *v_flats)):
        store_flat(ref, flat)
    low[...] = new[...].astype(LOW)
    v_low[...] = jnp.concatenate([v_new[...], older[24:]], axis=0).astype(LOW)


def soap_late(scale, place, received, state, v_state, early):
    out = shaped((24, TILE * TILE), jnp.float32)
    small = shaped(early[0].shape, jnp.float32)
    front = pl.BlockSpec((24, TILE * TILE), lambda i: (0, 0))
    group = whole((6, TILE, QUAD))
    flat = pltpu.VMEM((flat_rows(24), LANES), jnp.float32)
    return pl.pallas_call(
        functools.partial(soap_late_kernel, scale),
        grid=(1,),
        in_specs=[
            pl.BlockSpec(memory_space=pltpu.SMEM),
        ]
        + [whole(v.shape) for v in received]
        + [group] * 10
        + [pl.BlockSpec(memory_space=pl.ANY)] * 2
        + [whole(small.shape)],
        out_specs=[front] * 7 + [whole(small.shape)],
        out_shape=[out, out, out, shaped((24, TILE * TILE), LOW), small, small, small]
        + [shaped(small.shape, LOW)],
        scratch_shapes=[flat] * 6
        + [pltpu.VMEM((36, TILE, LANES), jnp.float32), pltpu.VMEM((4, *received[0].shape), LOW)],
        input_output_aliases={15: 4, 16: 5, 17: 6},
        compiler_params=params(),
    )(place, *received, *state, *v_state, *early)


def swap_core(values):
    return lax.ppermute(values, "core", [(0, 1), (1, 0)])


def swap_chip(values, shift):
    chips = lax.axis_size("chip")
    return lax.ppermute(values, "chip", [(i, i ^ shift) for i in range(chips)])


def gate(values, others):
    return lax.optimization_barrier((values, others))[0]


def send_pieces(values):
    chips = lax.axis_size("chip")
    return [values] + [swap_chip(values, shift) for shift in range(1, chips)]


def gather_pieces(values, fill=()):
    return swap_pieces(send_pieces(values), fill)


def swap_pieces(parts, fill=()):
    parts = gate(parts, fill)
    return [half for part in parts for half in (part, swap_core(part))]


def reduce_pieces(even, odd):
    return send_near(add_halves(even, swap_core(odd)))


def send_near(near):
    return [near[0]] + [swap_chip(near[shift], shift) for shift in range(1, len(near))]


def swap_batch(values, shift):
    return lax.ppermute(values, "batch", [(i, i ^ shift) for i in range(4)])


def pick(values, index):
    return lax.dynamic_index_in_dim(values, index, 0, keepdims=False)


def tree_sum(parts):
    while len(parts) > 1:
        parts = [parts[i] + parts[i + 1] for i in range(0, len(parts), 2)]
    return parts[0]


def wide_values(values):
    return values.astype(jnp.float32)


def gather_first(place, quarters, x, batch, fill):
    pieces = [x] + [swap_chip(x, shift) for shift in range(1, 4)]
    sent = [
        lax.ppermute(quarters[index], "batch", [(0, index)]) for index in range(1, 4)
    ]
    quarter = jnp.where(batch == 0, quarters[0], sent[0] + sent[1] + sent[2])
    lines = jnp.stack([quarter] + [swap_chip(quarter, shift) for shift in range(1, 4)])
    lines = gate(lines, fill)
    parts = [lines] + [swap_batch(lines, shift) for shift in range(1, 4)]
    pieces = [half for piece in pieces for half in (piece, swap_core(piece))]
    return assemble(place, parts + [swap_core(part) for part in parts], pieces)


def reduce_small(near):
    total = near[0]
    for shift in range(1, 4):
        total = total + wide_values(swap_batch(near[shift], shift))
    total = total.astype(LOW)
    others = [total] + [swap_chip(total, shift) for shift in range(1, 4)]
    return total, tree_sum([wide_values(v) for v in others]).astype(LOW)


def share_small(total, token):
    others = [total] + gate([swap_batch(total, shift) for shift in range(1, 4)], token)
    parts = jnp.stack(others)
    return jnp.stack([parts, swap_core(parts)])


def reduce_late(near, early, batch, fill, third, other):
    received = [swap_batch(near[shift], shift) for shift in range(1, 4)]
    received = gate(received, fill)
    total = near[0] + sum(wide_values(part) for part in received)
    shared = total[4 * OWNED_ROWS :]
    lines = [total[OWNED_ROWS * i : OWNED_ROWS * (i + 1)] for i in range(4)]
    sent = [
        jnp.concatenate([lines[shift], shared], axis=0).astype(LOW) for shift in range(1, 4)
    ]
    received = [swap_chip(part, shift) for shift, part in enumerate(sent, 1)]
    quarter = lines[0]
    shares = [wide_values(shared.astype(LOW))]
    for part in received:
        got = wide_values(part)
        quarter = quarter + got[0:OWNED_ROWS]
        shares.append(got[OWNED_ROWS:])
    shared = tree_sum(shares).astype(LOW)
    shared = jnp.concatenate([shared, swap_core(shared)], axis=0)
    quarter = jnp.pad(quarter.astype(LOW)[None], ((0, 3), (0, 0), (0, 0)))

    def outgoing(target):
        block = jnp.where(target == 0, quarter, pick(early, jnp.maximum(target - 1, 0)))
        return jnp.concatenate([block.reshape(4 * OWNED_ROWS, LANES), shared], axis=0)

    sent = gate([outgoing(batch ^ shift) for shift in range(4)], third)
    received = [swap_batch(part, shift) for shift, part in enumerate(sent) if shift]
    received = gate([sent[0]] + received, other)
    return received


def pad_to(matrix, height, breadth):
    return jnp.pad(matrix, ((0, height - matrix.shape[0]), (0, breadth - matrix.shape[1])))


def norm_rows(vector):
    return vector.reshape(NORM_ROWS, LANES)


def norm_vector(rows):
    return rows.reshape(-1)


def gather_plain(tiles, every):
    amount = tiles.shape[0]
    unit = math.gcd(amount, D // TILE)
    local = tiles.astype(LOW).reshape(amount // unit, unit, TILE, TILE)
    local = local.transpose(0, 2, 1, 3).reshape(amount // unit, TILE, unit * TILE)
    units = lax.all_gather(local, every, axis=0, tiled=True)
    blocks = units.reshape(-1, D // TILE // unit, TILE, unit * TILE).transpose(0, 2, 1, 3)
    blocks = blocks.reshape(-1, TILE, D)
    return blocks[0:24].reshape(3 * D, D), blocks


def soap_plain(weight, moment_one, moment_two, left, right, gradient, rates):
    left, right = as_square(left), as_square(right)
    high = lax.Precision.HIGHEST
    turned = jnp.einsum("tji,tjk->tik", left, gradient, precision=high)
    turned = jnp.einsum("tik,tkl->til", turned, right, precision=high)
    new_one = BETA_ONE * as_square(moment_one) + (1.0 - BETA_ONE) * turned
    new_two = BETA_TWO * as_square(moment_two) + (1.0 - BETA_TWO) * turned * turned
    direction = (
        new_one / (1.0 - BETA_ONE**STEP) / (jnp.sqrt(new_two / (1.0 - BETA_TWO**STEP)) + EPS_ADAM)
    )
    restored = jnp.einsum("tij,tjk->tik", left, direction, precision=high)
    restored = jnp.einsum("tik,tlk->til", restored, right, precision=high)
    weight = as_square(weight)
    new = weight - rates[:, None, None] * (restored + DECAY * weight)
    return as_flat(new_one), as_flat(new_two), as_flat(new)


def update_plain(g_late, g_early, g_small, every, scale, big, small, norms):
    amount = big[0].shape[0]
    unit = math.gcd(amount, D // TILE)
    g_late, g_small = jnp.stack(g_late), jnp.stack(g_small).reshape(EARLY_ROWS, WIDE)
    late = g_late[:, :, 0 : 4 * OWNED_ROWS].reshape(2, 4, 4, OWNED_ROWS, LANES)
    late = late.transpose(2, 0, 3, 1, 4).reshape(24, TILE, D)
    w_edge = g_late[:, :, 4 * OWNED_ROWS :].transpose(0, 2, 1, 3).reshape(DE, D)
    early = g_early.reshape(8, 3, 4, 3, TILE, LANES).transpose(1, 0, 3, 4, 2, 5)
    early = early.reshape(72, TILE, D)
    grads = jnp.concatenate([late, early], axis=0)
    grads = grads.reshape(-1, TILE, D // TILE // unit, unit * TILE).transpose(0, 2, 1, 3)
    own = lax.psum_scatter(
        grads.reshape(-1, TILE, unit * TILE), every, scatter_dimension=0, tiled=True
    )
    own = wide_values(own).reshape(amount // unit, TILE, unit, TILE).transpose(0, 2, 1, 3)
    own = own.reshape(amount, TILE, TILE) * scale
    w_edge, g_small = lax.psum((wide_values(w_edge), wide_values(g_small)), every)
    strips = g_small[0:1600, 0:DE].reshape(25, TILE, 3, TILE).transpose(0, 2, 1, 3)
    tiles = jnp.concatenate(
        [as_square(to_flat_tiles(w_edge)), strips.reshape(75, TILE, TILE)], axis=0
    )
    first = lax.axis_index(every) * amount
    rates = lax.dynamic_slice_in_dim(
        jnp.asarray(rate_table(big_shapes(), big_spreads())), first, amount
    )
    big_new = soap_plain(*big, own, rates)
    rates = jnp.asarray(rate_table(small_shapes(), small_spreads()))
    small_new = soap_plain(*small, tiles * scale, rates)
    norm_new = adam_step(*norms, norm_vector(g_small[1600:1619, 0:LANES]) * scale)
    return big_new, small_new, norm_new


def body(
    node,
    edge,
    dest_device,
    dest_local,
    node_valid,
    node_cot,
    edge_cot,
    big_weight,
    big_first,
    big_second,
    big_left,
    big_right,
    small_weight,
    small_first,
    small_second,
    small_left,
    small_right,
    norm_params,
    norm_first,
    norm_second,
):
    chips = lax.axis_size("chip")
    every = ("batch", "chip", "core")
    shards = 2 * chips
    owned = node.shape[1]
    nodes = owned * shards
    rows = owned * K
    complexes = node.shape[0] * lax.axis_size("batch")
    tuned = chips == 4 and lax.axis_size("batch") == 4 and big_weight.shape[0] == 24
    chip, core, batch = (lax.axis_index(axis) for axis in ("chip", "core", "batch"))
    grad_scale = 1.0 / math.sqrt(complexes * nodes * K)
    x = node[0]
    big_state = (big_weight, big_first, big_second, big_left, big_right)
    small_state = (small_weight, small_first, small_second, small_left, small_right)
    norm_state = (norm_params, norm_first, norm_second)

    place = jnp.stack([chip, core, batch]).astype(jnp.int32) * int(tuned)
    small_groups, w_edge, e_src, e_dst, e_edge, e_mid, e_out = regroup_weights(small_weight)
    small_groups = [small_groups]
    norms = norm_params[0 : 4 * D].reshape(4, D)
    edge_norms = pad_to(norm_params[4 * D :].reshape(2, DE), 8, WIDE)
    valid = node_valid[0].astype(jnp.float32).reshape(owned, 1)
    me = chip * 2 + core
    relative = (dest_device[0].reshape(1, rows) ^ me) * owned + dest_local
    edge_across = edge[0].T
    if tuned:
        own, *quarters = own_rows(big_weight)
        blocks = lax.all_gather(own, every, axis=0, tiled=True).reshape(-1, TILE, D)
        w_rows, x_all = gather_first(
            place, quarters, x, batch, (w_edge, relative)
        )
    else:
        w_rows, blocks = gather_plain(big_weight, every)
        x_all = jnp.concatenate(gather_pieces(x), axis=0)

    even, odd, hidden, slope_one, slope_two, tall = message_forward(
        relative, edge_across, valid, x_all, owned, w_rows, w_edge, ()
    )
    sums = reduce_pieces(even, odd)
    if tuned:
        small_groups += regroup_small(small_state[1:5], (even,))
    node_low, q_src, q_dst, inside, one, act, slope, summed, scale, sums = node_forward(
        x, valid, blocks, e_src, e_dst, norms, sums, small_groups[1:2]
    )
    big_groups = list(regroup_big(big_state, (q_dst,))) if tuned else []
    q_pieces = gather_pieces(q_dst, big_groups[0:1])
    (
        edge_new, part_edge, even, odd, d_q_src, g_e_edge, g_e_mid, g_e_out, g_e_norms,
    ) = edge_phase(
        tall, edge_across, edge_cot[0].T, q_pieces, q_src, e_edge, e_mid, e_out, edge_norms, (),
    )
    d_q_dst = reduce_pieces(even, odd)
    reply, d_inside, g_early, *g_small = node_backward(
        place,
        [
            node_cot[0], d_q_src, node_low, summed, one, inside, act, slope, scale, sums,
            blocks, e_src, e_dst, norms, g_e_edge, g_e_mid, g_e_out, g_e_norms,
        ],
        d_q_dst,
        (),
    )
    replies = send_pieces(reply)
    held = ()
    if tuned:
        near_small = gate(add_halves(g_small[0], swap_core(g_small[1])), replies[1])
        part_small, small_sum = reduce_small(near_small)
        held = (part_small,)
    replies = swap_pieces(replies, held)
    d_edges, even, odd, d_p_src, *g_late = message_backward(
        place, tall, edge_across, hidden, slope_one, slope_two, part_edge, x_all, w_rows, w_edge, replies, held,
    )
    near_p = add_halves(even, swap_core(odd))
    d_p_dst = send_near(near_p)
    d_features = node_gradient(d_inside, d_p_src, w_rows, d_p_dst)

    if tuned:
        norm_groups = [norm_rows(v) for v in norm_state]
        late_groups = small_groups
        early = lax.psum_scatter(
            gate(g_early, replies), ("chip", "core"), scatter_dimension=0, tiled=True
        )
        early = early.reshape(3, 4, OWNED_ROWS, LANES)
        near_late = add_halves(g_late[0], swap_core(gate(g_late[1], small_sum)))
        small_sum = share_small(small_sum, near_late[0])
        *early_new, norm_new, norm_one, norm_two = soap_early(
            grad_scale, place, small_sum, small_groups, norm_groups
        )
        mine = reduce_late(near_late, early, batch, early_new[0], d_p_dst[1], d_features)
        big_one, big_two, big_new, big_low, small_one, small_two, small_new, small_low = soap_late(
            grad_scale, place, mine, big_groups, late_groups, early_new
        )
        norm_one, norm_two, norm_new = (norm_vector(v) for v in (norm_one, norm_two, norm_new))
    else:
        (
            (big_one, big_two, big_new),
            (small_one, small_two, small_new),
            (norm_one, norm_two, norm_new),
        ) = update_plain(
            g_late, g_early, g_small, every, grad_scale, big_state, small_state, norm_state
        )
        big_low = big_new.astype(LOW)
        small_low = small_new.astype(LOW)
    return (
        node_low[None],
        edge_new.T[None],
        d_features[None],
        d_edges.T[None],
        big_one,
        big_two,
        big_new,
        big_low,
        small_one,
        small_two,
        small_new,
        small_low,
        norm_one,
        norm_two,
        norm_new,
    )


def solution(mesh):
    batch, shards = mesh.devices.shape
    fine = Mesh(mesh.devices.reshape(batch, shards // 2, 2), ("batch", "chip", "core"))
    edge = ("chip", "core")
    every = ("batch", "chip", "core")
    placed = (
        P("batch", edge, None),
        P("batch", edge, None),
        P("batch", edge, None),
        P("batch", edge),
        P("batch", edge),
        P("batch", edge, None),
        P("batch", edge, None),
        P(every, None),
        P(every, None),
        P(every, None),
        P(every, None),
        P(every, None),
        P(),
        P(),
        P(),
        P(),
        P(),
        P(),
        P(),
        P(),
    )
    return jax.shard_map(
        body,
        mesh=fine,
        in_specs=placed,
        out_specs=(
            P("batch", edge, None),
            P("batch", edge, None),
            P("batch", edge, None),
            P("batch", edge, None),
            P(every, None),
            P(every, None),
            P(every, None),
            P(every, None),
            P(),
            P(),
            P(),
            P(),
            P(),
            P(),
            P(),
        ),
        check_vma=False,
    )
```

```python
import functools
import math

import jax
import jax.numpy as jnp
import numpy as np
from jax import lax
from jax.experimental import pallas as pl
from jax.experimental.pallas import tpu as pltpu
from jax.sharding import Mesh
from jax.sharding import PartitionSpec as P

D = 512
DE = 192
FF = 2048
K = 60
TILE = 64
STEP = 10


BETA_ONE = 0.5
BETA_TWO = 0.5
EPS_ADAM = 1e-08
EPS_NORM = 1e-05
DECAY = 0.01
NORM_RATE = 0.4
PRECISION_HIGH = lax.Precision.HIGHEST


def big_shapes():
    return [(D, D), (D, D), (D, D), (D, D), (D, FF), (FF, D)]


def small_shapes():
    return [(DE, D), (D, DE), (D, DE), (DE, DE), (DE, DE), (DE, DE)]


def big_spreads():
    middle = (2 * D + DE) ** (-0.5)
    return [middle, middle, D ** (-0.5), 2.5 * D ** (-0.5), D ** (-0.5), FF ** (-0.5)]


def small_spreads():
    middle = (2 * D + DE) ** (-0.5)
    return [middle, middle, middle, middle, DE ** (-0.5), 1.5 * DE ** (-0.5)]


def rate_table(shapes, spreads):
    amounts = [height // TILE * (breadth // TILE) for height, breadth in shapes]
    return np.repeat(np.array(spreads, np.float32), amounts)


def as_square(flat_tiles):
    return flat_tiles.reshape(flat_tiles.shape[0], TILE, TILE)


def as_flat(square_tiles):
    return square_tiles.reshape(square_tiles.shape[0], TILE * TILE)


def from_tiles(tile_stack, shapes):
    matrices = []
    offset = 0
    for height, breadth in shapes:
        amount = height // TILE * (breadth // TILE)
        blocked = tile_stack[offset : offset + amount].reshape(
            height // TILE, breadth // TILE, TILE, TILE
        )
        matrices.append(blocked.transpose(0, 2, 1, 3).reshape(height, breadth))
        offset += amount
    return matrices


def to_flat_tiles(matrix):
    height, breadth = matrix.shape
    blocked = matrix.reshape(height // TILE, TILE, breadth // TILE, TILE)
    return blocked.transpose(0, 2, 1, 3).reshape(-1, TILE * TILE)


def adam_step(params, moment_one, moment_two, gradient):
    new_one = BETA_ONE * moment_one + (1.0 - BETA_ONE) * gradient
    new_two = BETA_TWO * moment_two + (1.0 - BETA_TWO) * gradient * gradient
    direction = (
        new_one / (1.0 - BETA_ONE**STEP) / (jnp.sqrt(new_two / (1.0 - BETA_TWO**STEP)) + EPS_ADAM)
    )
    return (new_one, new_two, params - NORM_RATE * direction)


def times_transposed(left_side, right_side):
    return lax.dot_general(
        left_side, right_side, (((1,), (1,)), ((), ())), preferred_element_type=jnp.float32
    )


LOW = jnp.bfloat16
WIDE = 256
GELU_A = math.sqrt(2.0 / math.pi)
GELU_B = GELU_A * 0.044715
OWNED_ROWS = 3 * TILE


def dot(left, right):
    return jnp.dot(left, right, preferred_element_type=jnp.float32)


def dot_rows(left, right):
    return lax.dot_general(
        left, right, (((0,), (0,)), ((), ())), preferred_element_type=jnp.float32
    )


def dot_turned(left, right):
    return lax.dot_general(
        left, right, (((1,), (1,)), ((), ())), preferred_element_type=jnp.float32
    )


def split_low(values):
    high = values.astype(LOW)
    return high, (values - high.astype(jnp.float32)).astype(LOW)


def gelu_pair(v):
    square = v * v
    half = 0.5 * jnp.tanh(v * (GELU_A + GELU_B * square)) + 0.5
    out = v * half
    slope = half + out * (1.0 - half) * (2.0 * GELU_A + 6.0 * GELU_B * square)
    return out, slope


def norm_parts(values, width):
    centre = jnp.sum(values, axis=-1, keepdims=True) * (1.0 / width)
    centered = values - centre
    if values.shape[-1] != width:
        lane = lax.broadcasted_iota(jnp.int32, values.shape, 1)
        centered = jnp.where(lane < width, centered, 0.0)
    spread = jnp.sum(centered * centered, axis=-1, keepdims=True) * (1.0 / width)
    inverse = lax.rsqrt(spread + EPS_NORM)
    return centered * inverse, inverse


def norm_back(scaled, inverse, gain, upstream, width):
    inner = upstream * gain
    mean_inner = jnp.sum(inner, axis=-1, keepdims=True) * (1.0 / width)
    mean_cross = jnp.sum(inner * scaled, axis=-1, keepdims=True) * (1.0 / width)
    return inverse * (inner - mean_inner - scaled * mean_cross)


def whole(shape):
    return pl.BlockSpec(shape, lambda *_: (0,) * len(shape), pipeline_mode=pl.Buffered(1))


def anywhere(values):
    return [pl.BlockSpec(memory_space=pl.ANY)] * len(values)


def kept(shape):
    return pl.BlockSpec(shape, lambda *_: (0,) * len(shape))


def params(limit=58):
    return pltpu.CompilerParams(vmem_limit_bytes=limit * 2**20)


def shaped(shape, dtype):
    return jax.ShapeDtypeStruct(shape, dtype)


def trimmed(kernel, inputs, unread):
    def run(*refs):
        kernel(*refs[:inputs], *refs[inputs + unread :])

    return run


def target_columns(targets, nodes):
    down = lax.broadcasted_iota(jnp.int32, (nodes, targets.shape[1]), 0)
    return jnp.where(down == targets, 1.0, 0.0).astype(LOW)


def source_mask(block):
    row = lax.broadcasted_iota(jnp.int32, (WIDE - DE, block), 0)
    source = lax.broadcasted_iota(jnp.int32, (WIDE - DE, block), 1) // K
    return jnp.where((row == source) | (row == source + block // K), 1.0, 0.0)


def block_of():
    return 32 * K


def lanes(height, block):
    return pl.BlockSpec((height, block), lambda i: (0, i))


def tall_lanes(nodes, block):
    buffers = pl.Buffered(2 if nodes <= 1024 else 1)
    return pl.BlockSpec((nodes, block), lambda i: (0, i), pipeline_mode=buffers)


def source_rows(values):
    high = values.astype(LOW).astype(jnp.float32)
    return jnp.concatenate([high, values - high], axis=0).astype(LOW)


def put_halves(halves, total, owned):
    for index in range(total.shape[0] // owned):
        rows = total[index * owned : (index + 1) * owned].astype(LOW)
        halves[index % 2][index // 2, 0:owned, :] = rows


COUNT_ROWS = 16


def message_kernel(
    targets, edge, valid, w_rows, w_edge, x_all,
    even, odd, hidden_out, slope_one, slope_two, tall,
    table, mixed, from_source, total, mid, counts, wide,
):
    step = pl.program_id(0)
    owned = from_source.shape[0]

    @pl.when(step == 0)
    def _():
        table[...] = dot(x_all[...], w_rows[D : 2 * D]).astype(LOW).T
        from_source[...] = dot(x_all[0:owned], w_rows[0:D])
        mixed[0:DE] = w_edge[...]
        mid[...] = w_rows[2 * D : 3 * D].T
        wide[DE:WIDE] = source_mask(edge.shape[1]).astype(LOW)
        total[...] = jnp.zeros_like(total)
        counts[...] = jnp.zeros_like(counts)

    nodes, block = tall.shape
    group = block // K
    wide[0:DE] = edge[...]
    tall[...] = target_columns(targets[...], nodes)
    mixed[DE:WIDE] = source_rows(from_source[pl.ds(step * group, group), :])
    pre = dot(table[...], tall[...]) + dot_rows(mixed[...], wide[...])
    hidden, slope = gelu_pair(pre)
    hidden = hidden.astype(LOW)
    hidden_out[...] = hidden
    slope_one[...] = slope.astype(LOW)
    second, slope = gelu_pair(dot(mid[...], hidden))
    ok = jnp.sum(source_mask(block)[0:group] * valid[...], axis=0, keepdims=True)
    slope_two[...] = (slope * ok).astype(LOW)
    total[...] += dot_turned(tall[...], (second * ok).astype(LOW))
    ok_rows = jnp.broadcast_to(ok, (COUNT_ROWS, ok.shape[1])).astype(LOW)
    counts[...] += dot_turned(ok_rows, tall[...])

    @pl.when(step == pl.num_programs(0) - 1)
    def _():
        put_halves((even, odd), total, owned)
        for index in range(total.shape[0] // owned):
            amount = counts[:, index * owned : (index + 1) * owned]
            high = jnp.floor(amount * (1.0 / LANES))
            place = (even, odd)[index % 2].at[index // 2]
            rows = pl.ds(owned, COUNT_ROWS)
            place[rows, :] = jnp.zeros((COUNT_ROWS, D), LOW)
            place[rows, 0:owned] = high.astype(LOW)
            place[rows, LANES : LANES + owned] = (amount - high * LANES).astype(LOW)


def message_forward(targets, edge, valid, x_all, owned, w_rows, w_edge, after):
    nodes, rows = x_all.shape[0], targets.shape[1]
    block = block_of()
    half = (nodes // owned // 2, owned + COUNT_ROWS, D)
    return pl.pallas_call(
        trimmed(message_kernel, 6, len(after)),
        grid=(rows // block,),
        in_specs=[
            lanes(1, block),
            lanes(DE, block),
            pl.BlockSpec((block // K, 1), lambda i: (i, 0)),
            whole((3 * D, D)),
            whole((DE, D)),
            whole((nodes, D)),
        ]
        + anywhere(after),
        out_specs=[kept(half), kept(half)] + [lanes(D, block)] * 3 + [tall_lanes(nodes, block)],
        out_shape=[shaped(half, LOW)] * 2
        + [shaped((D, rows), LOW)] * 3
        + [shaped((nodes, rows), LOW)],
        scratch_shapes=[
            pltpu.VMEM((D, nodes), LOW),
            pltpu.VMEM((WIDE, D), LOW),
            pltpu.VMEM((owned, D), jnp.float32),
            pltpu.VMEM((nodes, D), jnp.float32),
            pltpu.VMEM((D, D), LOW),
            pltpu.VMEM((COUNT_ROWS, nodes), jnp.float32),
            pltpu.VMEM((WIDE, block), LOW),
        ],
        compiler_params=params(),
    )(targets, edge, valid, w_rows, w_edge, x_all, *after)


def up_part(blocks, part):
    per, parts = D // TILE, FF // D
    strips = [blocks[4 * per + row * parts + part] for row in range(per)]
    return jnp.concatenate(strips, axis=0)


def out_part(blocks):
    per = D // TILE
    return blocks[3 * per : 4 * per].reshape(D, D)


def down_part(blocks, part):
    per = D // TILE
    first = per * (4 + FF // D + part)
    return blocks[first : first + per].reshape(D, D)


def node_forward_kernel(x, valid, blocks, u_src, u_dst, norms, *refs):
    pieces = refs[:-10]
    (
        low_out, q_src, q_dst, inside_out, one_out, act_out, slope_out, summed_out, scale_out,
        sums_out,
    ) = refs[-10:]
    summed_all = sum(piece[...].astype(jnp.float32) for piece in pieces)
    owned = x.shape[0]
    sums = summed_all[0:owned]
    tally = summed_all[owned : owned + 8, 0:LANES] * float(LANES)
    tally += summed_all[owned : owned + 8, LANES : 2 * LANES]
    amount = tally.T[0:owned, 0:1]
    scale = valid[...] / jnp.maximum(amount * valid[...], 1.0)
    scale_out[...] = scale
    sums_out[...] = sums
    high, low = split_low(sums * scale)
    w_out = out_part(blocks)
    inside = x[...].astype(jnp.float32) + (dot(high, w_out) + dot(low, w_out))
    scaled, _ = norm_parts(inside, D)
    one = scaled * norms[0:1] + norms[1:2]
    one_low = one.astype(LOW)
    narrowed = jnp.zeros_like(one)
    for part in range(FF // D):
        act, slope = gelu_pair(dot(one_low, up_part(blocks, part)))
        act = act.astype(LOW)
        act_out[:, part * D : (part + 1) * D] = act
        slope_out[:, part * D : (part + 1) * D] = slope.astype(LOW)
        narrowed += dot(act, down_part(blocks, part))
    summed = one + narrowed
    scaled, _ = norm_parts(summed, D)
    two = (scaled * norms[2:3] + norms[3:4]).astype(LOW)
    low_out[...] = two
    q_src[...] = dot(two, u_src[...])
    q_dst[...] = dot(two, u_dst[...]).astype(LOW)
    inside_out[...] = inside
    one_out[...] = one
    summed_out[...] = summed


def node_forward(x, valid, blocks, u_src, u_dst, norms, pieces, after):
    owned = x.shape[0]
    wide = shaped((owned, D), jnp.float32)
    operands = [x, valid, blocks, u_src, u_dst, norms, *pieces]
    return pl.pallas_call(
        trimmed(node_forward_kernel, len(operands), len(after)),
        in_specs=[pl.BlockSpec(memory_space=pltpu.VMEM)] * len(operands) + anywhere(after),
        out_shape=[
            shaped((owned, D), LOW),
            shaped((owned, WIDE), jnp.float32),
            shaped((owned, WIDE), LOW),
            wide,
            wide,
            shaped((owned, FF), LOW),
            shaped((owned, FF), LOW),
            wide,
            shaped((owned, 1), jnp.float32),
            wide,
        ],
        compiler_params=params(),
    )(*operands, *after)


def tall_norm(values):
    width = values.shape[0]
    centre = jnp.sum(values, axis=0, keepdims=True) * (1.0 / width)
    centered = values - centre
    spread = jnp.sum(centered * centered, axis=0, keepdims=True) * (1.0 / width)
    inverse = lax.rsqrt(spread + EPS_NORM)
    return centered * inverse, inverse


def tall_norm_back(scaled, inverse, gain, upstream):
    width = scaled.shape[0]
    inner = upstream * gain
    mean_inner = jnp.sum(inner, axis=0, keepdims=True) * (1.0 / width)
    mean_cross = jnp.sum(inner * scaled, axis=0, keepdims=True) * (1.0 / width)
    return inverse * (inner - mean_inner - scaled * mean_cross)


def lane_sums(values):
    return sum(
        values[:, first : first + LANES] for first in range(0, values.shape[1], LANES)
    )


def edge_kernel(count, tall, edge, cot, q_src, u_edge, u_mid, u_out, norms, *refs):
    pieces = refs[0:count]
    (
        edge_out, d_edge, even, odd, d_source, g_edge, g_mid, g_out, g_norms,
        table, mixed, total, mid_turned, out_turned, gain_sum, shift_sum, columns, wide,
    ) = refs[-18:]
    step = pl.program_id(0)
    last = pl.num_programs(0) - 1
    owned = q_src.shape[0]

    @pl.when(step == 0)
    def _():
        table[...] = jnp.concatenate([piece[...] for piece in pieces], axis=0).T
        mixed[0:DE] = u_edge[...]
        mid_turned[...] = u_mid[...].T
        out_turned[...] = u_out[...].T
        columns[...] = norms[...].T
        wide[DE:WIDE] = source_mask(edge.shape[1]).astype(LOW)
        for ref in (total, gain_sum, shift_sum, g_edge, g_mid, g_out):
            ref[...] = jnp.zeros_like(ref)

    group = edge_out.shape[1] // K
    mixed[DE:WIDE] = source_rows(q_src[pl.ds(step * group, group), :])
    wide[0:DE] = edge[...]
    both = wide[...]
    first, slope_one = gelu_pair(
        dot(table[0:DE], tall[...]) + dot(mixed[...].T[0:DE], both)
    )
    first = first.astype(LOW)
    second, slope_two = gelu_pair(dot(mid_turned[0:DE, 0:DE], first))
    second = second.astype(LOW)
    change = dot(out_turned[0:DE, 0:DE], second)
    scaled, inverse = tall_norm(both[0:DE].astype(jnp.float32) + change)
    gain, offset = columns[0:DE, 0:1], columns[0:DE, 1:2]
    edge_out[...] = (scaled * gain + offset).astype(LOW)
    back = cot[...].astype(jnp.float32)
    gain_sum[...] += lane_sums(back * scaled)
    shift_sum[...] += lane_sums(back)
    d_sum = tall_norm_back(scaled, inverse, gain, back)
    d_change = d_sum.astype(LOW)
    g_out[0:DE, 0:DE] += dot_turned(second, d_change)
    d_second = (dot(u_out[:, 0:DE], d_change) * slope_two).astype(LOW)
    g_mid[0:DE, 0:DE] += dot_turned(first, d_second)
    d_first = (dot(u_mid[:, 0:DE], d_second) * slope_one).astype(LOW)
    d_edge[...] = d_sum + dot(u_edge[:, 0:DE], d_first)
    turned = dot_turned(both, d_first)
    g_edge[:, 0:DE] += turned[0:DE]
    d_source[pl.ds(step * group, group), :] = turned[DE : DE + group]
    total[:, 0:DE] += dot_turned(tall[...], d_first)

    @pl.when(step == last)
    def _():
        put_halves((even, odd), total, owned)
        gain_row = jnp.sum(gain_sum[...].T, axis=0, keepdims=True)
        shift_row = jnp.sum(shift_sum[...].T, axis=0, keepdims=True)
        both_rows = jnp.concatenate([gain_row, shift_row], axis=1)
        g_norms[...] = jnp.zeros_like(g_norms)
        for index in range(3):
            g_norms[index : index + 1] = both_rows[:, index * LANES : (index + 1) * LANES]


def edge_phase(tall, edge, cot, pieces, q_src, u_edge, u_mid, u_out, norms, after):
    nodes, rows = tall.shape
    owned = q_src.shape[0]
    block = block_of()
    count = len(pieces)
    half = (count // 2, owned, WIDE)
    square = shaped((DE, WIDE), jnp.float32)
    line = shaped((8, LANES), jnp.float32)
    return pl.pallas_call(
        functools.partial(edge_kernel, count),
        grid=(rows // block,),
        in_specs=[
            tall_lanes(nodes, block),
            lanes(DE, block),
            lanes(DE, block),
            whole((owned, WIDE)),
            whole((DE, WIDE)),
            whole((DE, WIDE)),
            whole((DE, WIDE)),
            whole((8, WIDE)),
        ]
        + [whole((owned, WIDE))] * count
        + anywhere(after),
        out_specs=[
            lanes(DE, block),
            lanes(DE, block),
            kept(half),
            kept(half),
            kept((owned, DE)),
            kept((DE, WIDE)),
            kept((DE, WIDE)),
            kept((DE, WIDE)),
            kept((8, LANES)),
        ],
        out_shape=[
            shaped((DE, rows), LOW),
            shaped((DE, rows), jnp.float32),
            shaped(half, LOW),
            shaped(half, LOW),
            shaped((owned, DE), jnp.float32),
            square,
            square,
            square,
            line,
        ],
        scratch_shapes=[
            pltpu.VMEM((WIDE, nodes), LOW),
            pltpu.VMEM((WIDE, WIDE), LOW),
            pltpu.VMEM((nodes, WIDE), jnp.float32),
            pltpu.VMEM((WIDE, DE), LOW),
            pltpu.VMEM((WIDE, DE), LOW),
            pltpu.VMEM((DE, LANES), jnp.float32),
            pltpu.VMEM((DE, LANES), jnp.float32),
            pltpu.VMEM((WIDE, 8), jnp.float32),
            pltpu.VMEM((WIDE, block), LOW),
        ],
        compiler_params=params(),
    )(tall, edge, cot, q_src, u_edge, u_mid, u_out, norms, *pieces, *after)


def put_blocks(ref, base, matrix, step=1):
    for row in range(matrix.shape[0] // TILE):
        strip = matrix[row * TILE : (row + 1) * TILE].astype(ref.dtype)
        owner, batch, slot = early_place(base + row * step)
        for part in range(4):
            ref[owner, batch, part, slot * TILE : (slot + 1) * TILE, :] = strip[
                :, part * LANES : (part + 1) * LANES
            ]


def put_sides(refs, core, stores):
    for own in range(2):

        @pl.when(core == own)
        def _():
            for side, value, index in stores:
                refs[side ^ own][index] = value


def small_stores(batch, begin, matrix):
    stores = []
    piece = EARLY_ROWS // 8
    end = begin + matrix.shape[0]
    first = begin
    while first < end:
        index, offset = first // piece, first % piece
        amount = min(end - first, piece - offset)
        value = matrix[first - begin : first - begin + amount].astype(LOW)
        place = (index % 4 ^ batch, slice(offset, offset + amount), slice(None))
        stores.append((index // 4, value, place))
        first += amount
    return stores


def put_norm(ref, index, values):
    total = jnp.sum(values, axis=0, keepdims=True)
    for part in range(4):
        row = index * 4 + part
        ref[row : row + 1, 0:LANES] = total[:, part * LANES : (part + 1) * LANES]


def early_place(block):
    batch, rest = block // 24, block % 24
    return rest // 3, batch, rest % 3


def node_backward_kernel(
    place, cot, d_q_src, low, summed, one, inside, act, slope, scale, sums,
    blocks, u_src, u_dst, norms, g_edge, g_mid, g_out, g_edge_norms, *refs,
):
    reply, d_inside_out, g_blocks, g_even, g_odd, g_norms = refs[-6:]
    pieces = refs[:-6]
    core, batch = place[1], place[2]
    stores = []
    d_src = d_q_src[...].astype(LOW)
    d_dst = sum(piece[...].astype(jnp.float32) for piece in pieces).astype(LOW)
    low_now = low[...]
    blank = jnp.zeros((D, WIDE - DE), jnp.float32)
    stores += small_stores(batch, 0, jnp.concatenate([dot_rows(low_now, d_src), blank], axis=1))
    stores += small_stores(batch, D, dot_rows(low_now, d_dst))
    for index, ref in enumerate((g_edge, g_mid, g_out)):
        stores += small_stores(batch, 2 * D + index * DE, ref[...])
    g_norms[...] = jnp.zeros_like(g_norms)
    g_norms[16:24, 0:LANES] = g_edge_norms[...]
    d_final = (
        cot[...].astype(jnp.float32)
        + dot_turned(d_src, u_src[:, 0:DE])
        + dot_turned(d_dst, u_dst[...])
    )
    scaled, inverse = norm_parts(summed[...], D)
    d_summed = norm_back(scaled, inverse, norms[2:3], d_final, D)
    put_norm(g_norms, 2, d_final * scaled)
    put_norm(g_norms, 3, d_final)
    d_narrow = d_summed.astype(LOW)
    one_low = one[...].astype(LOW)
    d_one = d_summed
    first_up = D // TILE
    parts = FF // D
    first_down = first_up + first_up * parts
    for part in range(parts):
        cols = slice(part * D, (part + 1) * D)
        put_blocks(g_blocks, first_down + part * first_up, dot_rows(act[:, cols], d_narrow))
        d_wide = (
            dot_turned(d_narrow, down_part(blocks, part)) * slope[:, cols].astype(jnp.float32)
        ).astype(LOW)
        put_blocks(g_blocks, first_up + part, dot_rows(one_low, d_wide), parts)
        d_one += dot_turned(d_wide, up_part(blocks, part))
    scaled, inverse = norm_parts(inside[...], D)
    d_inside = norm_back(scaled, inverse, norms[0:1], d_one, D)
    put_norm(g_norms, 0, d_one * scaled)
    put_norm(g_norms, 1, d_one)
    d_inside_out[...] = d_inside
    per_target = (d_inside * scale[...]).astype(LOW)
    high, rest = split_low(sums[...])
    put_blocks(g_blocks, 0, dot_rows(high, per_target) + dot_rows(rest, per_target))
    reply[...] = dot_turned(per_target, out_part(blocks)).astype(LOW)
    stores += small_stores(batch, 2 * D + 3 * DE, g_norms[...])
    put_sides((g_even, g_odd), core, stores)


def node_backward(place, operands, pieces, after):
    owned = operands[0].shape[0]
    half = shaped((4, EARLY_ROWS // 8, WIDE), LOW)
    amount = len(operands) + len(pieces)
    return pl.pallas_call(
        trimmed(node_backward_kernel, amount + 1, len(after)),
        in_specs=[pl.BlockSpec(memory_space=pltpu.SMEM)]
        + [pl.BlockSpec(memory_space=pltpu.VMEM)] * amount
        + anywhere(after),
        out_shape=[
            shaped((owned, D), LOW),
            shaped((owned, D), jnp.float32),
            shaped((8, 3, 4, OWNED_ROWS, LANES), LOW),
            half,
            half,
        ],
        scratch_shapes=[pltpu.VMEM((TILE, WIDE), jnp.float32)],
        compiler_params=params(),
    )(place, *operands, *pieces, *after)


def message_back_kernel(
    count, place, tall, edge, hidden, slope_one, slope_two, part_edge, x_all, w_mid, w_edge, *refs
):
    pieces = refs[0:count]
    (
        d_edge, even, odd, d_source, late_even, late_odd, table, total, g_mid, g_edge, from_source, wide,
    ) = refs[-12:]
    step = pl.program_id(0)
    owned = d_source.shape[0]

    @pl.when(step == 0)
    def _():
        table[...] = jnp.concatenate([piece[...] for piece in pieces], axis=0).T
        wide[DE:WIDE] = source_mask(edge.shape[1]).astype(LOW)
        total[...] = jnp.zeros_like(total)
        g_mid[...] = jnp.zeros_like(g_mid)
        g_edge[...] = jnp.zeros_like(g_edge)

    wide[0:DE] = edge[...]
    d_hidden = dot(table[...], tall[...])
    d_second = (d_hidden * slope_two[...].astype(jnp.float32)).astype(LOW)
    g_mid[...] += dot_turned(hidden[...], d_second)
    d_pre = (dot(w_mid[...], d_second) * slope_one[...].astype(jnp.float32)).astype(LOW)
    d_edge[...] = part_edge[...] + dot(w_edge[...], d_pre)
    turned = dot_turned(wide[...], d_pre)
    g_edge[...] += turned[0:DE]
    group = hidden.shape[1] // K
    from_source[pl.ds(step * group, group), :] = turned[DE : DE + group]
    total[...] += dot_turned(tall[...], d_pre)

    @pl.when(step == pl.num_programs(0) - 1)
    def _():
        put_halves((even, odd), total, owned)
        gathered = x_all[...]
        sources_low = from_source[...].astype(LOW)
        d_source[...] = sources_low
        chip, core, batch = place[0], place[1], place[2]
        matrices = (
            dot_rows(gathered[0:owned], sources_low),
            dot_rows(gathered, total[...].astype(LOW)),
            g_mid[...],
        )
        stores = []
        for row in range(3 * (D // TILE)):
            owner, slot = row // 3, row % 3
            strip = matrices[row // (D // TILE)][row % (D // TILE) * TILE :][0:TILE].astype(LOW)
            first = pl.multiple_of((owner // 2 ^ chip) * OWNED_ROWS + slot * TILE, TILE)
            for part in range(4):
                value = strip[:, part * LANES : (part + 1) * LANES]
                stores.append((owner % 2, value, (part ^ batch, pl.ds(first, TILE), slice(None))))
        half = DE // 2
        for side in range(2):
            strip = g_edge[side * half : (side + 1) * half].astype(LOW)
            for part in range(4):
                value = strip[:, part * LANES : (part + 1) * LANES]
                rows = slice(4 * OWNED_ROWS, 4 * OWNED_ROWS + half)
                stores.append((side, value, (part ^ batch, rows, slice(None))))
        put_sides((late_even, late_odd), core, stores)


def message_backward(
    place, tall, edge, hidden, slope_one, slope_two, part_edge, x_all, w_rows, w_edge, pieces, after
):
    nodes, rows = tall.shape
    owned = pieces[0].shape[0]
    block = block_of()
    count = len(pieces)
    half = (count // 2, owned, D)
    feature = tall_lanes(D, block) if nodes <= 1024 else pl.BlockSpec(
        (D, block), lambda i: (0, i), pipeline_mode=pl.Buffered(1)
    )
    late = (4, 4 * OWNED_ROWS + DE // 2, LANES)
    return pl.pallas_call(
        functools.partial(message_back_kernel, count),
        grid=(rows // block,),
        in_specs=[
            pl.BlockSpec(memory_space=pltpu.SMEM),
            tall_lanes(nodes, block),
            lanes(DE, block),
            feature,
            feature,
            feature,
            lanes(DE, block),
            whole((nodes, D)),
            pl.BlockSpec((D, D), lambda i: (2, 0), pipeline_mode=pl.Buffered(1)),
            whole((DE, D)),
        ]
        + [whole((owned, D))] * count
        + anywhere(after),
        out_specs=[
            lanes(DE, block),
            kept(half),
            kept(half),
            kept((owned, D)),
            kept(late),
            kept(late),
        ],
        out_shape=[
            shaped((DE, rows), jnp.float32),
            shaped(half, LOW),
            shaped(half, LOW),
            shaped((owned, D), LOW),
            shaped(late, LOW),
            shaped(late, LOW),
        ],
        scratch_shapes=[
            pltpu.VMEM((D, nodes), LOW),
            pltpu.VMEM((nodes, D), jnp.float32),
            pltpu.VMEM((D, D), jnp.float32),
            pltpu.VMEM((DE, D), jnp.float32),
            pltpu.VMEM((owned, D), jnp.float32),
            pltpu.VMEM((WIDE, block), LOW),
        ],
        compiler_params=params(),
    )(
        place, tall, edge, hidden, slope_one, slope_two, part_edge, x_all, w_rows, w_edge,
        *pieces, *after,
    )


def node_gradient_kernel(inside, d_source, w_rows, *refs):
    pieces, out = refs[:-1], refs[-1]
    d_target = sum(piece[...].astype(jnp.float32) for piece in pieces).astype(LOW)
    out[...] = (
        inside[...]
        + dot_turned(d_source[...], w_rows[0:D])
        + dot_turned(d_target, w_rows[D : 2 * D])
    )


def node_gradient(inside, d_source, w_rows, pieces):
    return pl.pallas_call(
        node_gradient_kernel,
        out_shape=shaped(inside.shape, jnp.float32),
        compiler_params=params(12),
    )(inside, d_source, w_rows, *pieces)


def add_halves_kernel(left, right, *outs):
    for index, out in enumerate(outs):
        total = left[index].astype(jnp.float32) + right[index].astype(jnp.float32)
        out[...] = total.astype(out.dtype)


def add_halves(left, right):
    shape = left.shape[1:]
    return pl.pallas_call(
        add_halves_kernel,
        out_shape=[shaped(shape, jnp.float32)] + [shaped(shape, LOW)] * (left.shape[0] - 1),
        compiler_params=params(8),
    )(left, right)


def assemble_kernel(count, place, *refs):
    lines, pieces, rows, x_all = refs[0:8], refs[8:-2], refs[-2], refs[-1]
    chip, core, batch = place[0], place[1], place[2]
    owned = pieces[0].shape[0]
    for index, piece in enumerate(lines):
        side, part = index // 4, index % 4
        for line in range(4):
            row = ((line ^ chip) * 2 + (side ^ core)) * OWNED_ROWS
            lane = (part ^ batch) * LANES
            rows[
                pl.ds(pl.multiple_of(row, TILE), OWNED_ROWS),
                pl.ds(pl.multiple_of(lane, LANES), LANES),
            ] = piece[line]
    for index, piece in enumerate(pieces):
        x_all[index * owned : (index + 1) * owned] = piece[...]


def assemble(place, lines, pieces):
    owned = pieces[0].shape[0]
    amount = len(lines) + len(pieces)
    return pl.pallas_call(
        functools.partial(assemble_kernel, len(pieces)),
        in_specs=[pl.BlockSpec(memory_space=pltpu.SMEM)]
        + [pl.BlockSpec(memory_space=pltpu.VMEM)] * amount,
        out_shape=[shaped((3 * D, D), LOW), shaped((8 * owned, D), LOW)],
        compiler_params=params(12),
    )(place, *lines, *pieces)


def own_rows_kernel(tiles, rows, *refs):
    quarters, (flat, pair) = refs[0:4], refs[4:]
    load_flat(tiles, flat)
    for index, group in enumerate(group_list(0, 24, 4)):
        block, side = index // 2, index % 2
        value = group_in(flat, pair, group).astype(LOW)
        rows[block * TILE : (block + 1) * TILE, side * QUAD : (side + 1) * QUAD] = value
        for half in range(2):
            quarters[2 * side + half][block * TILE : (block + 1) * TILE, :] = value[
                :, half * LANES : (half + 1) * LANES
            ]


def own_rows(tiles):
    return pl.pallas_call(
        own_rows_kernel,
        out_shape=[
            shaped((OWNED_ROWS, D), LOW),
        ] + [shaped((OWNED_ROWS, LANES), LOW)] * 4 + [
        ],
        scratch_shapes=[
            pltpu.VMEM((flat_rows(24), LANES), jnp.float32),
            pltpu.VMEM((TILE, LANES), jnp.float32),
        ],
        compiler_params=params(),
    )(tiles)


LANES = 128
QUAD = 4 * TILE
FLAT = TILE * TILE // LANES


def group_list(first, last, size):
    return [list(range(t, min(t + size, last))) for t in range(first, last, size)]


def load_flat(ref, flat):
    amount = ref.shape[0]
    for top in range(0, amount, 8):
        rows = min(8, amount - top)
        for part in range(FLAT):
            flat[pl.ds(top * FLAT + 8 * part, rows), :] = ref[
                top : top + rows, part * LANES : (part + 1) * LANES
            ]


def store_flat(ref, flat, first=0, last=None):
    last = ref.shape[0] if last is None else last
    while first < last:
        rows = min(8 - first % 8, last - first)
        top = first // 8 * 8
        for part in range(FLAT):
            ref[first : first + rows, part * LANES : (part + 1) * LANES] = flat[
                pl.ds(top * FLAT + 8 * part + first - top, rows), :
            ]
        first += rows


def tile_rows(tile):
    return pl.ds(tile // 8 * 8 * FLAT + tile % 8, FLAT, stride=8)


def lower_half(shape):
    return lax.broadcasted_iota(jnp.int32, shape, 1) < TILE


def group_in(flat, pair, tiles):
    left = lower_half((FLAT, LANES))
    halves = []
    for first in range(0, 4, 2):
        here = tiles[first : first + 2]
        one = flat[tile_rows(here[0]), :] if here else jnp.zeros((FLAT, LANES), jnp.float32)
        two = flat[tile_rows(here[1]), :] if len(here) > 1 else jnp.zeros_like(one)
        pair[pl.ds(0, FLAT, stride=2), :] = jnp.where(left, one, pltpu.roll(two, TILE, 1))
        pair[pl.ds(1, FLAT, stride=2), :] = jnp.where(left, pltpu.roll(one, TILE, 1), two)
        halves.append(pair[...])
    return jnp.concatenate(halves, axis=1)


def group_out(value, flat, pair, tiles):
    left = lower_half((FLAT, LANES))
    for first in range(0, 4, 2):
        here = tiles[first : first + 2]
        if not here:
            continue
        pair[...] = value[:, first * TILE : first * TILE + LANES]
        even = pair[pl.ds(0, FLAT, stride=2), :]
        odd = pair[pl.ds(1, FLAT, stride=2), :]
        flat[tile_rows(here[0]), :] = jnp.where(left, even, pltpu.roll(odd, TILE, 1))
        if len(here) > 1:
            flat[tile_rows(here[1]), :] = jnp.where(left, pltpu.roll(even, TILE, 1), odd)


def flat_rows(amount):
    return -(-amount // 8) * 8 * FLAT


SPAN_GROUPS = 8


def regroup_small_kernel(count, *refs):
    tiles, outs = refs[0:count], refs[count : 2 * count]
    flat, pair = refs[-2:]
    step = pl.program_id(0)
    for condition, amount, size, spot in (
        (step == 0, 24, 4, 0),
        ((step > 0) & (step < 4), 24, 3, 0),
        (step == 4, 3, 3, 0),
    ):

        @pl.when(condition)
        def _():
            for ref, out in zip(tiles, outs):
                load_flat(ref, flat)
                for index, group in enumerate(group_list(0, amount, size)):
                    out[spot + index] = group_in(flat, pair, group)


def regroup_small(arrays, after=()):
    count = len(arrays)
    shape = (5 * SPAN_GROUPS, TILE, QUAD)
    out_spec = pl.BlockSpec((SPAN_GROUPS, TILE, QUAD), lambda i: (i, 0, 0))
    return pl.pallas_call(
        trimmed(functools.partial(regroup_small_kernel, count), count, len(after)),
        grid=(5,),
        in_specs=[pl.BlockSpec((24, TILE * TILE), lambda i: (i, 0))] * count + anywhere(after),
        out_specs=[out_spec] * count,
        out_shape=[shaped(shape, jnp.float32)] * count,
        scratch_shapes=[
            pltpu.VMEM((flat_rows(24), LANES), jnp.float32),
            pltpu.VMEM((TILE, LANES), jnp.float32),
        ],
        compiler_params=params(),
    )(*arrays, *after)


def regroup_weights_kernel(tiles, out, w_edge, e_src, e_dst, e_edge, e_mid, e_out, flat, pair):
    regroup_small_kernel(1, tiles, out, flat, pair)
    step = pl.program_id(0)

    @pl.when(step == 0)
    def _():
        for index in range(6):
            block, side = index // 2, index % 2
            w_edge[block * TILE : (block + 1) * TILE, side * QUAD : (side + 1) * QUAD] = out[
                index
            ].astype(LOW)

    for condition, ref, first, amount, start in (
        (step == 1, e_src, 0, 8, 0), (step == 2, e_dst, 0, 8, 0), (step == 3, e_edge, 0, 3, 0),
        (step == 3, e_mid, 3, 3, 0), (step == 3, e_out, 6, 2, 0), (step == 4, e_out, 0, 1, 2),
    ):

        @pl.when(condition)
        def _():
            for index in range(amount):
                here = slice((start + index) * TILE, (start + index + 1) * TILE)
                ref[here] = out[first + index].astype(LOW)


def regroup_weights(weights):
    shapes = [(DE, D), (D, WIDE), (D, WIDE)] + [(DE, WIDE)] * 3
    return pl.pallas_call(
        regroup_weights_kernel,
        grid=(5,),
        in_specs=[pl.BlockSpec((24, TILE * TILE), lambda i: (i, 0))],
        out_specs=[pl.BlockSpec((SPAN_GROUPS, TILE, QUAD), lambda i: (i, 0, 0))]
        + [kept(shape) for shape in shapes],
        out_shape=[shaped((5 * SPAN_GROUPS, TILE, QUAD), jnp.float32)]
        + [shaped(shape, LOW) for shape in shapes],
        scratch_shapes=[
            pltpu.VMEM((flat_rows(24), LANES), jnp.float32),
            pltpu.VMEM((TILE, LANES), jnp.float32),
        ],
        compiler_params=params(),
    )(weights)


def regroup_big_kernel(count, *refs):
    tiles, outs = refs[0:count], refs[count : 2 * count]
    flat, pair = refs[-2:]
    for ref, out in zip(tiles, outs):
        load_flat(ref, flat)
        for index, group in enumerate(group_list(0, 24, 4)):
            out[index] = group_in(flat, pair, group)


def regroup_big(arrays, after=()):
    count = len(arrays)
    return pl.pallas_call(
        trimmed(functools.partial(regroup_big_kernel, count), count, len(after)),
        in_specs=[pl.BlockSpec(memory_space=pltpu.VMEM)] * count + anywhere(after),
        out_shape=[shaped((6, TILE, QUAD), jnp.float32)] * count,
        scratch_shapes=[
            pltpu.VMEM((flat_rows(24), LANES), jnp.float32),
            pltpu.VMEM((TILE, LANES), jnp.float32),
        ],
        compiler_params=params(),
    )(*arrays, *after)


def soap_groups(grads, weights, firsts, seconds, lefts, rights, rates):
    count = range(len(grads))
    lane = lax.broadcasted_iota(jnp.int32, (TILE, QUAD), 1) // TILE
    masks = [jnp.where(lane == k, 1.0, 0.0) for k in range(4)]
    low_masks = [mask.astype(LOW) for mask in masks]

    def diagonal(values):
        return jnp.concatenate([values * mask for mask in low_masks], axis=0)

    def thrice(product_of, values, sides):
        parts = [split_low(v) for v in values]
        both = [product_of(jnp.concatenate(parts[i], axis=0), sides[i][0]) for i in count]
        rest = [product_of(parts[i][0], sides[i][1]) for i in count]
        return [both[i][0:TILE] + both[i][TILE:] + rest[i] for i in count]

    right_sides = [[diagonal(part) for part in split_low(v)] for v in rights]
    left_parts = [split_low(v) for v in lefts]
    left_sides = [jnp.concatenate([high, low, high], axis=0) for high, low in left_parts]
    half = [split_low(v) for v in thrice(dot, grads, right_sides)]
    half = [jnp.concatenate([high, high, low], axis=0) for high, low in half]
    full = [dot_rows(left_sides[i], half[i]) for i in count]
    turned = [sum(v[TILE * k : TILE * (k + 1)] * masks[k] for k in range(4)) for v in full]
    new_one = [BETA_ONE * firsts[i] + (1.0 - BETA_ONE) * turned[i] for i in count]
    new_two = [
        BETA_TWO * seconds[i] + (1.0 - BETA_TWO) * turned[i] * turned[i] for i in count
    ]
    fix_one = 1.0 / (1.0 - BETA_ONE**STEP)
    fix_two = 1.0 / (1.0 - BETA_TWO**STEP)
    steps = [
        new_one[i] * fix_one / (jnp.sqrt(new_two[i] * fix_two) + EPS_ADAM) for i in count
    ]
    sides = [diagonal(v.astype(LOW)) for v in steps]
    half = [dot(left_parts[i][0], sides[i]).astype(LOW) for i in count]
    restored = [dot_turned(half[i], right_sides[i][0]) for i in count]
    new = [
        weights[i] - rates[i] * (restored[i] + DECAY * weights[i]) for i in count
    ]
    return new_one, new_two, new


TOGETHER = 5
EARLY_ROWS = 1664


def block_rate(block):
    middle = (2 * D + DE) ** (-0.5)
    return jnp.where(
        block < 16,
        middle,
        jnp.where(
            block < 24,
            D ** (-0.5),
            jnp.where(block < 32, 2.5 * D ** (-0.5), jnp.where(block < 64, D ** (-0.5), FF ** (-0.5))),
        ),
    )


def small_rates():
    middle = (2 * D + DE) ** (-0.5)
    return [middle] * 19 + [DE ** (-0.5)] * 3 + [1.5 * DE ** (-0.5)] * 3


NORM_ROWS = 19


def soap_early_kernel(scale, place, grads, rates, weight, first, second, left, right, *refs):
    norms, outs = refs[0:3], refs[3:9]
    flats, pairs = refs[9:12], refs[12]
    step = pl.program_id(0)
    core, batch = place[1], place[2]
    piece = EARLY_ROWS // 8

    def rows_of(begin, end):
        parts = []
        while begin < end:
            index, offset = begin // piece, begin % piece
            amount = min(end - begin, piece - offset)
            parts.append(grads[index // 4 ^ core, index % 4 ^ batch, offset : offset + amount, :])
            begin += amount
        value = parts[0] if len(parts) == 1 else jnp.concatenate(parts, axis=0)
        return value.astype(jnp.float32) * scale

    def groups(start, amount):
        here = range(amount)
        state = [[ref[i] for i in here] for ref in (weight, first, second, left, right)]
        results = soap_groups(
            [rows_of((start + i) * TILE, (start + i + 1) * TILE) for i in here],
            *state,
            [rates[start + i : start + i + 1] for i in here],
        )
        for spot in here:
            tiles = list(range(spot * 3, spot * 3 + 3))
            for kind, flat in enumerate(flats):
                group_out(results[kind][spot], flat, pairs.at[kind * SPAN_GROUPS + spot], tiles)

    for index, amount in enumerate((8, 8, 8, 1)):

        @pl.when(step == index)
        def _():
            groups(8 * index, amount)

    @pl.when(step == 0)
    def _():
        rows = rows_of(25 * TILE, 25 * TILE + 32)[0:NORM_ROWS, 0:LANES]
        results = adam_step(*(ref[...] for ref in norms), rows)
        for ref, value in zip(outs[3:6], (results[2], results[0], results[1])):
            ref[...] = value

    for ref, flat in zip(outs[0:3], flats):
        store_flat(ref, flat)


def soap_early(scale, place, grads, state, norms):
    out = shaped((99, TILE * TILE), jnp.float32)
    line = shaped((NORM_ROWS, LANES), jnp.float32)
    rates = jnp.asarray(np.repeat(np.array(small_rates(), np.float32)[:, None], QUAD, axis=1))
    return pl.pallas_call(
        functools.partial(soap_early_kernel, scale),
        grid=(4,),
        in_specs=[pl.BlockSpec(memory_space=pltpu.SMEM), whole(grads.shape), whole(rates.shape)]
        + [pl.BlockSpec((SPAN_GROUPS, TILE, QUAD), lambda i: (1 + i, 0, 0))] * 5
        + [whole(line.shape)] * 3,
        out_specs=[pl.BlockSpec((24, TILE * TILE), lambda i: (1 + i, 0))] * 3
        + [kept(line.shape)] * 3,
        out_shape=[out, out, out, line, line, line],
        scratch_shapes=[pltpu.VMEM((flat_rows(24), LANES), jnp.float32)] * 3
        + [pltpu.VMEM((3 * SPAN_GROUPS, TILE, LANES), jnp.float32)],
        compiler_params=params(),
    )(place, grads, rates, *state, *norms)


def soap_late_kernel(scale, place, own, other_one, other_two, other_three, *refs):
    state, v_state = refs[0:5], refs[5:10]
    older = refs[12]
    one, two, new, low, v_one, v_two, v_new, v_low = refs[13:21]
    flats, v_flats, pairs, shared_of = refs[21:24], refs[24:27], refs[27], refs[28]
    chip, core, batch = place[0], place[1], place[2]
    groups = group_list(0, 24, 4)
    received = (own, other_one, other_two, other_three)
    for shift, ref in enumerate(received):
        shared_of[shift, 4 * OWNED_ROWS :, :] = ref[4 * OWNED_ROWS :, :]

    def v_block(block, side):
        parts = []
        for part in (2 * side, 2 * side + 1):
            rows = []
            for begin in range(block * TILE, (block + 1) * TILE, TILE // 2):
                half, offset = begin // (DE // 2), begin % (DE // 2)
                first = 4 * OWNED_ROWS + (half ^ core) * (DE // 2) + offset
                rows.append(shared_of[part ^ batch, pl.ds(pl.multiple_of(first, 32), TILE // 2), :])
            parts.append(jnp.concatenate(rows, axis=0))
        return jnp.concatenate(parts, axis=1).astype(jnp.float32)

    def own_part(block, part):
        rows = slice(block * TILE, (block + 1) * TILE)
        shifted = slice(part * OWNED_ROWS + rows.start, part * OWNED_ROWS + rows.stop)
        total = tree_sum([ref[shifted, :].astype(jnp.float32) for ref in received])
        return jnp.where(batch == 0, received[part][rows, :].astype(jnp.float32), total)

    def own_block(block, side):
        return jnp.concatenate([own_part(block, 2 * side), own_part(block, 2 * side + 1)], axis=1)

    first = batch * 24 + (chip * 2 + core) * 3
    own_rates = [block_rate(first + i // 2) for i in range(6)]
    v_rates = [(2 * D + DE) ** (-0.5)] * 6
    for grad_of, values, rates, targets, base in (
        (own_block, state, own_rates, flats, 0),
        (v_block, v_state, v_rates, v_flats, 18),
    ):
        here = range(6)
        grads = [grad_of(i // 2, i % 2) * scale for i in here]
        results = soap_groups(grads, *[[ref[i] for i in here] for ref in values], rates)
        for index in here:
            for kind, flat in enumerate(targets):
                group_out(results[kind][index], flat, pairs.at[base + kind * 6 + index], groups[index])
    for ref, flat in zip((one, two, new, v_one, v_two, v_new), (*flats, *v_flats)):
        store_flat(ref, flat)
    low[...] = new[...].astype(LOW)
    v_low[...] = jnp.concatenate([v_new[...], older[24:]], axis=0).astype(LOW)


def soap_late(scale, place, received, state, v_state, early):
    out = shaped((24, TILE * TILE), jnp.float32)
    small = shaped(early[0].shape, jnp.float32)
    front = pl.BlockSpec((24, TILE * TILE), lambda i: (0, 0))
    group = whole((6, TILE, QUAD))
    flat = pltpu.VMEM((flat_rows(24), LANES), jnp.float32)
    return pl.pallas_call(
        functools.partial(soap_late_kernel, scale),
        grid=(1,),
        in_specs=[
            pl.BlockSpec(memory_space=pltpu.SMEM),
        ]
        + [whole(v.shape) for v in received]
        + [group] * 10
        + [pl.BlockSpec(memory_space=pl.ANY)] * 2
        + [whole(small.shape)],
        out_specs=[front] * 7 + [whole(small.shape)],
        out_shape=[out, out, out, shaped((24, TILE * TILE), LOW), small, small, small]
        + [shaped(small.shape, LOW)],
        scratch_shapes=[flat] * 6
        + [pltpu.VMEM((36, TILE, LANES), jnp.float32), pltpu.VMEM((4, *received[0].shape), LOW)],
        input_output_aliases={15: 4, 16: 5, 17: 6},
        compiler_params=params(),
    )(place, *received, *state, *v_state, *early)


def swap_core(values):
    return lax.ppermute(values, "core", [(0, 1), (1, 0)])


def swap_chip(values, shift):
    chips = lax.axis_size("chip")
    return lax.ppermute(values, "chip", [(i, i ^ shift) for i in range(chips)])


def gate(values, others):
    return lax.optimization_barrier((values, others))[0]


def send_pieces(values):
    chips = lax.axis_size("chip")
    return [values] + [swap_chip(values, shift) for shift in range(1, chips)]


def gather_pieces(values, fill=()):
    return swap_pieces(send_pieces(values), fill)


def swap_pieces(parts, fill=()):
    parts = gate(parts, fill)
    return [half for part in parts for half in (part, swap_core(part))]


def reduce_pieces(even, odd):
    return send_near(add_halves(even, swap_core(odd)))


def send_near(near):
    return [near[0]] + [swap_chip(near[shift], shift) for shift in range(1, len(near))]


def swap_batch(values, shift):
    return lax.ppermute(values, "batch", [(i, i ^ shift) for i in range(4)])


def pick(values, index):
    return lax.dynamic_index_in_dim(values, index, 0, keepdims=False)


def tree_sum(parts):
    while len(parts) > 1:
        parts = [parts[i] + parts[i + 1] for i in range(0, len(parts), 2)]
    return parts[0]


def wide_values(values):
    return values.astype(jnp.float32)


def gather_first(place, quarters, x, batch, fill):
    pieces = [x] + [swap_chip(x, shift) for shift in range(1, 4)]
    sent = [
        lax.ppermute(quarters[index], "batch", [(0, index)]) for index in range(1, 4)
    ]
    quarter = jnp.where(batch == 0, quarters[0], sent[0] + sent[1] + sent[2])
    lines = jnp.stack([quarter] + [swap_chip(quarter, shift) for shift in range(1, 4)])
    lines = gate(lines, fill)
    parts = [lines] + [swap_batch(lines, shift) for shift in range(1, 4)]
    pieces = [half for piece in pieces for half in (piece, swap_core(piece))]
    return assemble(place, parts + [swap_core(part) for part in parts], pieces)


def reduce_small(near):
    total = near[0]
    for shift in range(1, 4):
        total = total + wide_values(swap_batch(near[shift], shift))
    total = total.astype(LOW)
    others = [total] + [swap_chip(total, shift) for shift in range(1, 4)]
    return total, tree_sum([wide_values(v) for v in others]).astype(LOW)


def share_small(total, token):
    others = [total] + gate([swap_batch(total, shift) for shift in range(1, 4)], token)
    parts = jnp.stack(others)
    return jnp.stack([parts, swap_core(parts)])


def reduce_late(near, early, batch, fill, third, other):
    received = [swap_batch(near[shift], shift) for shift in range(1, 4)]
    received = gate(received, fill)
    total = near[0] + sum(wide_values(part) for part in received)
    shared = total[4 * OWNED_ROWS :]
    lines = [total[OWNED_ROWS * i : OWNED_ROWS * (i + 1)] for i in range(4)]
    sent = [
        jnp.concatenate([lines[shift], shared], axis=0).astype(LOW) for shift in range(1, 4)
    ]
    received = [swap_chip(part, shift) for shift, part in enumerate(sent, 1)]
    quarter = lines[0]
    shares = [wide_values(shared.astype(LOW))]
    for part in received:
        got = wide_values(part)
        quarter = quarter + got[0:OWNED_ROWS]
        shares.append(got[OWNED_ROWS:])
    shared = tree_sum(shares).astype(LOW)
    shared = jnp.concatenate([shared, swap_core(shared)], axis=0)
    quarter = jnp.pad(quarter.astype(LOW)[None], ((0, 3), (0, 0), (0, 0)))

    def outgoing(target):
        block = jnp.where(target == 0, quarter, pick(early, jnp.maximum(target - 1, 0)))
        return jnp.concatenate([block.reshape(4 * OWNED_ROWS, LANES), shared], axis=0)

    sent = gate([outgoing(batch ^ shift) for shift in range(4)], third)
    received = [swap_batch(part, shift) for shift, part in enumerate(sent) if shift]
    received = gate([sent[0]] + received, other)
    return received


def pad_to(matrix, height, breadth):
    return jnp.pad(matrix, ((0, height - matrix.shape[0]), (0, breadth - matrix.shape[1])))


def norm_rows(vector):
    return vector.reshape(NORM_ROWS, LANES)


def norm_vector(rows):
    return rows.reshape(-1)


def gather_plain(tiles, every):
    amount = tiles.shape[0]
    unit = math.gcd(amount, D // TILE)
    local = tiles.astype(LOW).reshape(amount // unit, unit, TILE, TILE)
    local = local.transpose(0, 2, 1, 3).reshape(amount // unit, TILE, unit * TILE)
    units = lax.all_gather(local, every, axis=0, tiled=True)
    blocks = units.reshape(-1, D // TILE // unit, TILE, unit * TILE).transpose(0, 2, 1, 3)
    blocks = blocks.reshape(-1, TILE, D)
    return blocks[0:24].reshape(3 * D, D), blocks


def soap_plain(weight, moment_one, moment_two, left, right, gradient, rates):
    left, right = as_square(left), as_square(right)
    high = lax.Precision.HIGHEST
    turned = jnp.einsum("tji,tjk->tik", left, gradient, precision=high)
    turned = jnp.einsum("tik,tkl->til", turned, right, precision=high)
    new_one = BETA_ONE * as_square(moment_one) + (1.0 - BETA_ONE) * turned
    new_two = BETA_TWO * as_square(moment_two) + (1.0 - BETA_TWO) * turned * turned
    direction = (
        new_one / (1.0 - BETA_ONE**STEP) / (jnp.sqrt(new_two / (1.0 - BETA_TWO**STEP)) + EPS_ADAM)
    )
    restored = jnp.einsum("tij,tjk->tik", left, direction, precision=high)
    restored = jnp.einsum("tik,tlk->til", restored, right, precision=high)
    weight = as_square(weight)
    new = weight - rates[:, None, None] * (restored + DECAY * weight)
    return as_flat(new_one), as_flat(new_two), as_flat(new)


def update_plain(g_late, g_early, g_small, every, scale, big, small, norms):
    amount = big[0].shape[0]
    unit = math.gcd(amount, D // TILE)
    g_late, g_small = jnp.stack(g_late), jnp.stack(g_small).reshape(EARLY_ROWS, WIDE)
    late = g_late[:, :, 0 : 4 * OWNED_ROWS].reshape(2, 4, 4, OWNED_ROWS, LANES)
    late = late.transpose(2, 0, 3, 1, 4).reshape(24, TILE, D)
    w_edge = g_late[:, :, 4 * OWNED_ROWS :].transpose(0, 2, 1, 3).reshape(DE, D)
    early = g_early.reshape(8, 3, 4, 3, TILE, LANES).transpose(1, 0, 3, 4, 2, 5)
    early = early.reshape(72, TILE, D)
    grads = jnp.concatenate([late, early], axis=0)
    grads = grads.reshape(-1, TILE, D // TILE // unit, unit * TILE).transpose(0, 2, 1, 3)
    own = lax.psum_scatter(
        grads.reshape(-1, TILE, unit * TILE), every, scatter_dimension=0, tiled=True
    )
    own = wide_values(own).reshape(amount // unit, TILE, unit, TILE).transpose(0, 2, 1, 3)
    own = own.reshape(amount, TILE, TILE) * scale
    w_edge, g_small = lax.psum((wide_values(w_edge), wide_values(g_small)), every)
    strips = g_small[0:1600, 0:DE].reshape(25, TILE, 3, TILE).transpose(0, 2, 1, 3)
    tiles = jnp.concatenate(
        [as_square(to_flat_tiles(w_edge)), strips.reshape(75, TILE, TILE)], axis=0
    )
    first = lax.axis_index(every) * amount
    rates = lax.dynamic_slice_in_dim(
        jnp.asarray(rate_table(big_shapes(), big_spreads())), first, amount
    )
    big_new = soap_plain(*big, own, rates)
    rates = jnp.asarray(rate_table(small_shapes(), small_spreads()))
    small_new = soap_plain(*small, tiles * scale, rates)
    norm_new = adam_step(*norms, norm_vector(g_small[1600:1619, 0:LANES]) * scale)
    return big_new, small_new, norm_new


def body(
    node,
    edge,
    dest_device,
    dest_local,
    node_valid,
    node_cot,
    edge_cot,
    big_weight,
    big_first,
    big_second,
    big_left,
    big_right,
    small_weight,
    small_first,
    small_second,
    small_left,
    small_right,
    norm_params,
    norm_first,
    norm_second,
):
    chips = lax.axis_size("chip")
    every = ("batch", "chip", "core")
    shards = 2 * chips
    owned = node.shape[1]
    nodes = owned * shards
    rows = owned * K
    complexes = node.shape[0] * lax.axis_size("batch")
    tuned = chips == 4 and lax.axis_size("batch") == 4 and big_weight.shape[0] == 24
    chip, core, batch = (lax.axis_index(axis) for axis in ("chip", "core", "batch"))
    grad_scale = 1.0 / math.sqrt(complexes * nodes * K)
    x = node[0]
    big_state = (big_weight, big_first, big_second, big_left, big_right)
    small_state = (small_weight, small_first, small_second, small_left, small_right)
    norm_state = (norm_params, norm_first, norm_second)

    place = jnp.stack([chip, core, batch]).astype(jnp.int32) * int(tuned)
    small_groups, w_edge, e_src, e_dst, e_edge, e_mid, e_out = regroup_weights(small_weight)
    small_groups = [small_groups]
    norms = norm_params[0 : 4 * D].reshape(4, D)
    edge_norms = pad_to(norm_params[4 * D :].reshape(2, DE), 8, WIDE)
    valid = node_valid[0].astype(jnp.float32).reshape(owned, 1)
    me = chip * 2 + core
    relative = (dest_device[0].reshape(1, rows) ^ me) * owned + dest_local
    edge_across = edge[0].T
    if tuned:
        own, *quarters = own_rows(big_weight)
        blocks = lax.all_gather(own, every, axis=0, tiled=True).reshape(-1, TILE, D)
        w_rows, x_all = gather_first(
            place, quarters, x, batch, (w_edge, relative)
        )
    else:
        w_rows, blocks = gather_plain(big_weight, every)
        x_all = jnp.concatenate(gather_pieces(x), axis=0)

    even, odd, hidden, slope_one, slope_two, tall = message_forward(
        relative, edge_across, valid, x_all, owned, w_rows, w_edge, ()
    )
    sums = reduce_pieces(even, odd)
    if tuned:
        small_groups += regroup_small(small_state[1:5], (even,))
    node_low, q_src, q_dst, inside, one, act, slope, summed, scale, sums = node_forward(
        x, valid, blocks, e_src, e_dst, norms, sums, small_groups[1:2]
    )
    big_groups = list(regroup_big(big_state, (q_dst,))) if tuned else []
    q_pieces = gather_pieces(q_dst, big_groups[0:1])
    (
        edge_new, part_edge, even, odd, d_q_src, g_e_edge, g_e_mid, g_e_out, g_e_norms,
    ) = edge_phase(
        tall, edge_across, edge_cot[0].T, q_pieces, q_src, e_edge, e_mid, e_out, edge_norms, (),
    )
    d_q_dst = reduce_pieces(even, odd)
    reply, d_inside, g_early, *g_small = node_backward(
        place,
        [
            node_cot[0], d_q_src, node_low, summed, one, inside, act, slope, scale, sums,
            blocks, e_src, e_dst, norms, g_e_edge, g_e_mid, g_e_out, g_e_norms,
        ],
        d_q_dst,
        (),
    )
    replies = send_pieces(reply)
    held = ()
    if tuned:
        near_small = gate(add_halves(g_small[0], swap_core(g_small[1])), replies[1])
        part_small, small_sum = reduce_small(near_small)
        held = (part_small,)
    replies = swap_pieces(replies, held)
    d_edges, even, odd, d_p_src, *g_late = message_backward(
        place, tall, edge_across, hidden, slope_one, slope_two, part_edge, x_all, w_rows, w_edge, replies, held,
    )
    near_p = add_halves(even, swap_core(odd))
    d_p_dst = send_near(near_p)
    d_features = node_gradient(d_inside, d_p_src, w_rows, d_p_dst)

    if tuned:
        norm_groups = [norm_rows(v) for v in norm_state]
        late_groups = small_groups
        early = lax.psum_scatter(
            gate(g_early, replies), ("chip", "core"), scatter_dimension=0, tiled=True
        )
        early = early.reshape(3, 4, OWNED_ROWS, LANES)
        near_late = add_halves(g_late[0], swap_core(gate(g_late[1], small_sum)))
        small_sum = share_small(small_sum, near_late[0])
        *early_new, norm_new, norm_one, norm_two = soap_early(
            grad_scale, place, small_sum, small_groups, norm_groups
        )
        mine = reduce_late(near_late, early, batch, early_new[0], d_p_dst[1], d_features)
        big_one, big_two, big_new, big_low, small_one, small_two, small_new, small_low = soap_late(
            grad_scale, place, mine, big_groups, late_groups, early_new
        )
        norm_one, norm_two, norm_new = (norm_vector(v) for v in (norm_one, norm_two, norm_new))
    else:
        (
            (big_one, big_two, big_new),
            (small_one, small_two, small_new),
            (norm_one, norm_two, norm_new),
        ) = update_plain(
            g_late, g_early, g_small, every, grad_scale, big_state, small_state, norm_state
        )
        big_low = big_new.astype(LOW)
        small_low = small_new.astype(LOW)
    return (
        node_low[None],
        edge_new.T[None],
        d_features[None],
        d_edges.T[None],
        big_one,
        big_two,
        big_new,
        big_low,
        small_one,
        small_two,
        small_new,
        small_low,
        norm_one,
        norm_two,
        norm_new,
    )


def solution(mesh):
    batch, shards = mesh.devices.shape
    fine = Mesh(mesh.devices.reshape(batch, shards // 2, 2), ("batch", "chip", "core"))
    edge = ("chip", "core")
    every = ("batch", "chip", "core")
    placed = (
        P("batch", edge, None),
        P("batch", edge, None),
        P("batch", edge, None),
        P("batch", edge),
        P("batch", edge),
        P("batch", edge, None),
        P("batch", edge, None),
        P(every, None),
        P(every, None),
        P(every, None),
        P(every, None),
        P(every, None),
        P(),
        P(),
        P(),
        P(),
        P(),
        P(),
        P(),
        P(),
    )
    return jax.shard_map(
        body,
        mesh=fine,
        in_specs=placed,
        out_specs=(
            P("batch", edge, None),
            P("batch", edge, None),
            P("batch", edge, None),
            P("batch", edge, None),
            P(every, None),
            P(every, None),
            P(every, None),
            P(every, None),
            P(),
            P(),
            P(),
            P(),
            P(),
            P(),
            P(),
        ),
        check_vma=False,
    )
```

```python
import functools
import math

import jax
import jax.numpy as jnp
import numpy as np
from jax import lax
from jax.experimental import pallas as pl
from jax.experimental.pallas import tpu as pltpu
from jax.sharding import Mesh
from jax.sharding import PartitionSpec as P

D = 512
DE = 192
FF = 2048
K = 60
TILE = 64
STEP = 10


BETA_ONE = 0.5
BETA_TWO = 0.5
EPS_ADAM = 1e-08
EPS_NORM = 1e-05
DECAY = 0.01
NORM_RATE = 0.4
PRECISION_HIGH = lax.Precision.HIGHEST


def big_shapes():
    return [(D, D), (D, D), (D, D), (D, D), (D, FF), (FF, D)]


def small_shapes():
    return [(DE, D), (D, DE), (D, DE), (DE, DE), (DE, DE), (DE, DE)]


def big_spreads():
    middle = (2 * D + DE) ** (-0.5)
    return [middle, middle, D ** (-0.5), 2.5 * D ** (-0.5), D ** (-0.5), FF ** (-0.5)]


def small_spreads():
    middle = (2 * D + DE) ** (-0.5)
    return [middle, middle, middle, middle, DE ** (-0.5), 1.5 * DE ** (-0.5)]


def rate_table(shapes, spreads):
    amounts = [height // TILE * (breadth // TILE) for height, breadth in shapes]
    return np.repeat(np.array(spreads, np.float32), amounts)


def as_square(flat_tiles):
    return flat_tiles.reshape(flat_tiles.shape[0], TILE, TILE)


def as_flat(square_tiles):
    return square_tiles.reshape(square_tiles.shape[0], TILE * TILE)


def from_tiles(tile_stack, shapes):
    matrices = []
    offset = 0
    for height, breadth in shapes:
        amount = height // TILE * (breadth // TILE)
        blocked = tile_stack[offset : offset + amount].reshape(
            height // TILE, breadth // TILE, TILE, TILE
        )
        matrices.append(blocked.transpose(0, 2, 1, 3).reshape(height, breadth))
        offset += amount
    return matrices


def to_flat_tiles(matrix):
    height, breadth = matrix.shape
    blocked = matrix.reshape(height // TILE, TILE, breadth // TILE, TILE)
    return blocked.transpose(0, 2, 1, 3).reshape(-1, TILE * TILE)


def adam_step(params, moment_one, moment_two, gradient):
    new_one = BETA_ONE * moment_one + (1.0 - BETA_ONE) * gradient
    new_two = BETA_TWO * moment_two + (1.0 - BETA_TWO) * gradient * gradient
    direction = (
        new_one / (1.0 - BETA_ONE**STEP) / (jnp.sqrt(new_two / (1.0 - BETA_TWO**STEP)) + EPS_ADAM)
    )
    return (new_one, new_two, params - NORM_RATE * direction)


def times_transposed(left_side, right_side):
    return lax.dot_general(
        left_side, right_side, (((1,), (1,)), ((), ())), preferred_element_type=jnp.float32
    )


LOW = jnp.bfloat16
WIDE = 256
GELU_A = math.sqrt(2.0 / math.pi)
GELU_B = GELU_A * 0.044715
OWNED_ROWS = 3 * TILE


def dot(left, right):
    return jnp.dot(left, right, preferred_element_type=jnp.float32)


def dot_rows(left, right):
    return lax.dot_general(
        left, right, (((0,), (0,)), ((), ())), preferred_element_type=jnp.float32
    )


def dot_turned(left, right):
    return lax.dot_general(
        left, right, (((1,), (1,)), ((), ())), preferred_element_type=jnp.float32
    )


def split_low(values):
    high = values.astype(LOW)
    return high, (values - high.astype(jnp.float32)).astype(LOW)


def gelu_pair(v):
    square = v * v
    half = 0.5 * jnp.tanh(v * (GELU_A + GELU_B * square)) + 0.5
    out = v * half
    slope = half + out * (1.0 - half) * (2.0 * GELU_A + 6.0 * GELU_B * square)
    return out, slope


def norm_parts(values, width):
    centre = jnp.sum(values, axis=-1, keepdims=True) * (1.0 / width)
    centered = values - centre
    if values.shape[-1] != width:
        lane = lax.broadcasted_iota(jnp.int32, values.shape, 1)
        centered = jnp.where(lane < width, centered, 0.0)
    spread = jnp.sum(centered * centered, axis=-1, keepdims=True) * (1.0 / width)
    inverse = lax.rsqrt(spread + EPS_NORM)
    return centered * inverse, inverse


def norm_back(scaled, inverse, gain, upstream, width):
    inner = upstream * gain
    mean_inner = jnp.sum(inner, axis=-1, keepdims=True) * (1.0 / width)
    mean_cross = jnp.sum(inner * scaled, axis=-1, keepdims=True) * (1.0 / width)
    return inverse * (inner - mean_inner - scaled * mean_cross)


def whole(shape):
    return pl.BlockSpec(shape, lambda *_: (0,) * len(shape), pipeline_mode=pl.Buffered(1))


def anywhere(values):
    return [pl.BlockSpec(memory_space=pl.ANY)] * len(values)


def kept(shape):
    return pl.BlockSpec(shape, lambda *_: (0,) * len(shape))


def params(limit=58):
    return pltpu.CompilerParams(vmem_limit_bytes=limit * 2**20)


def shaped(shape, dtype):
    return jax.ShapeDtypeStruct(shape, dtype)


def trimmed(kernel, inputs, unread):
    def run(*refs):
        kernel(*refs[:inputs], *refs[inputs + unread :])

    return run


def target_columns(targets, nodes):
    down = lax.broadcasted_iota(jnp.int32, (nodes, targets.shape[1]), 0)
    return jnp.where(down == targets, 1.0, 0.0).astype(LOW)


def source_mask(block):
    row = lax.broadcasted_iota(jnp.int32, (WIDE - DE, block), 0)
    source = lax.broadcasted_iota(jnp.int32, (WIDE - DE, block), 1) // K
    return jnp.where((row == source) | (row == source + block // K), 1.0, 0.0)


def block_of():
    return 32 * K


def lanes(height, block):
    return pl.BlockSpec((height, block), lambda i: (0, i))


def tall_lanes(nodes, block):
    buffers = pl.Buffered(2 if nodes <= 1024 else 1)
    return pl.BlockSpec((nodes, block), lambda i: (0, i), pipeline_mode=buffers)


def source_rows(values):
    high = values.astype(LOW).astype(jnp.float32)
    return jnp.concatenate([high, values - high], axis=0).astype(LOW)


def put_halves(halves, total, owned):
    for index in range(total.shape[0] // owned):
        rows = total[index * owned : (index + 1) * owned].astype(LOW)
        halves[index % 2][index // 2, 0:owned, :] = rows


COUNT_ROWS = 16


def message_kernel(
    targets, edge, valid, w_rows, w_edge, x_all,
    even, odd, hidden_out, slope_one, slope_two, tall,
    table, mixed, from_source, total, mid, counts, wide,
):
    step = pl.program_id(0)
    owned = from_source.shape[0]

    @pl.when(step == 0)
    def _():
        table[...] = dot(x_all[...], w_rows[D : 2 * D]).astype(LOW).T
        from_source[...] = dot(x_all[0:owned], w_rows[0:D])
        mixed[0:DE] = w_edge[...]
        mid[...] = w_rows[2 * D : 3 * D].T
        wide[DE:WIDE] = source_mask(edge.shape[1]).astype(LOW)
        total[...] = jnp.zeros_like(total)
        counts[...] = jnp.zeros_like(counts)

    nodes, block = tall.shape
    group = block // K
    wide[0:DE] = edge[...]
    tall[...] = target_columns(targets[...], nodes)
    mixed[DE:WIDE] = source_rows(from_source[pl.ds(step * group, group), :])
    pre = dot(table[...], tall[...]) + dot_rows(mixed[...], wide[...])
    hidden, slope = gelu_pair(pre)
    hidden = hidden.astype(LOW)
    hidden_out[...] = hidden
    slope_one[...] = slope.astype(LOW)
    second, slope = gelu_pair(dot(mid[...], hidden))
    ok = jnp.sum(source_mask(block)[0:group] * valid[...], axis=0, keepdims=True)
    slope_two[...] = (slope * ok).astype(LOW)
    total[...] += dot_turned(tall[...], (second * ok).astype(LOW))
    ok_rows = jnp.broadcast_to(ok, (COUNT_ROWS, ok.shape[1])).astype(LOW)
    counts[...] += dot_turned(ok_rows, tall[...])

    @pl.when(step == pl.num_programs(0) - 1)
    def _():
        put_halves((even, odd), total, owned)
        for index in range(total.shape[0] // owned):
            amount = counts[:, index * owned : (index + 1) * owned]
            high = jnp.floor(amount * (1.0 / LANES))
            place = (even, odd)[index % 2].at[index // 2]
            rows = pl.ds(owned, COUNT_ROWS)
            place[rows, :] = jnp.zeros((COUNT_ROWS, D), LOW)
            place[rows, 0:owned] = high.astype(LOW)
            place[rows, LANES : LANES + owned] = (amount - high * LANES).astype(LOW)


def message_forward(targets, edge, valid, x_all, owned, w_rows, w_edge, after):
    nodes, rows = x_all.shape[0], targets.shape[1]
    block = block_of()
    half = (nodes // owned // 2, owned + COUNT_ROWS, D)
    return pl.pallas_call(
        trimmed(message_kernel, 6, len(after)),
        grid=(rows // block,),
        in_specs=[
            lanes(1, block),
            lanes(DE, block),
            pl.BlockSpec((block // K, 1), lambda i: (i, 0)),
            whole((3 * D, D)),
            whole((DE, D)),
            whole((nodes, D)),
        ]
        + anywhere(after),
        out_specs=[kept(half), kept(half)] + [lanes(D, block)] * 3 + [tall_lanes(nodes, block)],
        out_shape=[shaped(half, LOW)] * 2
        + [shaped((D, rows), LOW)] * 3
        + [shaped((nodes, rows), LOW)],
        scratch_shapes=[
            pltpu.VMEM((D, nodes), LOW),
            pltpu.VMEM((WIDE, D), LOW),
            pltpu.VMEM((owned, D), jnp.float32),
            pltpu.VMEM((nodes, D), jnp.float32),
            pltpu.VMEM((D, D), LOW),
            pltpu.VMEM((COUNT_ROWS, nodes), jnp.float32),
            pltpu.VMEM((WIDE, block), LOW),
        ],
        compiler_params=params(),
    )(targets, edge, valid, w_rows, w_edge, x_all, *after)


def up_part(blocks, part):
    per, parts = D // TILE, FF // D
    strips = [blocks[4 * per + row * parts + part] for row in range(per)]
    return jnp.concatenate(strips, axis=0)


def out_part(blocks):
    per = D // TILE
    return blocks[3 * per : 4 * per].reshape(D, D)


def down_part(blocks, part):
    per = D // TILE
    first = per * (4 + FF // D + part)
    return blocks[first : first + per].reshape(D, D)


def node_forward_kernel(x, valid, blocks, u_src, u_dst, norms, *refs):
    pieces = refs[:-10]
    (
        low_out, q_src, q_dst, inside_out, one_out, act_out, slope_out, summed_out, scale_out,
        sums_out,
    ) = refs[-10:]
    summed_all = sum(piece[...].astype(jnp.float32) for piece in pieces)
    owned = x.shape[0]
    sums = summed_all[0:owned]
    tally = summed_all[owned : owned + 8, 0:LANES] * float(LANES)
    tally += summed_all[owned : owned + 8, LANES : 2 * LANES]
    amount = tally.T[0:owned, 0:1]
    scale = valid[...] / jnp.maximum(amount * valid[...], 1.0)
    scale_out[...] = scale
    sums_out[...] = sums
    high, low = split_low(sums * scale)
    w_out = out_part(blocks)
    inside = x[...].astype(jnp.float32) + (dot(high, w_out) + dot(low, w_out))
    scaled, _ = norm_parts(inside, D)
    one = scaled * norms[0:1] + norms[1:2]
    one_low = one.astype(LOW)
    narrowed = jnp.zeros_like(one)
    for part in range(FF // D):
        act, slope = gelu_pair(dot(one_low, up_part(blocks, part)))
        act = act.astype(LOW)
        act_out[:, part * D : (part + 1) * D] = act
        slope_out[:, part * D : (part + 1) * D] = slope.astype(LOW)
        narrowed += dot(act, down_part(blocks, part))
    summed = one + narrowed
    scaled, _ = norm_parts(summed, D)
    two = (scaled * norms[2:3] + norms[3:4]).astype(LOW)
    low_out[...] = two
    q_src[...] = dot(two, u_src[...])
    q_dst[...] = dot(two, u_dst[...]).astype(LOW)
    inside_out[...] = inside
    one_out[...] = one
    summed_out[...] = summed


def node_forward(x, valid, blocks, u_src, u_dst, norms, pieces, after):
    owned = x.shape[0]
    wide = shaped((owned, D), jnp.float32)
    operands = [x, valid, blocks, u_src, u_dst, norms, *pieces]
    return pl.pallas_call(
        trimmed(node_forward_kernel, len(operands), len(after)),
        in_specs=[pl.BlockSpec(memory_space=pltpu.VMEM)] * len(operands) + anywhere(after),
        out_shape=[
            shaped((owned, D), LOW),
            shaped((owned, WIDE), jnp.float32),
            shaped((owned, WIDE), LOW),
            wide,
            wide,
            shaped((owned, FF), LOW),
            shaped((owned, FF), LOW),
            wide,
            shaped((owned, 1), jnp.float32),
            wide,
        ],
        compiler_params=params(),
    )(*operands, *after)


def tall_norm(values):
    width = values.shape[0]
    centre = jnp.sum(values, axis=0, keepdims=True) * (1.0 / width)
    centered = values - centre
    spread = jnp.sum(centered * centered, axis=0, keepdims=True) * (1.0 / width)
    inverse = lax.rsqrt(spread + EPS_NORM)
    return centered * inverse, inverse


def tall_norm_back(scaled, inverse, gain, upstream):
    width = scaled.shape[0]
    inner = upstream * gain
    mean_inner = jnp.sum(inner, axis=0, keepdims=True) * (1.0 / width)
    mean_cross = jnp.sum(inner * scaled, axis=0, keepdims=True) * (1.0 / width)
    return inverse * (inner - mean_inner - scaled * mean_cross)


def lane_sums(values):
    return sum(
        values[:, first : first + LANES] for first in range(0, values.shape[1], LANES)
    )


def edge_kernel(count, tall, edge, cot, q_src, u_edge, u_mid, u_out, norms, *refs):
    pieces = refs[0:count]
    (
        edge_out, d_edge, even, odd, d_source, g_edge, g_mid, g_out, g_norms,
        table, mixed, total, mid_turned, out_turned, gain_sum, shift_sum, columns, wide,
    ) = refs[-18:]
    step = pl.program_id(0)
    last = pl.num_programs(0) - 1
    owned = q_src.shape[0]

    @pl.when(step == 0)
    def _():
        table[...] = jnp.concatenate([piece[...] for piece in pieces], axis=0).T
        mixed[0:DE] = u_edge[...]
        mid_turned[...] = u_mid[...].T
        out_turned[...] = u_out[...].T
        columns[...] = norms[...].T
        wide[DE:WIDE] = source_mask(edge.shape[1]).astype(LOW)
        for ref in (total, gain_sum, shift_sum, g_edge, g_mid, g_out):
            ref[...] = jnp.zeros_like(ref)

    group = edge_out.shape[1] // K
    mixed[DE:WIDE] = source_rows(q_src[pl.ds(step * group, group), :])
    wide[0:DE] = edge[...]
    both = wide[...]
    first, slope_one = gelu_pair(
        dot(table[0:DE], tall[...]) + dot(mixed[...].T[0:DE], both)
    )
    first = first.astype(LOW)
    second, slope_two = gelu_pair(dot(mid_turned[0:DE, 0:DE], first))
    second = second.astype(LOW)
    change = dot(out_turned[0:DE, 0:DE], second)
    scaled, inverse = tall_norm(both[0:DE].astype(jnp.float32) + change)
    gain, offset = columns[0:DE, 0:1], columns[0:DE, 1:2]
    edge_out[...] = (scaled * gain + offset).astype(LOW)
    back = cot[...].astype(jnp.float32)
    gain_sum[...] += lane_sums(back * scaled)
    shift_sum[...] += lane_sums(back)
    d_sum = tall_norm_back(scaled, inverse, gain, back)
    d_change = d_sum.astype(LOW)
    g_out[0:DE, 0:DE] += dot_turned(second, d_change)
    d_second = (dot(u_out[:, 0:DE], d_change) * slope_two).astype(LOW)
    g_mid[0:DE, 0:DE] += dot_turned(first, d_second)
    d_first = (dot(u_mid[:, 0:DE], d_second) * slope_one).astype(LOW)
    d_edge[...] = d_sum + dot(u_edge[:, 0:DE], d_first)
    turned = dot_turned(both, d_first)
    g_edge[:, 0:DE] += turned[0:DE]
    d_source[pl.ds(step * group, group), :] = turned[DE : DE + group]
    total[:, 0:DE] += dot_turned(tall[...], d_first)

    @pl.when(step == last)
    def _():
        put_halves((even, odd), total, owned)
        gain_row = jnp.sum(gain_sum[...].T, axis=0, keepdims=True)
        shift_row = jnp.sum(shift_sum[...].T, axis=0, keepdims=True)
        both_rows = jnp.concatenate([gain_row, shift_row], axis=1)
        g_norms[...] = jnp.zeros_like(g_norms)
        for index in range(3):
            g_norms[index : index + 1] = both_rows[:, index * LANES : (index + 1) * LANES]


def edge_phase(tall, edge, cot, pieces, q_src, u_edge, u_mid, u_out, norms, after):
    nodes, rows = tall.shape
    owned = q_src.shape[0]
    block = block_of()
    count = len(pieces)
    half = (count // 2, owned, WIDE)
    square = shaped((DE, WIDE), jnp.float32)
    line = shaped((8, LANES), jnp.float32)
    return pl.pallas_call(
        functools.partial(edge_kernel, count),
        grid=(rows // block,),
        in_specs=[
            tall_lanes(nodes, block),
            lanes(DE, block),
            lanes(DE, block),
            whole((owned, WIDE)),
            whole((DE, WIDE)),
            whole((DE, WIDE)),
            whole((DE, WIDE)),
            whole((8, WIDE)),
        ]
        + [whole((owned, WIDE))] * count
        + anywhere(after),
        out_specs=[
            lanes(DE, block),
            lanes(DE, block),
            kept(half),
            kept(half),
            kept((owned, DE)),
            kept((DE, WIDE)),
            kept((DE, WIDE)),
            kept((DE, WIDE)),
            kept((8, LANES)),
        ],
        out_shape=[
            shaped((DE, rows), LOW),
            shaped((DE, rows), jnp.float32),
            shaped(half, LOW),
            shaped(half, LOW),
            shaped((owned, DE), jnp.float32),
            square,
            square,
            square,
            line,
        ],
        scratch_shapes=[
            pltpu.VMEM((WIDE, nodes), LOW),
            pltpu.VMEM((WIDE, WIDE), LOW),
            pltpu.VMEM((nodes, WIDE), jnp.float32),
            pltpu.VMEM((WIDE, DE), LOW),
            pltpu.VMEM((WIDE, DE), LOW),
            pltpu.VMEM((DE, LANES), jnp.float32),
            pltpu.VMEM((DE, LANES), jnp.float32),
            pltpu.VMEM((WIDE, 8), jnp.float32),
            pltpu.VMEM((WIDE, block), LOW),
        ],
        compiler_params=params(),
    )(tall, edge, cot, q_src, u_edge, u_mid, u_out, norms, *pieces, *after)


def put_blocks(ref, base, matrix, step=1):
    for row in range(matrix.shape[0] // TILE):
        strip = matrix[row * TILE : (row + 1) * TILE].astype(ref.dtype)
        owner, batch, slot = early_place(base + row * step)
        for part in range(4):
            ref[owner, batch, part, slot * TILE : (slot + 1) * TILE, :] = strip[
                :, part * LANES : (part + 1) * LANES
            ]


def put_sides(refs, core, stores):
    for own in range(2):

        @pl.when(core == own)
        def _():
            for side, value, index in stores:
                refs[side ^ own][index] = value


def small_stores(batch, begin, matrix):
    stores = []
    piece = EARLY_ROWS // 8
    end = begin + matrix.shape[0]
    first = begin
    while first < end:
        index, offset = first // piece, first % piece
        amount = min(end - first, piece - offset)
        value = matrix[first - begin : first - begin + amount].astype(LOW)
        place = (index % 4 ^ batch, slice(offset, offset + amount), slice(None))
        stores.append((index // 4, value, place))
        first += amount
    return stores


def put_norm(ref, index, values):
    total = jnp.sum(values, axis=0, keepdims=True)
    for part in range(4):
        row = index * 4 + part
        ref[row : row + 1, 0:LANES] = total[:, part * LANES : (part + 1) * LANES]


def early_place(block):
    batch, rest = block // 24, block % 24
    return rest // 3, batch, rest % 3


def node_backward_kernel(
    place, cot, d_q_src, low, summed, one, inside, act, slope, scale, sums,
    blocks, u_src, u_dst, norms, g_edge, g_mid, g_out, g_edge_norms, *refs,
):
    reply, d_inside_out, g_blocks, g_even, g_odd, g_norms = refs[-6:]
    pieces = refs[:-6]
    core, batch = place[1], place[2]
    stores = []
    d_src = d_q_src[...].astype(LOW)
    d_dst = sum(piece[...].astype(jnp.float32) for piece in pieces).astype(LOW)
    low_now = low[...]
    blank = jnp.zeros((D, WIDE - DE), jnp.float32)
    stores += small_stores(batch, 0, jnp.concatenate([dot_rows(low_now, d_src), blank], axis=1))
    stores += small_stores(batch, D, dot_rows(low_now, d_dst))
    for index, ref in enumerate((g_edge, g_mid, g_out)):
        stores += small_stores(batch, 2 * D + index * DE, ref[...])
    g_norms[...] = jnp.zeros_like(g_norms)
    g_norms[16:24, 0:LANES] = g_edge_norms[...]
    d_final = (
        cot[...].astype(jnp.float32)
        + dot_turned(d_src, u_src[:, 0:DE])
        + dot_turned(d_dst, u_dst[...])
    )
    scaled, inverse = norm_parts(summed[...], D)
    d_summed = norm_back(scaled, inverse, norms[2:3], d_final, D)
    put_norm(g_norms, 2, d_final * scaled)
    put_norm(g_norms, 3, d_final)
    d_narrow = d_summed.astype(LOW)
    one_low = one[...].astype(LOW)
    d_one = d_summed
    first_up = D // TILE
    parts = FF // D
    first_down = first_up + first_up * parts
    for part in range(parts):
        cols = slice(part * D, (part + 1) * D)
        put_blocks(g_blocks, first_down + part * first_up, dot_rows(act[:, cols], d_narrow))
        d_wide = (
            dot_turned(d_narrow, down_part(blocks, part)) * slope[:, cols].astype(jnp.float32)
        ).astype(LOW)
        put_blocks(g_blocks, first_up + part, dot_rows(one_low, d_wide), parts)
        d_one += dot_turned(d_wide, up_part(blocks, part))
    scaled, inverse = norm_parts(inside[...], D)
    d_inside = norm_back(scaled, inverse, norms[0:1], d_one, D)
    put_norm(g_norms, 0, d_one * scaled)
    put_norm(g_norms, 1, d_one)
    d_inside_out[...] = d_inside
    per_target = (d_inside * scale[...]).astype(LOW)
    high, rest = split_low(sums[...])
    put_blocks(g_blocks, 0, dot_rows(high, per_target) + dot_rows(rest, per_target))
    reply[...] = dot_turned(per_target, out_part(blocks)).astype(LOW)
    stores += small_stores(batch, 2 * D + 3 * DE, g_norms[...])
    put_sides((g_even, g_odd), core, stores)


def node_backward(place, operands, pieces, after):
    owned = operands[0].shape[0]
    half = shaped((4, EARLY_ROWS // 8, WIDE), LOW)
    amount = len(operands) + len(pieces)
    return pl.pallas_call(
        trimmed(node_backward_kernel, amount + 1, len(after)),
        in_specs=[pl.BlockSpec(memory_space=pltpu.SMEM)]
        + [pl.BlockSpec(memory_space=pltpu.VMEM)] * amount
        + anywhere(after),
        out_shape=[
            shaped((owned, D), LOW),
            shaped((owned, D), jnp.float32),
            shaped((8, 3, 4, OWNED_ROWS, LANES), LOW),
            half,
            half,
        ],
        scratch_shapes=[pltpu.VMEM((TILE, WIDE), jnp.float32)],
        compiler_params=params(),
    )(place, *operands, *pieces, *after)


def message_back_kernel(
    count, place, tall, edge, hidden, slope_one, slope_two, part_edge, x_all, w_mid, w_edge, *refs
):
    pieces = refs[0:count]
    (
        d_edge, even, odd, d_source, late_even, late_odd, table, total, g_mid, g_edge, from_source, wide,
    ) = refs[-12:]
    step = pl.program_id(0)
    owned = d_source.shape[0]

    @pl.when(step == 0)
    def _():
        table[...] = jnp.concatenate([piece[...] for piece in pieces], axis=0).T
        wide[DE:WIDE] = source_mask(edge.shape[1]).astype(LOW)
        total[...] = jnp.zeros_like(total)
        g_mid[...] = jnp.zeros_like(g_mid)
        g_edge[...] = jnp.zeros_like(g_edge)

    wide[0:DE] = edge[...]
    d_hidden = dot(table[...], tall[...])
    d_second = (d_hidden * slope_two[...].astype(jnp.float32)).astype(LOW)
    g_mid[...] += dot_turned(hidden[...], d_second)
    d_pre = (dot(w_mid[...], d_second) * slope_one[...].astype(jnp.float32)).astype(LOW)
    d_edge[...] = part_edge[...] + dot(w_edge[...], d_pre)
    turned = dot_turned(wide[...], d_pre)
    g_edge[...] += turned[0:DE]
    group = hidden.shape[1] // K
    from_source[pl.ds(step * group, group), :] = turned[DE : DE + group]
    total[...] += dot_turned(tall[...], d_pre)

    @pl.when(step == pl.num_programs(0) - 1)
    def _():
        put_halves((even, odd), total, owned)
        gathered = x_all[...]
        sources_low = from_source[...].astype(LOW)
        d_source[...] = sources_low
        chip, core, batch = place[0], place[1], place[2]
        matrices = (
            dot_rows(gathered[0:owned], sources_low),
            dot_rows(gathered, total[...].astype(LOW)),
            g_mid[...],
        )
        stores = []
        for row in range(3 * (D // TILE)):
            owner, slot = row // 3, row % 3
            strip = matrices[row // (D // TILE)][row % (D // TILE) * TILE :][0:TILE].astype(LOW)
            first = pl.multiple_of((owner // 2 ^ chip) * OWNED_ROWS + slot * TILE, TILE)
            for part in range(4):
                value = strip[:, part * LANES : (part + 1) * LANES]
                stores.append((owner % 2, value, (part ^ batch, pl.ds(first, TILE), slice(None))))
        half = DE // 2
        for side in range(2):
            strip = g_edge[side * half : (side + 1) * half].astype(LOW)
            for part in range(4):
                value = strip[:, part * LANES : (part + 1) * LANES]
                rows = slice(4 * OWNED_ROWS, 4 * OWNED_ROWS + half)
                stores.append((side, value, (part ^ batch, rows, slice(None))))
        put_sides((late_even, late_odd), core, stores)


def message_backward(
    place, tall, edge, hidden, slope_one, slope_two, part_edge, x_all, w_rows, w_edge, pieces, after
):
    nodes, rows = tall.shape
    owned = pieces[0].shape[0]
    block = block_of()
    count = len(pieces)
    half = (count // 2, owned, D)
    feature = tall_lanes(D, block) if nodes <= 1024 else pl.BlockSpec(
        (D, block), lambda i: (0, i), pipeline_mode=pl.Buffered(1)
    )
    late = (4, 4 * OWNED_ROWS + DE // 2, LANES)
    return pl.pallas_call(
        functools.partial(message_back_kernel, count),
        grid=(rows // block,),
        in_specs=[
            pl.BlockSpec(memory_space=pltpu.SMEM),
            tall_lanes(nodes, block),
            lanes(DE, block),
            feature,
            feature,
            feature,
            lanes(DE, block),
            whole((nodes, D)),
            pl.BlockSpec((D, D), lambda i: (2, 0), pipeline_mode=pl.Buffered(1)),
            whole((DE, D)),
        ]
        + [whole((owned, D))] * count
        + anywhere(after),
        out_specs=[
            lanes(DE, block),
            kept(half),
            kept(half),
            kept((owned, D)),
            kept(late),
            kept(late),
        ],
        out_shape=[
            shaped((DE, rows), jnp.float32),
            shaped(half, LOW),
            shaped(half, LOW),
            shaped((owned, D), LOW),
            shaped(late, LOW),
            shaped(late, LOW),
        ],
        scratch_shapes=[
            pltpu.VMEM((D, nodes), LOW),
            pltpu.VMEM((nodes, D), jnp.float32),
            pltpu.VMEM((D, D), jnp.float32),
            pltpu.VMEM((DE, D), jnp.float32),
            pltpu.VMEM((owned, D), jnp.float32),
            pltpu.VMEM((WIDE, block), LOW),
        ],
        compiler_params=params(),
    )(
        place, tall, edge, hidden, slope_one, slope_two, part_edge, x_all, w_rows, w_edge,
        *pieces, *after,
    )


def node_gradient_kernel(inside, d_source, w_rows, *refs):
    pieces, out = refs[:-1], refs[-1]
    d_target = sum(piece[...].astype(jnp.float32) for piece in pieces).astype(LOW)
    out[...] = (
        inside[...]
        + dot_turned(d_source[...], w_rows[0:D])
        + dot_turned(d_target, w_rows[D : 2 * D])
    )


def node_gradient(inside, d_source, w_rows, pieces):
    return pl.pallas_call(
        node_gradient_kernel,
        out_shape=shaped(inside.shape, jnp.float32),
        compiler_params=params(12),
    )(inside, d_source, w_rows, *pieces)


def add_halves_kernel(left, right, *outs):
    for index, out in enumerate(outs):
        total = left[index].astype(jnp.float32) + right[index].astype(jnp.float32)
        out[...] = total.astype(out.dtype)


def add_halves(left, right):
    shape = left.shape[1:]
    return pl.pallas_call(
        add_halves_kernel,
        out_shape=[shaped(shape, jnp.float32)] + [shaped(shape, LOW)] * (left.shape[0] - 1),
        compiler_params=params(8),
    )(left, right)


def assemble_kernel(count, place, *refs):
    lines, pieces, rows, x_all = refs[0:8], refs[8:-2], refs[-2], refs[-1]
    chip, core, batch = place[0], place[1], place[2]
    owned = pieces[0].shape[0]
    for index, piece in enumerate(lines):
        side, part = index // 4, index % 4
        for line in range(4):
            row = ((line ^ chip) * 2 + (side ^ core)) * OWNED_ROWS
            lane = (part ^ batch) * LANES
            rows[
                pl.ds(pl.multiple_of(row, TILE), OWNED_ROWS),
                pl.ds(pl.multiple_of(lane, LANES), LANES),
            ] = piece[line]
    for index, piece in enumerate(pieces):
        x_all[index * owned : (index + 1) * owned] = piece[...]


def assemble(place, lines, pieces):
    owned = pieces[0].shape[0]
    amount = len(lines) + len(pieces)
    return pl.pallas_call(
        functools.partial(assemble_kernel, len(pieces)),
        in_specs=[pl.BlockSpec(memory_space=pltpu.SMEM)]
        + [pl.BlockSpec(memory_space=pltpu.VMEM)] * amount,
        out_shape=[shaped((3 * D, D), LOW), shaped((8 * owned, D), LOW)],
        compiler_params=params(12),
    )(place, *lines, *pieces)


def own_rows_kernel(tiles, rows, *refs):
    quarters, (flat, pair) = refs[0:4], refs[4:]
    load_flat(tiles, flat)
    for index, group in enumerate(group_list(0, 24, 4)):
        block, side = index // 2, index % 2
        value = group_in(flat, pair, group).astype(LOW)
        rows[block * TILE : (block + 1) * TILE, side * QUAD : (side + 1) * QUAD] = value
        for half in range(2):
            quarters[2 * side + half][block * TILE : (block + 1) * TILE, :] = value[
                :, half * LANES : (half + 1) * LANES
            ]


def own_rows(tiles):
    return pl.pallas_call(
        own_rows_kernel,
        out_shape=[
            shaped((OWNED_ROWS, D), LOW),
        ] + [shaped((OWNED_ROWS, LANES), LOW)] * 4 + [
        ],
        scratch_shapes=[
            pltpu.VMEM((flat_rows(24), LANES), jnp.float32),
            pltpu.VMEM((TILE, LANES), jnp.float32),
        ],
        compiler_params=params(),
    )(tiles)


LANES = 128
QUAD = 4 * TILE
FLAT = TILE * TILE // LANES


def group_list(first, last, size):
    return [list(range(t, min(t + size, last))) for t in range(first, last, size)]


def load_flat(ref, flat):
    amount = ref.shape[0]
    for top in range(0, amount, 8):
        rows = min(8, amount - top)
        for part in range(FLAT):
            flat[pl.ds(top * FLAT + 8 * part, rows), :] = ref[
                top : top + rows, part * LANES : (part + 1) * LANES
            ]


def store_flat(ref, flat, first=0, last=None):
    last = ref.shape[0] if last is None else last
    while first < last:
        rows = min(8 - first % 8, last - first)
        top = first // 8 * 8
        for part in range(FLAT):
            ref[first : first + rows, part * LANES : (part + 1) * LANES] = flat[
                pl.ds(top * FLAT + 8 * part + first - top, rows), :
            ]
        first += rows


def tile_rows(tile):
    return pl.ds(tile // 8 * 8 * FLAT + tile % 8, FLAT, stride=8)


def lower_half(shape):
    return lax.broadcasted_iota(jnp.int32, shape, 1) < TILE


def group_in(flat, pair, tiles):
    left = lower_half((FLAT, LANES))
    halves = []
    for first in range(0, 4, 2):
        here = tiles[first : first + 2]
        one = flat[tile_rows(here[0]), :] if here else jnp.zeros((FLAT, LANES), jnp.float32)
        two = flat[tile_rows(here[1]), :] if len(here) > 1 else jnp.zeros_like(one)
        pair[pl.ds(0, FLAT, stride=2), :] = jnp.where(left, one, pltpu.roll(two, TILE, 1))
        pair[pl.ds(1, FLAT, stride=2), :] = jnp.where(left, pltpu.roll(one, TILE, 1), two)
        halves.append(pair[...])
    return jnp.concatenate(halves, axis=1)


def group_out(value, flat, pair, tiles):
    left = lower_half((FLAT, LANES))
    for first in range(0, 4, 2):
        here = tiles[first : first + 2]
        if not here:
            continue
        pair[...] = value[:, first * TILE : first * TILE + LANES]
        even = pair[pl.ds(0, FLAT, stride=2), :]
        odd = pair[pl.ds(1, FLAT, stride=2), :]
        flat[tile_rows(here[0]), :] = jnp.where(left, even, pltpu.roll(odd, TILE, 1))
        if len(here) > 1:
            flat[tile_rows(here[1]), :] = jnp.where(left, pltpu.roll(even, TILE, 1), odd)


def flat_rows(amount):
    return -(-amount // 8) * 8 * FLAT


SPAN_GROUPS = 8


def regroup_small_kernel(count, *refs):
    tiles, outs = refs[0:count], refs[count : 2 * count]
    flat, pair = refs[-2:]
    step = pl.program_id(0)
    for condition, amount, size, spot in (
        (step == 0, 24, 4, 0),
        ((step > 0) & (step < 4), 24, 3, 0),
        (step == 4, 3, 3, 0),
    ):

        @pl.when(condition)
        def _():
            for ref, out in zip(tiles, outs):
                load_flat(ref, flat)
                for index, group in enumerate(group_list(0, amount, size)):
                    out[spot + index] = group_in(flat, pair, group)


def regroup_small(arrays, after=()):
    count = len(arrays)
    shape = (5 * SPAN_GROUPS, TILE, QUAD)
    out_spec = pl.BlockSpec((SPAN_GROUPS, TILE, QUAD), lambda i: (i, 0, 0))
    return pl.pallas_call(
        trimmed(functools.partial(regroup_small_kernel, count), count, len(after)),
        grid=(5,),
        in_specs=[pl.BlockSpec((24, TILE * TILE), lambda i: (i, 0))] * count + anywhere(after),
        out_specs=[out_spec] * count,
        out_shape=[shaped(shape, jnp.float32)] * count,
        scratch_shapes=[
            pltpu.VMEM((flat_rows(24), LANES), jnp.float32),
            pltpu.VMEM((TILE, LANES), jnp.float32),
        ],
        compiler_params=params(),
    )(*arrays, *after)


def regroup_weights_kernel(tiles, out, w_edge, e_src, e_dst, e_edge, e_mid, e_out, flat, pair):
    regroup_small_kernel(1, tiles, out, flat, pair)
    step = pl.program_id(0)

    @pl.when(step == 0)
    def _():
        for index in range(6):
            block, side = index // 2, index % 2
            w_edge[block * TILE : (block + 1) * TILE, side * QUAD : (side + 1) * QUAD] = out[
                index
            ].astype(LOW)

    for condition, ref, first, amount, start in (
        (step == 1, e_src, 0, 8, 0), (step == 2, e_dst, 0, 8, 0), (step == 3, e_edge, 0, 3, 0),
        (step == 3, e_mid, 3, 3, 0), (step == 3, e_out, 6, 2, 0), (step == 4, e_out, 0, 1, 2),
    ):

        @pl.when(condition)
        def _():
            for index in range(amount):
                here = slice((start + index) * TILE, (start + index + 1) * TILE)
                ref[here] = out[first + index].astype(LOW)


def regroup_weights(weights):
    shapes = [(DE, D), (D, WIDE), (D, WIDE)] + [(DE, WIDE)] * 3
    return pl.pallas_call(
        regroup_weights_kernel,
        grid=(5,),
        in_specs=[pl.BlockSpec((24, TILE * TILE), lambda i: (i, 0))],
        out_specs=[pl.BlockSpec((SPAN_GROUPS, TILE, QUAD), lambda i: (i, 0, 0))]
        + [kept(shape) for shape in shapes],
        out_shape=[shaped((5 * SPAN_GROUPS, TILE, QUAD), jnp.float32)]
        + [shaped(shape, LOW) for shape in shapes],
        scratch_shapes=[
            pltpu.VMEM((flat_rows(24), LANES), jnp.float32),
            pltpu.VMEM((TILE, LANES), jnp.float32),
        ],
        compiler_params=params(),
    )(weights)


def regroup_big_kernel(count, *refs):
    tiles, outs = refs[0:count], refs[count : 2 * count]
    flat, pair = refs[-2:]
    for ref, out in zip(tiles, outs):
        load_flat(ref, flat)
        for index, group in enumerate(group_list(0, 24, 4)):
            out[index] = group_in(flat, pair, group)


def regroup_big(arrays, after=()):
    count = len(arrays)
    return pl.pallas_call(
        trimmed(functools.partial(regroup_big_kernel, count), count, len(after)),
        in_specs=[pl.BlockSpec(memory_space=pltpu.VMEM)] * count + anywhere(after),
        out_shape=[shaped((6, TILE, QUAD), jnp.float32)] * count,
        scratch_shapes=[
            pltpu.VMEM((flat_rows(24), LANES), jnp.float32),
            pltpu.VMEM((TILE, LANES), jnp.float32),
        ],
        compiler_params=params(),
    )(*arrays, *after)


def soap_groups(grads, weights, firsts, seconds, lefts, rights, rates):
    count = range(len(grads))
    lane = lax.broadcasted_iota(jnp.int32, (TILE, QUAD), 1) // TILE
    masks = [jnp.where(lane == k, 1.0, 0.0) for k in range(4)]
    low_masks = [mask.astype(LOW) for mask in masks]

    def diagonal(values):
        return jnp.concatenate([values * mask for mask in low_masks], axis=0)

    right_sides = [diagonal(v.astype(LOW)) for v in rights]
    left_low = [v.astype(LOW) for v in lefts]
    half = [dot(grads[i].astype(LOW), right_sides[i]).astype(LOW) for i in count]
    full = [dot_rows(left_low[i], half[i]) for i in count]
    turned = [sum(v[TILE * k : TILE * (k + 1)] * masks[k] for k in range(4)) for v in full]
    new_one = [BETA_ONE * firsts[i] + (1.0 - BETA_ONE) * turned[i] for i in count]
    new_two = [
        BETA_TWO * seconds[i] + (1.0 - BETA_TWO) * turned[i] * turned[i] for i in count
    ]
    fix_one = 1.0 / (1.0 - BETA_ONE**STEP)
    fix_two = 1.0 / (1.0 - BETA_TWO**STEP)
    steps = [
        new_one[i] * fix_one / (jnp.sqrt(new_two[i] * fix_two) + EPS_ADAM) for i in count
    ]
    sides = [diagonal(v.astype(LOW)) for v in steps]
    half = [dot(left_low[i], sides[i]).astype(LOW) for i in count]
    restored = [dot_turned(half[i], right_sides[i]) for i in count]
    new = [
        weights[i] - rates[i] * (restored[i] + DECAY * weights[i]) for i in count
    ]
    return new_one, new_two, new


TOGETHER = 5
EARLY_ROWS = 1664


def block_rate(block):
    middle = (2 * D + DE) ** (-0.5)
    return jnp.where(
        block < 16,
        middle,
        jnp.where(
            block < 24,
            D ** (-0.5),
            jnp.where(block < 32, 2.5 * D ** (-0.5), jnp.where(block < 64, D ** (-0.5), FF ** (-0.5))),
        ),
    )


def small_rates():
    middle = (2 * D + DE) ** (-0.5)
    return [middle] * 19 + [DE ** (-0.5)] * 3 + [1.5 * DE ** (-0.5)] * 3


NORM_ROWS = 19


def soap_early_kernel(scale, place, grads, rates, weight, first, second, left, right, *refs):
    norms, outs = refs[0:3], refs[3:9]
    flats, pairs = refs[9:12], refs[12]
    step = pl.program_id(0)
    core, batch = place[1], place[2]
    piece = EARLY_ROWS // 8

    def rows_of(begin, end):
        parts = []
        while begin < end:
            index, offset = begin // piece, begin % piece
            amount = min(end - begin, piece - offset)
            parts.append(grads[index // 4 ^ core, index % 4 ^ batch, offset : offset + amount, :])
            begin += amount
        value = parts[0] if len(parts) == 1 else jnp.concatenate(parts, axis=0)
        return value.astype(jnp.float32) * scale

    def groups(start, amount):
        here = range(amount)
        state = [[ref[i] for i in here] for ref in (weight, first, second, left, right)]
        results = soap_groups(
            [rows_of((start + i) * TILE, (start + i + 1) * TILE) for i in here],
            *state,
            [rates[start + i : start + i + 1] for i in here],
        )
        for spot in here:
            tiles = list(range(spot * 3, spot * 3 + 3))
            for kind, flat in enumerate(flats):
                group_out(results[kind][spot], flat, pairs.at[kind * SPAN_GROUPS + spot], tiles)

    for index, amount in enumerate((8, 8, 8, 1)):

        @pl.when(step == index)
        def _():
            groups(8 * index, amount)

    @pl.when(step == 0)
    def _():
        rows = rows_of(25 * TILE, 25 * TILE + 32)[0:NORM_ROWS, 0:LANES]
        results = adam_step(*(ref[...] for ref in norms), rows)
        for ref, value in zip(outs[3:6], (results[2], results[0], results[1])):
            ref[...] = value

    for ref, flat in zip(outs[0:3], flats):
        store_flat(ref, flat)


def soap_early(scale, place, grads, state, norms):
    out = shaped((99, TILE * TILE), jnp.float32)
    line = shaped((NORM_ROWS, LANES), jnp.float32)
    rates = jnp.asarray(np.repeat(np.array(small_rates(), np.float32)[:, None], QUAD, axis=1))
    return pl.pallas_call(
        functools.partial(soap_early_kernel, scale),
        grid=(4,),
        in_specs=[pl.BlockSpec(memory_space=pltpu.SMEM), whole(grads.shape), whole(rates.shape)]
        + [pl.BlockSpec((SPAN_GROUPS, TILE, QUAD), lambda i: (1 + i, 0, 0))] * 5
        + [whole(line.shape)] * 3,
        out_specs=[pl.BlockSpec((24, TILE * TILE), lambda i: (1 + i, 0))] * 3
        + [kept(line.shape)] * 3,
        out_shape=[out, out, out, line, line, line],
        scratch_shapes=[pltpu.VMEM((flat_rows(24), LANES), jnp.float32)] * 3
        + [pltpu.VMEM((3 * SPAN_GROUPS, TILE, LANES), jnp.float32)],
        compiler_params=params(),
    )(place, grads, rates, *state, *norms)


def soap_late_kernel(scale, place, own, other_one, other_two, other_three, *refs):
    state, v_state = refs[0:5], refs[5:10]
    older = refs[12]
    one, two, new, low, v_one, v_two, v_new, v_low = refs[13:21]
    flats, v_flats, pairs, shared_of = refs[21:24], refs[24:27], refs[27], refs[28]
    chip, core, batch = place[0], place[1], place[2]
    groups = group_list(0, 24, 4)
    received = (own, other_one, other_two, other_three)
    for shift, ref in enumerate(received):
        shared_of[shift, 4 * OWNED_ROWS :, :] = ref[4 * OWNED_ROWS :, :]

    def v_block(block, side):
        parts = []
        for part in (2 * side, 2 * side + 1):
            rows = []
            for begin in range(block * TILE, (block + 1) * TILE, TILE // 2):
                half, offset = begin // (DE // 2), begin % (DE // 2)
                first = 4 * OWNED_ROWS + (half ^ core) * (DE // 2) + offset
                rows.append(shared_of[part ^ batch, pl.ds(pl.multiple_of(first, 32), TILE // 2), :])
            parts.append(jnp.concatenate(rows, axis=0))
        return jnp.concatenate(parts, axis=1).astype(jnp.float32)

    def own_part(block, part):
        rows = slice(block * TILE, (block + 1) * TILE)
        shifted = slice(part * OWNED_ROWS + rows.start, part * OWNED_ROWS + rows.stop)
        total = tree_sum([ref[shifted, :].astype(jnp.float32) for ref in received])
        return jnp.where(batch == 0, received[part][rows, :].astype(jnp.float32), total)

    def own_block(block, side):
        return jnp.concatenate([own_part(block, 2 * side), own_part(block, 2 * side + 1)], axis=1)

    first = batch * 24 + (chip * 2 + core) * 3
    own_rates = [block_rate(first + i // 2) for i in range(6)]
    v_rates = [(2 * D + DE) ** (-0.5)] * 6
    for grad_of, values, rates, targets, base in (
        (own_block, state, own_rates, flats, 0),
        (v_block, v_state, v_rates, v_flats, 18),
    ):
        here = range(6)
        grads = [grad_of(i // 2, i % 2) * scale for i in here]
        results = soap_groups(grads, *[[ref[i] for i in here] for ref in values], rates)
        for index in here:
            for kind, flat in enumerate(targets):
                group_out(results[kind][index], flat, pairs.at[base + kind * 6 + index], groups[index])
    for ref, flat in zip((one, two, new, v_one, v_two, v_new), (*flats, *v_flats)):
        store_flat(ref, flat)
    low[...] = new[...].astype(LOW)
    v_low[...] = jnp.concatenate([v_new[...], older[24:]], axis=0).astype(LOW)


def soap_late(scale, place, received, state, v_state, early):
    out = shaped((24, TILE * TILE), jnp.float32)
    small = shaped(early[0].shape, jnp.float32)
    front = pl.BlockSpec((24, TILE * TILE), lambda i: (0, 0))
    group = whole((6, TILE, QUAD))
    flat = pltpu.VMEM((flat_rows(24), LANES), jnp.float32)
    return pl.pallas_call(
        functools.partial(soap_late_kernel, scale),
        grid=(1,),
        in_specs=[
            pl.BlockSpec(memory_space=pltpu.SMEM),
        ]
        + [whole(v.shape) for v in received]
        + [group] * 10
        + [pl.BlockSpec(memory_space=pl.ANY)] * 2
        + [whole(small.shape)],
        out_specs=[front] * 7 + [whole(small.shape)],
        out_shape=[out, out, out, shaped((24, TILE * TILE), LOW), small, small, small]
        + [shaped(small.shape, LOW)],
        scratch_shapes=[flat] * 6
        + [pltpu.VMEM((36, TILE, LANES), jnp.float32), pltpu.VMEM((4, *received[0].shape), LOW)],
        input_output_aliases={15: 4, 16: 5, 17: 6},
        compiler_params=params(),
    )(place, *received, *state, *v_state, *early)


def swap_core(values):
    return lax.ppermute(values, "core", [(0, 1), (1, 0)])


def swap_chip(values, shift):
    chips = lax.axis_size("chip")
    return lax.ppermute(values, "chip", [(i, i ^ shift) for i in range(chips)])


def gate(values, others):
    return lax.optimization_barrier((values, others))[0]


def send_pieces(values):
    chips = lax.axis_size("chip")
    return [values] + [swap_chip(values, shift) for shift in range(1, chips)]


def gather_pieces(values, fill=()):
    return swap_pieces(send_pieces(values), fill)


def swap_pieces(parts, fill=()):
    parts = gate(parts, fill)
    return [half for part in parts for half in (part, swap_core(part))]


def reduce_pieces(even, odd):
    return send_near(add_halves(even, swap_core(odd)))


def send_near(near):
    return [near[0]] + [swap_chip(near[shift], shift) for shift in range(1, len(near))]


def swap_batch(values, shift):
    return lax.ppermute(values, "batch", [(i, i ^ shift) for i in range(4)])


def pick(values, index):
    return lax.dynamic_index_in_dim(values, index, 0, keepdims=False)


def tree_sum(parts):
    while len(parts) > 1:
        parts = [parts[i] + parts[i + 1] for i in range(0, len(parts), 2)]
    return parts[0]


def wide_values(values):
    return values.astype(jnp.float32)


def gather_first(place, quarters, x, batch, fill):
    pieces = [x] + [swap_chip(x, shift) for shift in range(1, 4)]
    sent = [
        lax.ppermute(quarters[index], "batch", [(0, index)]) for index in range(1, 4)
    ]
    quarter = jnp.where(batch == 0, quarters[0], sent[0] + sent[1] + sent[2])
    lines = jnp.stack([quarter] + [swap_chip(quarter, shift) for shift in range(1, 4)])
    lines = gate(lines, fill)
    parts = [lines] + [swap_batch(lines, shift) for shift in range(1, 4)]
    pieces = [half for piece in pieces for half in (piece, swap_core(piece))]
    return assemble(place, parts + [swap_core(part) for part in parts], pieces)


def reduce_small(near):
    total = near[0]
    for shift in range(1, 4):
        total = total + wide_values(swap_batch(near[shift], shift))
    total = total.astype(LOW)
    others = [total] + [swap_chip(total, shift) for shift in range(1, 4)]
    return total, tree_sum([wide_values(v) for v in others]).astype(LOW)


def share_small(total, token):
    others = [total] + gate([swap_batch(total, shift) for shift in range(1, 4)], token)
    parts = jnp.stack(others)
    return jnp.stack([parts, swap_core(parts)])


def reduce_late(near, early, batch, fill, third, other):
    received = [swap_batch(near[shift], shift) for shift in range(1, 4)]
    received = gate(received, fill)
    total = near[0] + sum(wide_values(part) for part in received)
    shared = total[4 * OWNED_ROWS :]
    lines = [total[OWNED_ROWS * i : OWNED_ROWS * (i + 1)] for i in range(4)]
    sent = [
        jnp.concatenate([lines[shift], shared], axis=0).astype(LOW) for shift in range(1, 4)
    ]
    received = [swap_chip(part, shift) for shift, part in enumerate(sent, 1)]
    quarter = lines[0]
    shares = [wide_values(shared.astype(LOW))]
    for part in received:
        got = wide_values(part)
        quarter = quarter + got[0:OWNED_ROWS]
        shares.append(got[OWNED_ROWS:])
    shared = tree_sum(shares).astype(LOW)
    shared = jnp.concatenate([shared, swap_core(shared)], axis=0)
    quarter = jnp.pad(quarter.astype(LOW)[None], ((0, 3), (0, 0), (0, 0)))

    def outgoing(target):
        block = jnp.where(target == 0, quarter, pick(early, jnp.maximum(target - 1, 0)))
        return jnp.concatenate([block.reshape(4 * OWNED_ROWS, LANES), shared], axis=0)

    sent = gate([outgoing(batch ^ shift) for shift in range(4)], third)
    received = [swap_batch(part, shift) for shift, part in enumerate(sent) if shift]
    received = gate([sent[0]] + received, other)
    return received


def pad_to(matrix, height, breadth):
    return jnp.pad(matrix, ((0, height - matrix.shape[0]), (0, breadth - matrix.shape[1])))


def norm_rows(vector):
    return vector.reshape(NORM_ROWS, LANES)


def norm_vector(rows):
    return rows.reshape(-1)


def gather_plain(tiles, every):
    amount = tiles.shape[0]
    unit = math.gcd(amount, D // TILE)
    local = tiles.astype(LOW).reshape(amount // unit, unit, TILE, TILE)
    local = local.transpose(0, 2, 1, 3).reshape(amount // unit, TILE, unit * TILE)
    units = lax.all_gather(local, every, axis=0, tiled=True)
    blocks = units.reshape(-1, D // TILE // unit, TILE, unit * TILE).transpose(0, 2, 1, 3)
    blocks = blocks.reshape(-1, TILE, D)
    return blocks[0:24].reshape(3 * D, D), blocks


def soap_plain(weight, moment_one, moment_two, left, right, gradient, rates):
    left, right = as_square(left), as_square(right)
    high = lax.Precision.HIGHEST
    turned = jnp.einsum("tji,tjk->tik", left, gradient, precision=high)
    turned = jnp.einsum("tik,tkl->til", turned, right, precision=high)
    new_one = BETA_ONE * as_square(moment_one) + (1.0 - BETA_ONE) * turned
    new_two = BETA_TWO * as_square(moment_two) + (1.0 - BETA_TWO) * turned * turned
    direction = (
        new_one / (1.0 - BETA_ONE**STEP) / (jnp.sqrt(new_two / (1.0 - BETA_TWO**STEP)) + EPS_ADAM)
    )
    restored = jnp.einsum("tij,tjk->tik", left, direction, precision=high)
    restored = jnp.einsum("tik,tlk->til", restored, right, precision=high)
    weight = as_square(weight)
    new = weight - rates[:, None, None] * (restored + DECAY * weight)
    return as_flat(new_one), as_flat(new_two), as_flat(new)


def update_plain(g_late, g_early, g_small, every, scale, big, small, norms):
    amount = big[0].shape[0]
    unit = math.gcd(amount, D // TILE)
    g_late, g_small = jnp.stack(g_late), jnp.stack(g_small).reshape(EARLY_ROWS, WIDE)
    late = g_late[:, :, 0 : 4 * OWNED_ROWS].reshape(2, 4, 4, OWNED_ROWS, LANES)
    late = late.transpose(2, 0, 3, 1, 4).reshape(24, TILE, D)
    w_edge = g_late[:, :, 4 * OWNED_ROWS :].transpose(0, 2, 1, 3).reshape(DE, D)
    early = g_early.reshape(8, 3, 4, 3, TILE, LANES).transpose(1, 0, 3, 4, 2, 5)
    early = early.reshape(72, TILE, D)
    grads = jnp.concatenate([late, early], axis=0)
    grads = grads.reshape(-1, TILE, D // TILE // unit, unit * TILE).transpose(0, 2, 1, 3)
    own = lax.psum_scatter(
        grads.reshape(-1, TILE, unit * TILE), every, scatter_dimension=0, tiled=True
    )
    own = wide_values(own).reshape(amount // unit, TILE, unit, TILE).transpose(0, 2, 1, 3)
    own = own.reshape(amount, TILE, TILE) * scale
    w_edge, g_small = lax.psum((wide_values(w_edge), wide_values(g_small)), every)
    strips = g_small[0:1600, 0:DE].reshape(25, TILE, 3, TILE).transpose(0, 2, 1, 3)
    tiles = jnp.concatenate(
        [as_square(to_flat_tiles(w_edge)), strips.reshape(75, TILE, TILE)], axis=0
    )
    first = lax.axis_index(every) * amount
    rates = lax.dynamic_slice_in_dim(
        jnp.asarray(rate_table(big_shapes(), big_spreads())), first, amount
    )
    big_new = soap_plain(*big, own, rates)
    rates = jnp.asarray(rate_table(small_shapes(), small_spreads()))
    small_new = soap_plain(*small, tiles * scale, rates)
    norm_new = adam_step(*norms, norm_vector(g_small[1600:1619, 0:LANES]) * scale)
    return big_new, small_new, norm_new


def body(
    node,
    edge,
    dest_device,
    dest_local,
    node_valid,
    node_cot,
    edge_cot,
    big_weight,
    big_first,
    big_second,
    big_left,
    big_right,
    small_weight,
    small_first,
    small_second,
    small_left,
    small_right,
    norm_params,
    norm_first,
    norm_second,
):
    chips = lax.axis_size("chip")
    every = ("batch", "chip", "core")
    shards = 2 * chips
    owned = node.shape[1]
    nodes = owned * shards
    rows = owned * K
    complexes = node.shape[0] * lax.axis_size("batch")
    tuned = chips == 4 and lax.axis_size("batch") == 4 and big_weight.shape[0] == 24
    chip, core, batch = (lax.axis_index(axis) for axis in ("chip", "core", "batch"))
    grad_scale = 1.0 / math.sqrt(complexes * nodes * K)
    x = node[0]
    big_state = (big_weight, big_first, big_second, big_left, big_right)
    small_state = (small_weight, small_first, small_second, small_left, small_right)
    norm_state = (norm_params, norm_first, norm_second)

    place = jnp.stack([chip, core, batch]).astype(jnp.int32) * int(tuned)
    small_groups, w_edge, e_src, e_dst, e_edge, e_mid, e_out = regroup_weights(small_weight)
    small_groups = [small_groups]
    norms = norm_params[0 : 4 * D].reshape(4, D)
    edge_norms = pad_to(norm_params[4 * D :].reshape(2, DE), 8, WIDE)
    valid = node_valid[0].astype(jnp.float32).reshape(owned, 1)
    me = chip * 2 + core
    relative = (dest_device[0].reshape(1, rows) ^ me) * owned + dest_local
    edge_across = edge[0].T
    if tuned:
        own, *quarters = own_rows(big_weight)
        blocks = lax.all_gather(own, every, axis=0, tiled=True).reshape(-1, TILE, D)
        w_rows, x_all = gather_first(
            place, quarters, x, batch, (w_edge, relative)
        )
    else:
        w_rows, blocks = gather_plain(big_weight, every)
        x_all = jnp.concatenate(gather_pieces(x), axis=0)

    even, odd, hidden, slope_one, slope_two, tall = message_forward(
        relative, edge_across, valid, x_all, owned, w_rows, w_edge, ()
    )
    sums = reduce_pieces(even, odd)
    if tuned:
        small_groups += regroup_small(small_state[1:5], (even,))
    node_low, q_src, q_dst, inside, one, act, slope, summed, scale, sums = node_forward(
        x, valid, blocks, e_src, e_dst, norms, sums, small_groups[1:2]
    )
    big_groups = list(regroup_big(big_state, (q_dst,))) if tuned else []
    q_pieces = gather_pieces(q_dst, big_groups[0:1])
    (
        edge_new, part_edge, even, odd, d_q_src, g_e_edge, g_e_mid, g_e_out, g_e_norms,
    ) = edge_phase(
        tall, edge_across, edge_cot[0].T, q_pieces, q_src, e_edge, e_mid, e_out, edge_norms, (),
    )
    d_q_dst = reduce_pieces(even, odd)
    reply, d_inside, g_early, *g_small = node_backward(
        place,
        [
            node_cot[0], d_q_src, node_low, summed, one, inside, act, slope, scale, sums,
            blocks, e_src, e_dst, norms, g_e_edge, g_e_mid, g_e_out, g_e_norms,
        ],
        d_q_dst,
        (),
    )
    replies = send_pieces(reply)
    held = ()
    if tuned:
        near_small = gate(add_halves(g_small[0], swap_core(g_small[1])), replies[1])
        part_small, small_sum = reduce_small(near_small)
        held = (part_small,)
    replies = swap_pieces(replies, held)
    d_edges, even, odd, d_p_src, *g_late = message_backward(
        place, tall, edge_across, hidden, slope_one, slope_two, part_edge, x_all, w_rows, w_edge, replies, held,
    )
    near_p = add_halves(even, swap_core(odd))
    d_p_dst = send_near(near_p)
    d_features = node_gradient(d_inside, d_p_src, w_rows, d_p_dst)

    if tuned:
        norm_groups = [norm_rows(v) for v in norm_state]
        late_groups = small_groups
        early = lax.psum_scatter(
            gate(g_early, replies), ("chip", "core"), scatter_dimension=0, tiled=True
        )
        early = early.reshape(3, 4, OWNED_ROWS, LANES)
        near_late = add_halves(g_late[0], swap_core(gate(g_late[1], small_sum)))
        small_sum = share_small(small_sum, near_late[0])
        *early_new, norm_new, norm_one, norm_two = soap_early(
            grad_scale, place, small_sum, small_groups, norm_groups
        )
        mine = reduce_late(near_late, early, batch, early_new[0], d_p_dst[1], d_features)
        big_one, big_two, big_new, big_low, small_one, small_two, small_new, small_low = soap_late(
            grad_scale, place, mine, big_groups, late_groups, early_new
        )
        norm_one, norm_two, norm_new = (norm_vector(v) for v in (norm_one, norm_two, norm_new))
    else:
        (
            (big_one, big_two, big_new),
            (small_one, small_two, small_new),
            (norm_one, norm_two, norm_new),
        ) = update_plain(
            g_late, g_early, g_small, every, grad_scale, big_state, small_state, norm_state
        )
        big_low = big_new.astype(LOW)
        small_low = small_new.astype(LOW)
    return (
        node_low[None],
        edge_new.T[None],
        d_features[None],
        d_edges.T[None],
        big_one,
        big_two,
        big_new,
        big_low,
        small_one,
        small_two,
        small_new,
        small_low,
        norm_one,
        norm_two,
        norm_new,
    )


def solution(mesh):
    batch, shards = mesh.devices.shape
    fine = Mesh(mesh.devices.reshape(batch, shards // 2, 2), ("batch", "chip", "core"))
    edge = ("chip", "core")
    every = ("batch", "chip", "core")
    placed = (
        P("batch", edge, None),
        P("batch", edge, None),
        P("batch", edge, None),
        P("batch", edge),
        P("batch", edge),
        P("batch", edge, None),
        P("batch", edge, None),
        P(every, None),
        P(every, None),
        P(every, None),
        P(every, None),
        P(every, None),
        P(),
        P(),
        P(),
        P(),
        P(),
        P(),
        P(),
        P(),
    )
    return jax.shard_map(
        body,
        mesh=fine,
        in_specs=placed,
        out_specs=(
            P("batch", edge, None),
            P("batch", edge, None),
            P("batch", edge, None),
            P("batch", edge, None),
            P(every, None),
            P(every, None),
            P(every, None),
            P(every, None),
            P(),
            P(),
            P(),
            P(),
            P(),
            P(),
            P(),
        ),
        check_vma=False,
    )
```
